32 devices in a mesh: dp: 8 (over z, y), seq: 2 (over x), ffn: 2 (over core).
Axes of the slice: x: 2, y: 2, z: 4, core: 2. Of those that a mesh axis runs over, the one named last changes fastest.
Arguments:
- tokens: bfloat16 [8, 2048, 512], P('dp', ('seq', 'ffn')), may hold values from -6 to 6
- doc_starts: int32 [8, 8], P('dp'), may hold values from 0 to 2047, as said below
- norm1_gain: float32 [512], replicated, may hold values from 0.1 to 1.9
- norm1_bias: float32 [512], replicated, may hold values from -3 to 3
- in_weight: bfloat16 [512, 2048], replicated, may hold values from -0.5 to 0.5
- out_weight: bfloat16 [512, 512], replicated, may hold values from -0.375 to 0.375
- norm2_gain: float32 [512], replicated, may hold values from 0.1 to 1.9
- norm2_bias: float32 [512], replicated, may hold values from -3 to 3
- up_weight: bfloat16 [512, 2048], P(None, 'ffn'), may hold values from -0.25 to 0.25
- down_weight: bfloat16 [512, 2048], P(None, 'ffn'), may hold values from -0.1875 to 0.1875
- output_cotangent: bfloat16 [8, 2048, 512], P('dp', ('seq', 'ffn')), may hold values from -6 to 6
Outputs:
- output: bfloat16 [8, 2048, 512], P('dp', ('seq', 'ffn'))
- grad_tokens: float32 [8, 2048, 512], P('dp', ('seq', 'ffn'))
- grad_in_proj: float32 [512, 2048], P(('dp', 'seq'))
- grad_out_proj: float32 [512, 512], P(('dp', 'seq'))
- grad_up: float32 [512, 2048], P(('dp', 'seq'), 'ffn')
- grad_down: float32 [512, 2048], P(('dp', 'seq'), 'ffn')
- grad_norm1_gain: float32 [512], P(('dp', 'seq'))
- grad_norm1_bias: float32 [512], P(('dp', 'seq'))
- grad_norm2_gain: float32 [512], P(('dp', 'seq'))
- grad_norm2_bias: float32 [512], P(('dp', 'seq'))
The draws below stay inside these ranges and needn't reach their ends.
Inputs may be any that keep to these rules, and one draw needn't show every extreme that they name: `doc_starts`: in each row the 8 document starts are distinct and increasing, and the first is 0; in the first row the last document is the row's last token alone.
All inputs are finite; a program needn't handle non-finite values.
Results may differ from the reference program's by a relative error of at most 0.017.
The reference program's roundings to bfloat16 on the way count: a program that leaves them out, or rounds other values in their place, can miss the bound.
Values may be sent and summed in bfloat16 or wider, within the bound.
No kernel may reach another device: no remote copies, remote signals or barrier semaphores. Data moves between devices by JAX's collectives and lax.ppermute only.
A program may use at most 192 MiB of HBM per device.

```python
import jax
import jax.numpy as jnp
from jax import lax

MODEL_DIM = 512
HEAD_COUNT = 8
HEAD_SIZE = 64
MEMORY_SLOTS = 64
FF = 2048
DOCS_PER_ROW = 8
BLOCK = 512
ROW_LENGTH = 2048
ROW_TOTAL = 8


def draw_doc_starts(key, part):
    row_keys = jax.random.split(key, ROW_TOTAL)
    row_ids = jnp.arange(ROW_TOTAL, dtype=jnp.int32)
    slot_places = jnp.arange(DOCS_PER_ROW - 1, dtype=jnp.int32)

    def one_row(row_random_key, row_number):
        picked_rows = jax.random.permutation(row_random_key, ROW_LENGTH - 2)[:DOCS_PER_ROW - 1] + 1
        sorted_order = jnp.sort(picked_rows).astype(jnp.int32)
        forced_reset = jnp.where((row_number == 0) & (slot_places == DOCS_PER_ROW - 2), ROW_LENGTH - 1, sorted_order).astype(jnp.int32)
        return jnp.concatenate([jnp.zeros((1,), jnp.int32), forced_reset])
    return jax.vmap(one_row)(row_keys, row_ids)


def strengthened(values, stream_key, source, target, parts, factor):
    owner, partner = [(jnp.arange(values.shape[dim]) // (values.shape[dim] // parts)).reshape([-1 if axis == dim else 1 for axis in range(values.ndim)]) for dim in (source, target)]
    chosen = jax.random.permutation(stream_key, parts)[partner]
    strong = (owner == chosen) | (owner == (partner + parts // 2) % parts)
    return jnp.where(strong, factor * values, values)


def levels(stream_key, extent, cuts, low, largest):
    factor_of = 1.0
    for dim, parts in cuts:
        heights = jax.random.uniform(jax.random.fold_in(jax.random.fold_in(stream_key, 6), dim), (parts,), jnp.float32, low / len(cuts), largest / len(cuts))
        factor_of = factor_of * jnp.repeat(jnp.exp(heights), extent[dim] // parts).reshape((-1,) + (1,) * (len(extent) - 1 - dim))
    return factor_of


def bell_draw(stream_key, dims, scale, bound, pieces=(), held_as=jnp.bfloat16):
    drawn = scale * jax.random.normal(stream_key, dims, jnp.float32)
    if pieces:
        drawn = drawn * levels(stream_key, dims, pieces, -0.22, 0.18)
    return jnp.clip(drawn, -bound, bound).astype(held_as)


def heavy_noise(key, shape, width, bound, pieces, heavy, held_as=jnp.bfloat16):
    drawn = width * jax.random.normal(key, shape, jnp.float32)
    if pieces:
        drawn = drawn * levels(key, shape, pieces, -0.22, 0.18)
    return jnp.clip(strengthened(drawn, jax.random.fold_in(key, 3), *heavy), -bound, bound).astype(held_as)


def setup_inputs(seed: int = 0) -> dict:
    key_of = jax.random.split(jax.random.key(seed), 12)
    return {
        "tokens": heavy_noise(key_of[0], (ROW_TOTAL, ROW_LENGTH, MODEL_DIM), 1.0, 6.0, ((0, 8), (1, 4)), (0, 2, 8, 2.0)),
        "doc_starts": draw_doc_starts(jax.random.fold_in(key_of[11], 71), 0),
        "norm1_gain": jnp.clip(1.0 + 0.18 * jax.random.normal(key_of[2], (MODEL_DIM,), jnp.float32), 0.1, 1.9),
        "norm1_bias": bell_draw(key_of[3], (MODEL_DIM,), 0.5, 3.0, (), jnp.float32),
        "in_weight": bell_draw(key_of[4], (MODEL_DIM, 3 * MODEL_DIM + HEAD_COUNT * MEMORY_SLOTS), (MODEL_DIM // 4) ** -0.5, 0.5),
        "out_weight": bell_draw(key_of[5], (MODEL_DIM, MODEL_DIM), (MODEL_DIM // 2) ** -0.5, 0.375),
        "norm2_gain": jnp.clip(1.0 + 0.18 * jax.random.normal(key_of[6], (MODEL_DIM,), jnp.float32), 0.1, 1.9),
        "norm2_bias": bell_draw(key_of[7], (MODEL_DIM,), 0.5, 3.0, (), jnp.float32),
        "up_weight": bell_draw(key_of[8], (MODEL_DIM, FF), MODEL_DIM ** -0.5, 0.25, ((1, 2),)),
        "down_weight": bell_draw(key_of[9], (MODEL_DIM, FF), (FF // 2) ** -0.5, 0.1875, ((1, 2),)),
        "output_cotangent": bell_draw(key_of[10], (ROW_TOTAL, ROW_LENGTH, MODEL_DIM), 1.0, 6.0, ((0, 8), (1, 4))),
    }


PRECISE = lax.Precision.HIGHEST
EPSILON = 1e-05

@jax.custom_vjp
def lower_bound(v):
    return lax.optimization_barrier(v.astype(jnp.bfloat16)).astype(jnp.float32)

@jax.custom_vjp
def low_back(v):
    return v

def low_keep(v):
    return (lower_bound(v), None)

def low_pass(kept, grad):
    return (grad,)

def back_keep(v):
    return (v, None)

def back_low(kept, grad):
    return (lower_bound(grad),)
lower_bound.defvjp(low_keep, low_pass)
low_back.defvjp(back_keep, back_low)

def layer_norm(values, gain_vec, bias_vec):
    mean_val = lax.optimization_barrier(jnp.mean(values, axis=-1, keepdims=True))
    centered = values - mean_val
    variance = lax.optimization_barrier(jnp.mean(centered * centered, axis=-1, keepdims=True))
    return centered * lax.rsqrt(variance + EPSILON) * gain_vec + bias_vec

def slot_block(carry_state, block_items):
    key_state, value_state, norm_state, carry_doc = carry_state
    query_per_head, key_per_head, value_per_head, control_per_head, documents = block_items
    block_len = query_per_head.shape[0]
    slot_places = jnp.arange(block_len, dtype=jnp.int32)
    same_doc = ((documents[:, None] == documents[None, :]) & (slot_places[None, :] <= slot_places[:, None])).astype(jnp.float32)
    carry_keep = (documents == carry_doc).astype(jnp.float32)
    score_scale = query_per_head.shape[-1] ** (-0.5)
    pair_terms = jnp.einsum('the,ihe->hti', query_per_head, key_per_head, precision=PRECISE) * same_doc[None]
    numerator = jnp.einsum('the,hse->hts', query_per_head, key_state, precision=PRECISE) * carry_keep[None, :, None]
    numerator = numerator + jnp.einsum('hti,ihs->hts', pair_terms, control_per_head, precision=PRECISE)
    totals = norm_state[:, None, :] * carry_keep[None, :, None] + jnp.einsum('ti,ihs->hts', same_doc, control_per_head, precision=PRECISE)
    scores = numerator * score_scale / totals
    top_score = lax.optimization_barrier(jnp.max(scores, axis=-1, keepdims=True))
    expo = jnp.exp(scores - top_score)
    weight = expo / lax.optimization_barrier(jnp.sum(expo, axis=-1, keepdims=True))
    spread = weight / totals
    carried = jnp.einsum('hts,hse->the', spread, value_state, precision=PRECISE) * carry_keep[:, None, None]
    link_terms = jnp.einsum('hts,ihs->hti', spread, control_per_head, precision=PRECISE) * same_doc[None]
    mixed_output = carried + jnp.einsum('hti,ihe->the', link_terms, value_per_head, precision=PRECISE)
    last_doc = documents[block_len - 1]
    last_keep = carry_keep[block_len - 1]
    tail_ctrl = control_per_head * (documents == last_doc).astype(jnp.float32)[:, None, None]
    new_key = key_state * last_keep + jnp.einsum('ihs,ihe->hse', tail_ctrl, key_per_head, precision=PRECISE)
    new_value = value_state * last_keep + jnp.einsum('ihs,ihe->hse', tail_ctrl, value_per_head, precision=PRECISE)
    new_norm = norm_state * last_keep + lax.optimization_barrier(jnp.sum(tail_ctrl, axis=0))
    return ((new_key, new_value, new_norm, last_doc), mixed_output)

def slot_attention(query_per_head, key_per_head, value_per_head, control_per_head, documents, key_state, value_state, norm_state, carry_doc, block_len):
    block_count = query_per_head.shape[0] // block_len

    def to_blocks(array_in):
        return array_in.reshape((block_count, block_len) + array_in.shape[1:])
    start_state = (key_state, value_state, norm_state, carry_doc)
    _, mixed_output = lax.scan(jax.checkpoint(slot_block), start_state, (to_blocks(query_per_head), to_blocks(key_per_head), to_blocks(value_per_head), to_blocks(control_per_head), to_blocks(documents)))
    return mixed_output.reshape(query_per_head.shape)

def reference(tokens, doc_starts, norm1_gain, norm1_bias, in_weight, out_weight, norm2_gain, norm2_bias, up_weight, down_weight, output_cotangent):
    params = (norm1_gain.astype(jnp.float32), norm1_bias.astype(jnp.float32), in_weight.astype(jnp.float32), out_weight.astype(jnp.float32), norm2_gain.astype(jnp.float32), norm2_bias.astype(jnp.float32), up_weight.astype(jnp.float32), down_weight.astype(jnp.float32))
    token_positions = jnp.arange(ROW_LENGTH, dtype=jnp.int32)

    def forward(param_set, token_row, starts):
        gain_one, bias_one, w_in, w_out, gain_two, bias_two, w_up, w_down = param_set
        documents = lax.optimization_barrier(jnp.sum((starts[None, :] <= token_positions[:, None]).astype(jnp.int32), axis=1)).astype(jnp.int32)
        xn1 = lower_bound(layer_norm(token_row, gain_one, bias_one))
        projected_input = low_back(jnp.dot(xn1, w_in, precision=PRECISE))
        query_per_head = lower_bound(projected_input[:, :MODEL_DIM]).reshape(ROW_LENGTH, HEAD_COUNT, HEAD_SIZE)
        key_per_head = lower_bound(projected_input[:, MODEL_DIM:2 * MODEL_DIM]).reshape(ROW_LENGTH, HEAD_COUNT, HEAD_SIZE)
        value_per_head = lower_bound(projected_input[:, 2 * MODEL_DIM:3 * MODEL_DIM]).reshape(ROW_LENGTH, HEAD_COUNT, HEAD_SIZE)
        control_per_head = lower_bound(jnp.exp(projected_input[:, 3 * MODEL_DIM:])).reshape(ROW_LENGTH, HEAD_COUNT, MEMORY_SLOTS)
        zero_mem = jnp.zeros((HEAD_COUNT, MEMORY_SLOTS, HEAD_SIZE), jnp.float32)
        zero_norm = jnp.zeros((HEAD_COUNT, MEMORY_SLOTS), jnp.float32)
        mixed_output = slot_attention(query_per_head, key_per_head, value_per_head, control_per_head, documents, zero_mem, zero_mem, zero_norm, jnp.zeros((), jnp.int32), BLOCK)
        mixed_output = lower_bound(mixed_output.reshape(ROW_LENGTH, MODEL_DIM))
        hidden1 = token_row + low_back(jnp.dot(mixed_output, w_out, precision=PRECISE))
        xn2 = lower_bound(layer_norm(hidden1, gain_two, bias_two))
        pre_act = low_back(jnp.dot(xn2, w_up, precision=PRECISE))
        hidden = lower_bound(jax.nn.gelu(pre_act))
        return hidden1 + jnp.dot(hidden, w_down.T, precision=PRECISE)

    def one_row(totals, row_items):
        token_row, starts, cotangent = row_items
        result, pullback = jax.vjp(lambda param_set, row_in: forward(param_set, row_in, starts), params, token_row.astype(jnp.float32))
        grad_params, grad_row = pullback(cotangent.astype(jnp.float32))
        totals = jax.tree.map(lambda left, right: left + right, totals, grad_params)
        return (totals, (result.astype(jnp.bfloat16), grad_row))
    zero_grads = jax.tree.map(jnp.zeros_like, params)
    totals, (output, grad_tokens) = lax.scan(one_row, zero_grads, (tokens, doc_starts, output_cotangent))
    return (output, grad_tokens, totals[2], totals[3], totals[6], totals[7], totals[0], totals[1], totals[4], totals[5])
```

```python
import functools

import jax
import jax.numpy as jnp
from jax import lax
from jax.sharding import PartitionSpec as P

HEADS = 8
HEAD = 64
EPSILON = 1e-05
BF = jnp.bfloat16
F32 = jnp.float32


def dot(a, b, dims):
    return lax.dot_general(
        a.astype(BF), b.astype(BF), (dims, ((), ())), preferred_element_type=F32
    )


def heads_dot(spec, a, b):
    return jnp.einsum(spec, a.astype(BF), b.astype(BF), preferred_element_type=F32)


def swap(a, axis, bit):
    size = lax.axis_size(axis)
    return lax.ppermute(a, axis, [(i, i ^ bit) for i in range(size)])


def norm(x, gain, bias):
    mean = jnp.mean(x, axis=-1, keepdims=True)
    centered = x - mean
    inverse = lax.rsqrt(jnp.mean(centered * centered, axis=-1, keepdims=True) + EPSILON)
    n = centered * inverse
    return n, inverse, (n * gain + bias).astype(BF)


def norm_back(d_out, n, inverse, gain):
    d_n = d_out * gain
    d_in = (
        d_n
        - jnp.mean(d_n, axis=-1, keepdims=True)
        - n * jnp.mean(d_n * n, axis=-1, keepdims=True)
    ) * inverse
    return d_in, jnp.sum(d_out * n, axis=0), jnp.sum(d_out, axis=0)


GELU_A = 0.7978845608028654
GELU_B = 0.044715


def gelu_pair(v):
    v2 = v * v
    th = jnp.tanh(GELU_A * v * (1.0 + GELU_B * v2))
    value = 0.5 * v * (1.0 + th)
    slope = 0.5 * (1.0 + th) + 0.5 * v * (1.0 - th * th) * GELU_A * (1.0 + 3.0 * GELU_B * v2)
    return value, slope


def scatter_plan():
    count = lax.axis_size("dp")
    bits = [("seq", 1)]
    step = 1
    while step < count:
        bits.append(("dp", step))
        step *= 2
    return bits


def reduce_rows(group, lead):
    bits = scatter_plan()
    first = [(i + lead) % 3 for i in range(3)]
    order = first + list(range(3, len(bits)))
    rows, width = group.shape
    shape = (2,) * len(bits) + (rows >> len(bits), width)
    value = group.reshape(shape)
    left = list(reversed(range(len(bits))))
    for b in order:
        axis, step = bits[b]
        at = left.index(b)
        mine = (lax.axis_index(axis) // step) % 2
        keep = lax.dynamic_index_in_dim(value, mine, at, False)
        send = lax.dynamic_index_in_dim(value, 1 - mine, at, False)
        left.pop(at)
        value = keep + swap(send.astype(BF), axis, step).astype(F32)
    return value


def on_device(
    tokens,
    doc_starts,
    norm1_gain,
    norm1_bias,
    in_weight,
    out_weight,
    norm2_gain,
    norm2_bias,
    up_own,
    down_own,
    output_cotangent,
):
    seq, ffn = lax.axis_index("seq"), lax.axis_index("ffn")
    up_other, down_other = swap(up_own, "ffn", 1), swap(down_own, "ffn", 1)
    x = tokens[0].astype(F32)
    cotangent = output_cotangent[0]
    length, width = x.shape
    starts = doc_starts[0]
    shard = seq * lax.axis_size("ffn") + ffn
    begin = shard * length
    positions = begin + jnp.arange(length, dtype=jnp.int32)
    documents = jnp.sum((starts[None, :] <= positions[:, None]).astype(jnp.int32), axis=1)

    def doc_at(place):
        return jnp.sum((starts <= place).astype(jnp.int32))

    def passes(which):
        return (doc_at(which * length + length - 1) == doc_at(which * length - 1)).astype(F32)

    carry_doc, last_doc = doc_at(begin - 1), doc_at(begin + length - 1)
    causal = positions[None, :] <= positions[:, None]
    mask = ((documents[:, None] == documents[None, :]) & causal).astype(F32)
    enters = (documents == carry_doc).astype(F32)[None, :, None]
    tail = (documents == last_doc).astype(F32)[None, :, None]

    n1, inv1, xn1 = norm(x, norm1_gain, norm1_bias)
    projected = dot(xn1, in_weight, ((1,), (0,)))

    def split(a):
        return a.reshape(length, HEADS, HEAD).transpose(1, 0, 2)

    def join(a):
        return a.transpose(1, 0, 2).reshape(length, width)

    q = split(projected[:, :width].astype(BF))
    k = split(projected[:, width : 2 * width].astype(BF))
    v = split(projected[:, 2 * width : 3 * width].astype(BF))
    control = jnp.exp(projected[:, 3 * width :])
    c = split(control.astype(BF))
    c_tail = c * tail.astype(BF)
    own = jnp.concatenate(
        [
            heads_dot("his,hie->hse", c_tail, k),
            heads_dot("his,hie->hse", c_tail, v),
            jnp.broadcast_to(
                jnp.sum(c_tail.astype(F32), axis=1)[:, :, None], (HEADS, HEAD, HEAD)
            ),
        ],
        axis=2,
    )
    first, second = 2 * seq, 2 * seq + 1
    is_first = ffn == 0
    partner = swap(own, "ffn", 1)
    both = jnp.where(is_first, partner + passes(second) * own, own + passes(second) * partner)
    entered = lax.ppermute(both, "seq", [(0, 1)])
    memory = jnp.where(is_first, entered, partner + passes(first) * entered)
    mem_k, mem_v, mem_n = memory[:, :, :HEAD], memory[:, :, HEAD : 2 * HEAD], memory[:, :, 2 * HEAD]

    pairs = (heads_dot("hte,hie->hti", q, k) * mask).astype(BF)
    total = heads_dot("ti,his->hts", mask, c) + enters * mem_n[:, None, :]
    number = heads_dot("hti,his->hts", pairs, c) + enters * heads_dot("hte,hse->hts", q, mem_k)
    inverse = 1.0 / total
    score = number * inverse * (HEAD**-0.5)
    top = jnp.max(score, axis=-1, keepdims=True)
    e = jnp.exp(score - top)
    weight = e / jnp.sum(e, axis=-1, keepdims=True)
    spread = weight * inverse
    links = (heads_dot("hts,his->hti", spread, c) * mask).astype(BF)
    mixed = heads_dot("hti,hie->hte", links, v) + enters * heads_dot("hts,hse->hte", spread, mem_v)
    mixed = join(mixed.astype(BF))
    hidden1 = x + dot(mixed, out_weight, ((1,), (0,)))
    n2, inv2, xn2 = norm(hidden1, norm2_gain, norm2_bias)

    def half(up, down):
        pre = dot(xn2, up, ((1,), (0,)))
        hidden, slope = gelu_pair(pre)
        hidden = hidden.astype(BF)
        part = dot(hidden, down, ((1,), (1,)))
        d_hidden = dot(cotangent, down, ((1,), (0,)))
        grad_pre = (d_hidden * slope).astype(BF)
        d_part = dot(grad_pre, up, ((1,), (1,)))
        grad_down = dot(cotangent, hidden, ((0,), (0,)))
        grad_up = dot(xn2, grad_pre, ((0,), (0,)))
        return part, d_part, grad_up, grad_down

    part_a, d_a, up_a, down_a = half(up_own, down_own)
    part_b, d_b, up_b, down_b = half(up_other, down_other)
    output = (hidden1 + (part_a + part_b)).astype(BF)
    grad_up = up_a + swap(up_b.astype(BF), "ffn", 1).astype(F32)
    grad_down = down_a + swap(down_b.astype(BF), "ffn", 1).astype(F32)

    d2, grad_gain2, grad_bias2 = norm_back(d_a + d_b, n2, inv2, norm2_gain)
    d_hidden1 = cotangent.astype(F32) + d2
    d_branch = d_hidden1.astype(BF)
    grad_out = dot(mixed, d_branch, ((0,), (0,)))
    g = split(dot(d_branch, out_weight, ((1,), (1,))).astype(BF))

    values = (heads_dot("hte,hie->hti", g, v) * mask).astype(BF)
    number_v = heads_dot("hti,his->hts", values, c) + enters * heads_dot("hte,hse->hts", g, mem_v)
    d_weight = number_v * inverse
    d_score = weight * (d_weight - jnp.sum(weight * d_weight, axis=-1, keepdims=True))
    a = d_score * inverse * (HEAD**-0.5)
    d_total = -(a * number + spread * number_v) * inverse
    d_memory = jnp.concatenate(
        [
            heads_dot("hts,hte->hse", a * enters, q),
            heads_dot("hts,hte->hse", spread * enters, g),
            jnp.broadcast_to(
                jnp.sum(d_total * enters, axis=1)[:, :, None], (HEADS, HEAD, HEAD)
            ),
        ],
        axis=2,
    )
    d_partner = swap(d_memory, "ffn", 1)
    d_both = jnp.where(
        is_first, d_memory + passes(first) * d_partner, d_partner + passes(first) * d_memory
    )
    d_later = lax.ppermute(d_both, "seq", [(1, 0)])
    after = jnp.where(is_first, d_partner + passes(second) * d_later, d_later)
    after_k, after_v, after_n = after[:, :, :HEAD], after[:, :, HEAD : 2 * HEAD], after[:, :, 2 * HEAD]

    steps = (heads_dot("hts,his->hti", a, c) * mask).astype(BF)
    d_query = heads_dot("hti,hie->hte", steps, k) + enters * heads_dot("hts,hse->hte", a, mem_k)
    d_key = heads_dot("hti,hte->hie", steps, q) + heads_dot("his,hse->hie", c_tail, after_k)
    d_value = heads_dot("hti,hte->hie", links, g) + heads_dot("his,hse->hie", c_tail, after_v)
    d_control = (
        heads_dot("hti,hts->his", pairs, a)
        + heads_dot("hti,hts->his", values, spread)
        + heads_dot("ti,hts->his", mask, d_total)
        + tail
        * (
            heads_dot("hie,hse->his", k, after_k)
            + heads_dot("hie,hse->his", v, after_v)
            + after_n[:, None, :]
        )
    )
    d_proj = jnp.concatenate(
        [join(d_query), join(d_key), join(d_value), join(d_control) * control], axis=1
    ).astype(BF)
    grad_in = dot(xn1, d_proj, ((0,), (0,)))
    d1, grad_gain1, grad_bias1 = norm_back(
        dot(d_proj, in_weight, ((1,), (1,))), n1, inv1, norm1_gain
    )
    grad_tokens = d_hidden1 + d1

    def core_half(a):
        half_width = a.shape[1] // 2
        keep = lax.dynamic_slice_in_dim(a, ffn * half_width, half_width, 1)
        send = lax.dynamic_slice_in_dim(a, (1 - ffn) * half_width, half_width, 1)
        return keep + swap(send.astype(BF), "ffn", 1).astype(F32)

    def core_join(a):
        other = swap(a.astype(BF), "ffn", 1)
        a = a.astype(BF)
        return jnp.where(
            is_first, jnp.concatenate([a, other], 1), jnp.concatenate([other, a], 1)
        ).astype(F32)

    norms = jnp.stack([grad_gain1, grad_bias1, grad_gain2, grad_bias2], axis=1)
    norms = norms + swap(norms, "ffn", 1)
    grad_down = reduce_rows(grad_down, 0)
    grad_up = reduce_rows(grad_up, 1)
    grad_out = core_join(reduce_rows(core_half(grad_out), 2))
    grad_in = core_join(reduce_rows(core_half(grad_in), 2))
    norms = reduce_rows(norms, 1)
    return (
        output[None],
        grad_tokens[None],
        grad_in,
        grad_out,
        grad_up,
        grad_down,
        norms[:, 0],
        norms[:, 1],
        norms[:, 2],
        norms[:, 3],
    )


def solution(mesh):
    rows = P("dp", ("seq", "ffn"), None)
    owned = P(("dp", "seq"))
    return jax.shard_map(
        on_device,
        mesh=mesh,
        in_specs=(
            rows, P("dp", None), P(), P(), P(), P(), P(), P(),
            P(None, "ffn"), P(None, "ffn"), rows,
        ),
        out_specs=(
            rows, rows, P(("dp", "seq"), None), P(("dp", "seq"), None),
            P(("dp", "seq"), "ffn"), P(("dp", "seq"), "ffn"),
            owned, owned, owned, owned,
        ),
        check_vma=False,
    )
```

```python
import functools

import jax
import jax.numpy as jnp
from jax import lax
from jax.experimental import pallas as pl
from jax.experimental.pallas import tpu as pltpu
from jax.sharding import PartitionSpec as P

HEADS = 8
HEAD = 64
EPSILON = 1e-05
BF = jnp.bfloat16
F32 = jnp.float32
GELU_A = 0.7978845608028654
GELU_B = 0.044715
SCALE = HEAD**-0.5
PACK = HEADS * HEAD + 64
VMEM_LIMIT = 56 * 1024 * 1024


def nn(a, b):
    return lax.dot_general(a, b, (((1,), (0,)), ((), ())), preferred_element_type=F32)


def nt(a, b):
    return lax.dot_general(a, b, (((1,), (1,)), ((), ())), preferred_element_type=F32)


def tn(a, b):
    return lax.dot_general(a, b, (((0,), (0,)), ((), ())), preferred_element_type=F32)


def swap(a, axis, bit):
    size = lax.axis_size(axis)
    return lax.ppermute(a, axis, [(i, i ^ bit) for i in range(size)])


def call(body, grid, in_specs, out_specs, out_shape, scratch=(), flops=0, **kw):
    return pl.pallas_call(
        body,
        grid=grid,
        in_specs=in_specs,
        out_specs=out_specs,
        out_shape=out_shape,
        scratch_shapes=list(scratch),
        cost_estimate=pl.CostEstimate(flops=flops, bytes_accessed=2**21, transcendentals=0),
        compiler_params=pltpu.CompilerParams(vmem_limit_bytes=VMEM_LIMIT),
        **kw,
    )


def whole(shape):
    return pl.BlockSpec(shape, lambda *_: (0,) * len(shape))


SMEM = pl.BlockSpec(memory_space=pltpu.SMEM)


def shard_of():
    return lax.axis_index("seq") * 2 + lax.axis_index("ffn")


def doc_begin_row(starts_ref, length):
    begin = shard_of() * length
    place = lax.broadcasted_iota(jnp.int32, (1, length), 1)
    row = jnp.full((1, length), -(2**30), jnp.int32)
    for j in range(starts_ref.shape[1]):
        s = starts_ref[0, j] - begin
        row = jnp.where(place >= s, jnp.maximum(row, s), row)
    return row


def passes(starts_ref, which, length):
    hit = jnp.int32(0)
    for j in range(starts_ref.shape[1]):
        s = starts_ref[0, j]
        hit = hit | ((s >= which * length) & (s < which * length + length)).astype(jnp.int32)
    return 1.0 - hit.astype(F32)


def visible(doc_row, length):
    i = lax.broadcasted_iota(jnp.int32, (length, length), 0)
    t = lax.broadcasted_iota(jnp.int32, (length, length), 1)
    return jnp.where((i <= t) & (i >= doc_row), 1.0, 0.0).astype(BF)


def tail_row(doc_row, length):
    place = lax.broadcasted_iota(jnp.int32, (1, length), 1)
    last = doc_row[:, length - 1 :]
    return jnp.where(place >= last, 1.0, 0.0)


def pack_totals(pack_ref, totals8):
    base = HEADS * HEAD
    hi = totals8.astype(BF)
    lo = (totals8 - hi.astype(F32)).astype(BF)
    for a in range(4):
        cols = slice(128 * a, 128 * a + 128)
        pack_ref[base + 16 * a : base + 16 * a + 16, :] = jnp.concatenate(
            [hi[:, cols], lo[:, cols]], axis=0
        )


def unpack(rows, totals8_of):
    base = HEADS * HEAD
    out = []
    for a in range(4):
        block = totals8_of(slice(base + 16 * a, base + 16 * a + 16))
        out.append(block[:8] + block[8:])
    return rows(slice(0, base)), jnp.concatenate(out, axis=1)


def combine_body(backward, length, starts_ref, own_ref, partner_ref, out_ref):
    first = 2 * lax.axis_index("seq")
    is_first = (lax.axis_index("ffn") == 0).astype(F32)
    base = HEADS * HEAD
    if backward:
        p = passes(starts_ref, first, length)
        own_by, partner_by = is_first + (1 - is_first) * p, is_first * p + (1 - is_first)
    else:
        p = passes(starts_ref, first + 1, length)
        own_by, partner_by = is_first * p + (1 - is_first), is_first + (1 - is_first) * p

    def sum_of(at):
        return own_ref[at, :].astype(F32) * own_by + partner_ref[at, :].astype(F32) * partner_by

    memory, totals8 = unpack(sum_of, sum_of)
    out_ref[:base, :] = memory.astype(BF)
    pack_totals(out_ref, totals8)


def combine(backward, length, starts, own, partner):
    return call(
        functools.partial(combine_body, backward, length),
        (),
        [SMEM, whole((PACK, 128)), whole((PACK, 128))],
        whole((PACK, 128)),
        jax.ShapeDtypeStruct((PACK, 128), BF),
    )(starts, own, partner)


def arrived(backward, length, starts_ref, partner_ref, far_ref, mem_ref, totals_ref):
    first = 2 * lax.axis_index("seq")
    is_first = (lax.axis_index("ffn") == 0).astype(F32)
    if backward:
        p = passes(starts_ref, first + 1, length)
        far_by, partner_by = is_first * p + (1 - is_first), is_first
    else:
        p = passes(starts_ref, first, length)
        far_by, partner_by = is_first + (1 - is_first) * p, 1 - is_first

    def sum_of(at):
        return far_ref[at, :].astype(F32) * far_by + partner_ref[at, :].astype(F32) * partner_by

    memory, totals8 = unpack(sum_of, sum_of)
    mem_ref[...] = memory.astype(BF)
    totals_ref[...] = totals8.T


def project_body(x_ref, gain_ref, bias_ref, w_ref, starts_ref,
                 heads_ref, control_ref, xnt_ref, pack_ref, xn_ref):
    j = pl.program_id(0)
    length = x_ref.shape[0]

    @pl.when(j == 0)
    def _():
        x = x_ref[...].astype(F32)
        mean = jnp.mean(x, axis=-1, keepdims=True)
        centered = x - mean
        inverse = lax.rsqrt(jnp.mean(centered * centered, axis=-1, keepdims=True) + EPSILON)
        xn = (centered * inverse * gain_ref[...] + bias_ref[...]).astype(BF)
        xn_ref[...] = xn
        xnt_ref[...] = xn.T

    projected = nn(xn_ref[...], w_ref[...])

    @pl.when(j < 3)
    def _():
        t = projected.astype(BF).T
        for h in range(HEADS):
            heads_ref[h, pl.ds(pl.multiple_of(j * HEAD, HEAD), HEAD), :] = t[h * HEAD : h * HEAD + HEAD]

    @pl.when(j == 3)
    def _():
        control = jnp.exp(projected).T
        control_ref[...] = control
        c = control.astype(BF)
        tail = tail_row(doc_begin_row(starts_ref, length), length)
        c_tail = (c.astype(F32) * tail).astype(BF)
        for h in range(HEADS):
            rows = slice(h * HEAD, h * HEAD + HEAD)
            heads_ref[h, 3 * HEAD :, :] = c[rows]
            mem_k = nt(c_tail[rows], heads_ref[h, HEAD : 2 * HEAD, :])
            mem_vt = nt(heads_ref[h, 2 * HEAD : 3 * HEAD, :], c_tail[rows])
            pack_ref[rows, :] = jnp.concatenate([mem_k, mem_vt], axis=1).astype(BF)
        tail8 = jnp.broadcast_to(tail, (8, length)).astype(BF)
        pack_totals(pack_ref, nt(tail8, c))


def project(x, gain, bias, w, starts):
    length, width = x.shape
    return call(
        project_body,
        (4,),
        [
            whole((length, width)), whole((1, width)), whole((1, width)),
            pl.BlockSpec((width, width), lambda j: (0, j)), SMEM,
        ],
        [
            whole((HEADS, 4 * HEAD, length)), whole((width, length)), whole((width, length)),
            whole((PACK, 128)),
        ],
        [
            jax.ShapeDtypeStruct((HEADS, 4 * HEAD, length), BF),
            jax.ShapeDtypeStruct((width, length), F32),
            jax.ShapeDtypeStruct((width, length), BF),
            jax.ShapeDtypeStruct((PACK, 128), BF),
        ],
        [pltpu.VMEM((length, width), BF)],
        flops=2 * length * width * 4 * width,
    )(x, gain, bias, w, starts)


HEAD_BLOCK = lambda rows, length: pl.BlockSpec((1, rows, length), lambda h: (h, 0, 0))
ROW_BLOCK = lambda length: pl.BlockSpec((HEAD, length), lambda h: (h, 0))


def causal_pairs(left, right, mask_ref):
    half = mask_ref.shape[0] // 2
    rows = left.T
    a = nn(rows[:half], right[:, :half]).astype(BF) * mask_ref[:half, :half]
    b = nn(rows, right[:, half:]).astype(BF) * mask_ref[:, half:]
    return a, b


def causal_sum(left, pairs):
    a, b = pairs
    half = a.shape[0]
    return jnp.concatenate([nn(left[:, :half], a), nn(left, b)], axis=1)


def causal_back(left, pairs):
    a, b = pairs
    half = a.shape[0]
    late = nt(left[:, half:], b)
    return jnp.concatenate([late[:, :half] + nt(left[:, :half], a), late[:, half:]], axis=1)


def mask_pair(mask_ref):
    half = mask_ref.shape[0] // 2
    return mask_ref[:half, :half], mask_ref[:, half:]


def parts(heads_ref):
    return [heads_ref[0, j * HEAD : j * HEAD + HEAD, :] for j in range(4)]


def local_body(starts_ref, heads_ref, number_ref, total_ref, mask_ref):
    length = heads_ref.shape[2]

    @pl.when(pl.program_id(0) == 0)
    def _():
        mask_ref[...] = visible(doc_begin_row(starts_ref, length), length)

    q, k, v, c = parts(heads_ref)
    number_ref[...] = causal_sum(c, causal_pairs(k, q, mask_ref))
    total_ref[...] = causal_sum(c, mask_pair(mask_ref))


def local_sums(starts, heads):
    length = heads.shape[2]
    width = HEADS * HEAD
    return call(
        local_body,
        (HEADS,),
        [SMEM, HEAD_BLOCK(4 * HEAD, length)],
        [ROW_BLOCK(length)] * 2,
        [jax.ShapeDtypeStruct((width, length), F32)] * 2,
        [pltpu.VMEM((length, length), BF)],
        flops=6 * length * length * width,
    )(starts, heads)


def enters_row(starts_ref, length):
    return jnp.where(doc_begin_row(starts_ref, length) < 0, 1.0, 0.0)


def softmax(number, inverse):
    score = number * (inverse * SCALE)
    e = jnp.exp(score - jnp.max(score, axis=0, keepdims=True))
    return e / jnp.sum(e, axis=0, keepdims=True)


def mix_body(starts_ref, heads_ref, number_ref, total_ref, partner_ref, far_ref,
             number_out, total_out, mixed_ref, mem_out, mask_ref, mem_ref, totals_ref):
    length = heads_ref.shape[2]
    h = pl.program_id(0)

    @pl.when(h == 0)
    def _():
        mask_ref[...] = visible(doc_begin_row(starts_ref, length), length)
        arrived(False, length, starts_ref, partner_ref, far_ref, mem_ref, totals_ref)
        mem_out[...] = mem_ref[...]

    enters = enters_row(starts_ref, length)
    rows = pl.ds(pl.multiple_of(h * HEAD, HEAD), HEAD)
    q, k, v, c = parts(heads_ref)
    mem = mem_ref[rows, :]
    mem_k, mem_vt = mem[:, :HEAD], mem[:, HEAD:]
    number = number_ref[...] + enters * nn(mem_k, q)
    total = total_ref[...] + enters * totals_ref[rows, 0:1]
    number_out[...] = number
    total_out[...] = total
    inverse = 1.0 / total
    spread = (softmax(number, inverse) * inverse).astype(BF)
    links = causal_pairs(c, spread, mask_ref)
    mixed = causal_sum(v, links) + enters * nn(mem_vt, spread)
    mixed_ref[...] = mixed.astype(BF)


def mix(starts, heads, number, total, partner, far):
    length = heads.shape[2]
    width = HEADS * HEAD
    return call(
        mix_body,
        (HEADS,),
        [SMEM, HEAD_BLOCK(4 * HEAD, length), ROW_BLOCK(length), ROW_BLOCK(length),
         whole((PACK, 128)), whole((PACK, 128))],
        [ROW_BLOCK(length), ROW_BLOCK(length), ROW_BLOCK(length), whole((width, 128))],
        [
            jax.ShapeDtypeStruct((width, length), F32),
            jax.ShapeDtypeStruct((width, length), F32),
            jax.ShapeDtypeStruct((width, length), BF),
            jax.ShapeDtypeStruct((width, 128), BF),
        ],
        [pltpu.VMEM((length, length), BF), pltpu.VMEM((width, 128), BF), pltpu.VMEM((width, 8), F32)],
        flops=6 * length * length * width,
    )(starts, heads, number, total, partner, far)


def feed_body(x_ref, mixed_ref, cot_ref, w_out_ref, gain_ref, bias_ref,
              up_own, up_other, down_own, down_other,
              output_ref, d_hidden1_ref, g_ref, grad_out_ref, gain_grad_ref, bias_grad_ref,
              gup_own, gup_other, gdown_own, gdown_other,
              hidden1_ref, n_ref, inv_ref, xn_ref, xnt_ref, cott_ref, part_ref, d_ref):
    j = pl.program_id(0)

    @pl.when(j == 0)
    def _():
        hidden1 = x_ref[...].astype(F32) + tn(mixed_ref[...], w_out_ref[...])
        hidden1_ref[...] = hidden1
        mean = jnp.mean(hidden1, axis=-1, keepdims=True)
        centered = hidden1 - mean
        inverse = lax.rsqrt(jnp.mean(centered * centered, axis=-1, keepdims=True) + EPSILON)
        n = centered * inverse
        n_ref[...] = n
        inv_ref[...] = inverse
        xn = (n * gain_ref[...] + bias_ref[...]).astype(BF)
        xn_ref[...] = xn
        xnt_ref[...] = xn.T
        cott_ref[...] = cot_ref[...].T

    def step(up_ref, down_ref, gup_ref, gdown_ref, is_start):
        up, down = up_ref[...], down_ref[...]
        pre = nn(xn_ref[...], up)
        v2 = pre * pre
        th = jnp.tanh(GELU_A * pre * (1.0 + GELU_B * v2))
        half = 0.5 * (1.0 + th)
        hidden = (pre * half).astype(BF)
        slope = half + 0.5 * pre * (1.0 - th * th) * (GELU_A * (1.0 + 3.0 * GELU_B * v2))
        grad_pre = (nn(cot_ref[...], down) * slope).astype(BF)
        part = nt(hidden, down)
        d = nt(grad_pre, up)
        if is_start:
            part_ref[...] = part
            d_ref[...] = d
        else:
            part_ref[...] += part
            d_ref[...] += d
        gdown_ref[...] = nn(cott_ref[...], hidden).astype(gdown_ref.dtype)
        gup_ref[...] = nn(xnt_ref[...], grad_pre).astype(gup_ref.dtype)

    @pl.when(j == 0)
    def _():
        step(up_own, down_own, gup_own, gdown_own, True)

    @pl.when(j == 1)
    def _():
        step(up_own, down_own, gup_own, gdown_own, False)

    @pl.when(j >= 2)
    def _():
        step(up_other, down_other, gup_other, gdown_other, False)

    @pl.when(j == 3)
    def _():
        output_ref[...] = (hidden1_ref[...] + part_ref[...]).astype(BF)
        d, n = d_ref[...], n_ref[...]
        gain_grad_ref[...] = jnp.broadcast_to(jnp.sum(d * n, axis=0, keepdims=True), gain_grad_ref.shape)
        bias_grad_ref[...] = jnp.broadcast_to(jnp.sum(d, axis=0, keepdims=True), bias_grad_ref.shape)
        d_n = d * gain_ref[...]
        d_in = (
            d_n
            - jnp.mean(d_n, axis=-1, keepdims=True)
            - n * jnp.mean(d_n * n, axis=-1, keepdims=True)
        ) * inv_ref[...]
        d_hidden1 = cot_ref[...].astype(F32) + d_in
        d_hidden1_ref[...] = d_hidden1
        d_branch = d_hidden1.astype(BF)
        grad_out_ref[...] = nn(mixed_ref[...], d_branch).astype(grad_out_ref.dtype)
        g_ref[...] = nt(w_out_ref[...], d_branch).astype(BF)


def feed(x, mixed, cotangent, w_out, gain, bias, up_own, up_other, down_own, down_other):
    length, width = x.shape
    square = whole((length, width))
    row = whole((1, width))
    own = pl.BlockSpec((width, 512), lambda j: (0, jnp.minimum(j, 1)))
    other = pl.BlockSpec((width, 512), lambda j: (0, jnp.maximum(j - 2, 0)))
    half = up_own.shape[1]
    vec = whole((8, width))
    return call(
        feed_body,
        (4,),
        [square, square, square, square, row, row, own, other, own, other],
        [square, square, square, square, vec, vec, own, other, own, other],
        [
            jax.ShapeDtypeStruct((length, width), BF),
            jax.ShapeDtypeStruct((length, width), F32),
            jax.ShapeDtypeStruct((width, length), BF),
            jax.ShapeDtypeStruct((width, width), BF),
            jax.ShapeDtypeStruct((8, width), F32),
            jax.ShapeDtypeStruct((8, width), F32),
        ]
        + [jax.ShapeDtypeStruct((width, half), BF)] * 4,
        [
            pltpu.VMEM((length, width), F32), pltpu.VMEM((length, width), F32),
            pltpu.VMEM((length, 1), F32), pltpu.VMEM((length, width), BF),
            pltpu.VMEM((width, length), BF), pltpu.VMEM((width, length), BF),
            pltpu.VMEM((length, width), F32), pltpu.VMEM((length, width), F32),
        ],
        flops=2 * length * width * 2048 * 7,
    )(x, mixed, cotangent, w_out, gain, bias, up_own, up_other, down_own, down_other)


def scores_back_body(starts_ref, heads_ref, g_ref, number_ref, total_ref, mem_ref,
                     a_ref, spread_ref, d_total_ref, pack_ref, mask_ref, sums_ref):
    length = heads_ref.shape[2]
    h = pl.program_id(0)

    @pl.when(h == 0)
    def _():
        mask_ref[...] = visible(doc_begin_row(starts_ref, length), length)

    enters = enters_row(starts_ref, length)
    rows = pl.ds(pl.multiple_of(h * HEAD, HEAD), HEAD)
    q, k, v, c = parts(heads_ref)
    g = g_ref[...]
    mem_vt = mem_ref[:, HEAD:]
    number, inverse = number_ref[...], 1.0 / total_ref[...]
    weight = softmax(number, inverse)
    number_v = causal_sum(c, causal_pairs(v, g, mask_ref)) + enters * tn(mem_vt, g)
    d_weight = number_v * inverse
    d_score = weight * (d_weight - jnp.sum(weight * d_weight, axis=0, keepdims=True))
    a = d_score * (inverse * SCALE)
    spread = weight * inverse
    d_total = -(a * number + spread * number_v) * inverse
    a_ref[...] = a.astype(BF)
    spread_ref[...] = spread.astype(BF)
    d_total_ref[...] = d_total.astype(BF)
    mem_k = nt((a * enters).astype(BF), q)
    d_vt = nt(g, (spread * enters).astype(BF))
    pack_ref[rows, :] = jnp.concatenate([mem_k, d_vt], axis=1).astype(BF)
    sums_ref[rows, 0:1] = jnp.sum(d_total * enters, axis=1, keepdims=True)

    @pl.when(h == HEADS - 1)
    def _():
        pack_totals(pack_ref, jnp.broadcast_to(sums_ref[...].T[0:1], (8, HEADS * HEAD)))


def scores_back(starts, heads, g, number, total, mem):
    length = heads.shape[2]
    width = HEADS * HEAD
    row = ROW_BLOCK(length)
    return call(
        scores_back_body,
        (HEADS,),
        [SMEM, HEAD_BLOCK(4 * HEAD, length), row, row, row, pl.BlockSpec((HEAD, 128), lambda h: (h, 0))],
        [row, row, row, whole((PACK, 128))],
        [jax.ShapeDtypeStruct((width, length), BF)] * 3 + [jax.ShapeDtypeStruct((PACK, 128), BF)],
        [pltpu.VMEM((length, length), BF), pltpu.VMEM((width, 8), F32)],
        flops=6 * length * length * width,
    )(starts, heads, g, number, total, mem)


def heads_back_body(starts_ref, heads_ref, g_ref, a_ref, spread_ref, d_total_ref, mem_ref,
                    d_ref, mask_ref):
    length = heads_ref.shape[2]

    @pl.when(pl.program_id(0) == 0)
    def _():
        mask_ref[...] = visible(doc_begin_row(starts_ref, length), length)

    enters = enters_row(starts_ref, length)
    q, k, v, c = parts(heads_ref)
    g, a, spread, d_total = g_ref[...], a_ref[...], spread_ref[...], d_total_ref[...]
    mem_k = mem_ref[:, :HEAD]
    steps = causal_pairs(c, a, mask_ref)
    d_ref[0, :HEAD, :] = causal_sum(k, steps) + enters * tn(mem_k, a)
    d_ref[0, HEAD : 2 * HEAD, :] = causal_back(q, steps)
    links = causal_pairs(c, spread, mask_ref)
    d_ref[0, 2 * HEAD : 3 * HEAD, :] = causal_back(g, links)
    d_ref[0, 3 * HEAD :, :] = (
        causal_back(a, causal_pairs(k, q, mask_ref))
        + causal_back(spread, causal_pairs(v, g, mask_ref))
        + causal_back(d_total, mask_pair(mask_ref))
    )


def heads_back(starts, heads, g, a, spread, d_total, mem):
    length = heads.shape[2]
    width = HEADS * HEAD
    row = ROW_BLOCK(length)
    return call(
        heads_back_body,
        (HEADS,),
        [SMEM, HEAD_BLOCK(4 * HEAD, length), row, row, row, row, pl.BlockSpec((HEAD, 128), lambda h: (h, 0))],
        HEAD_BLOCK(4 * HEAD, length),
        jax.ShapeDtypeStruct((HEADS, 4 * HEAD, length), F32),
        [pltpu.VMEM((length, length), BF)],
        flops=20 * length * length * width,
    )(starts, heads, g, a, spread, d_total, mem)


def project_back_body(starts_ref, heads_ref, d_ref, control_ref, partner_ref, far_ref, xnt_ref,
                      wq_ref, wk_ref, wv_ref, wc_ref, x_ref, gain_ref, d_hidden1_ref,
                      send_ref, keep_ref, grad_x_ref, gain_grad_ref, bias_grad_ref,
                      mem_ref, totals_ref, proj_ref, dx_ref):
    j = pl.program_id(0)
    length = x_ref.shape[0]
    ffn = lax.axis_index("ffn")

    @pl.when(j == 0)
    def _():
        arrived(True, length, starts_ref, partner_ref, far_ref, mem_ref, totals_ref)

    pair = jnp.where(j < 2, 1 - ffn, ffn) * 2 + j % 2
    tail = tail_row(doc_begin_row(starts_ref, length), length)
    for i in range(2):
        rows = pl.ds(pl.multiple_of((pair * 2 + i) * HEAD, HEAD), HEAD)
        mem = mem_ref[rows, :]
        back_k, back_vt = mem[:, :HEAD], mem[:, HEAD:]
        k, v, c = [heads_ref[i, m * HEAD : m * HEAD + HEAD, :] for m in (1, 2, 3)]
        c_tail = (c.astype(F32) * tail).astype(BF)
        d_q = d_ref[i, :HEAD, :]
        d_k = d_ref[i, HEAD : 2 * HEAD, :] + tn(back_k, c_tail)
        d_v = d_ref[i, 2 * HEAD : 3 * HEAD, :] + nn(back_vt, c_tail)
        d_c = d_ref[i, 3 * HEAD :, :] + tail * (
            nn(back_k, k) + tn(back_vt, v) + totals_ref[rows, 0:1]
        )
        d_c = d_c * control_ref[i * HEAD : i * HEAD + HEAD, :]
        for m, value in enumerate((d_q, d_k, d_v, d_c)):
            proj_ref[m * 128 + i * HEAD : m * 128 + i * HEAD + HEAD, :] = value.astype(BF)
    d_proj = proj_ref[...]
    grad = nt(xnt_ref[...], d_proj).astype(BF)

    @pl.when(j < 2)
    def _():
        send_ref[...] = grad

    @pl.when(j >= 2)
    def _():
        keep_ref[...] = grad

    w = jnp.concatenate([wq_ref[...], wk_ref[...], wv_ref[...], wc_ref[...]], axis=1)
    dx = nn(w, d_proj)

    @pl.when(j == 0)
    def _():
        dx_ref[...] = dx

    @pl.when(j > 0)
    def _():
        dx_ref[...] += dx

    @pl.when(j == 3)
    def _():
        x = x_ref[...].astype(F32)
        mean = jnp.mean(x, axis=-1, keepdims=True)
        centered = x - mean
        inverse = lax.rsqrt(jnp.mean(centered * centered, axis=-1, keepdims=True) + EPSILON)
        n = centered * inverse
        d = dx_ref[...].T
        gain_grad_ref[...] = jnp.broadcast_to(jnp.sum(d * n, axis=0, keepdims=True), gain_grad_ref.shape)
        bias_grad_ref[...] = jnp.broadcast_to(jnp.sum(d, axis=0, keepdims=True), bias_grad_ref.shape)
        d_n = d * gain_ref[...]
        grad_x_ref[...] = d_hidden1_ref[...] + (
            d_n
            - jnp.mean(d_n, axis=-1, keepdims=True)
            - n * jnp.mean(d_n * n, axis=-1, keepdims=True)
        ) * inverse


def project_back(starts, heads, d, control, partner, far, xnt, w, x, gain, d_hidden1):
    length, width = x.shape
    square = whole((length, width))
    row, vec = whole((1, width)), whole((8, width))

    def pair(j):
        ffn = lax.axis_index("ffn")
        return jnp.where(j < 2, 1 - ffn, ffn) * 2 + j % 2

    two = pl.BlockSpec((2, 4 * HEAD, length), lambda j: (pair(j), 0, 0))
    weights = [
        pl.BlockSpec((width, 128), functools.partial(lambda m, j: (0, 4 * m + pair(j)), m))
        for m in range(4)
    ]
    return call(
        project_back_body,
        (4,),
        [SMEM, two, two, pl.BlockSpec((128, length), lambda j: (pair(j), 0)),
         whole((PACK, 128)), whole((PACK, 128)), square]
        + weights
        + [square, row, square],
        [
            pl.BlockSpec((width, 512), lambda j: (0, jnp.minimum(j, 1))),
            pl.BlockSpec((width, 512), lambda j: (0, jnp.maximum(j - 2, 0))),
            square, vec, vec,
        ],
        [
            jax.ShapeDtypeStruct((width, 1024), BF),
            jax.ShapeDtypeStruct((width, 1024), BF),
            jax.ShapeDtypeStruct((length, width), F32),
            jax.ShapeDtypeStruct((8, width), F32),
            jax.ShapeDtypeStruct((8, width), F32),
        ],
        [
            pltpu.VMEM((width, 128), BF), pltpu.VMEM((width, 8), F32),
            pltpu.VMEM((512, length), BF), pltpu.VMEM((width, length), F32),
        ],
        flops=2 * length * width * 2048 * 2,
    )(starts, heads, d, control, partner, far, xnt, w, w, w, w, x, gain, d_hidden1)


def scatter_plan():
    count = lax.axis_size("dp")
    bits = [("seq", 1)]
    step = 1
    while step < count:
        bits.append(("dp", step))
        step *= 2
    return bits


def reduce_rows(group, lead):
    bits = scatter_plan()
    order = [(i + lead) % 3 for i in range(3)] + list(range(3, len(bits)))
    rows, width = group.shape
    value = group.reshape((2,) * len(bits) + (rows >> len(bits), width))
    left = list(reversed(range(len(bits))))
    for b in order:
        axis, step = bits[b]
        at = left.index(b)
        mine = (lax.axis_index(axis) // step) % 2
        keep = lax.dynamic_index_in_dim(value, mine, at, False)
        send = lax.dynamic_index_in_dim(value, 1 - mine, at, False)
        left.pop(at)
        value = keep.astype(F32) + swap(send.astype(BF), axis, step).astype(F32)
    return value


def on_device(tokens, doc_starts, norm1_gain, norm1_bias, in_weight, out_weight,
              norm2_gain, norm2_bias, up_own, down_own, output_cotangent):
    ffn = lax.axis_index("ffn")
    is_first = ffn == 0
    up_other, down_other = swap(up_own, "ffn", 1), swap(down_own, "ffn", 1)
    x, cotangent, starts = tokens[0], output_cotangent[0], doc_starts
    length, width = x.shape
    row = lambda a: a.reshape(1, width)

    heads, control, xnt, own = project(x, row(norm1_gain), row(norm1_bias), in_weight, starts)
    partner = swap(own, "ffn", 1)
    both = combine(False, length, starts, own, partner)
    far = lax.ppermute(both, "seq", [(0, 1)])
    number, total = local_sums(starts, heads)
    number, total, mixed, memory = mix(starts, heads, number, total, partner, far)
    (output, d_hidden1, g, grad_out, gain2, bias2,
     gup_own, gup_other, gdown_own, gdown_other) = feed(
        x, mixed, cotangent, out_weight, row(norm2_gain), row(norm2_bias),
        up_own, up_other, down_own, down_other)
    a, spread, d_total, d_own = scores_back(starts, heads, g, number, total, memory)
    d_partner = swap(d_own, "ffn", 1)
    d_both = combine(True, length, starts, d_own, d_partner)
    d_far = lax.ppermute(d_both, "seq", [(1, 0)])
    d_heads = heads_back(starts, heads, g, a, spread, d_total, memory)
    send, keep, grad_tokens, gain1, bias1 = project_back(
        starts, heads, d_heads, control, d_partner, d_far, xnt, in_weight, x,
        row(norm1_gain), d_hidden1)

    grad_up = gup_own.astype(F32) + swap(gup_other, "ffn", 1).astype(F32)
    grad_down = gdown_own.astype(F32) + swap(gdown_other, "ffn", 1).astype(F32)
    grad_in = keep.astype(F32) + swap(send, "ffn", 1).astype(F32)

    def core_half(a):
        half_width = a.shape[1] // 2
        kept = lax.dynamic_slice_in_dim(a, ffn * half_width, half_width, 1)
        sent = lax.dynamic_slice_in_dim(a, (1 - ffn) * half_width, half_width, 1)
        return kept.astype(F32) + swap(sent, "ffn", 1).astype(F32)

    def core_join(a):
        a = a.astype(BF)
        other = swap(a, "ffn", 1)
        return jnp.where(is_first, a, other), jnp.where(is_first, other, a)

    norms = jnp.stack([gain1[0], bias1[0], gain2[0], bias2[0]], axis=1)
    norms = norms + swap(norms, "ffn", 1)
    grad_down = reduce_rows(grad_down, 0)
    grad_up = reduce_rows(grad_up, 1)
    grad_out = jnp.concatenate(core_join(reduce_rows(core_half(grad_out), 2)), axis=1).astype(F32)
    lo, hi = core_join(reduce_rows(grad_in, 2))
    count = lo.shape[0]
    both_halves = jnp.stack([lo.reshape(count, 2, 4, 128), hi.reshape(count, 2, 4, 128)], axis=1)
    grad_in = both_halves.transpose(0, 3, 1, 2, 4).reshape(count, 2048).astype(F32)
    norms = reduce_rows(norms, 1)
    return (
        output[None], grad_tokens[None], grad_in, grad_out, grad_up, grad_down,
        norms[:, 0], norms[:, 1], norms[:, 2], norms[:, 3],
    )


def solution(mesh):
    rows = P("dp", ("seq", "ffn"), None)
    owned = P(("dp", "seq"))
    return jax.shard_map(
        on_device,
        mesh=mesh,
        in_specs=(
            rows, P("dp", None), P(), P(), P(), P(), P(), P(),
            P(None, "ffn"), P(None, "ffn"), rows,
        ),
        out_specs=(
            rows, rows, P(("dp", "seq"), None), P(("dp", "seq"), None),
            P(("dp", "seq"), "ffn"), P(("dp", "seq"), "ffn"),
            owned, owned, owned, owned,
        ),
        check_vma=False,
    )
```

```python
import functools

import jax
import jax.numpy as jnp
from jax import lax
from jax.experimental import pallas as pl
from jax.experimental.pallas import tpu as pltpu
from jax.sharding import PartitionSpec as P

HEADS = 8
HEAD = 64
EPSILON = 1e-05
BF = jnp.bfloat16
F32 = jnp.float32
GELU_A = 0.7978845608028654
GELU_B = 0.044715
SCALE = HEAD**-0.5
PACK = HEADS * HEAD + 64


def nn(a, b):
    return lax.dot_general(a, b, (((1,), (0,)), ((), ())), preferred_element_type=F32)


def nt(a, b):
    return lax.dot_general(a, b, (((1,), (1,)), ((), ())), preferred_element_type=F32)


def tn(a, b):
    return lax.dot_general(a, b, (((0,), (0,)), ((), ())), preferred_element_type=F32)


def swap(a, axis, bit):
    size = lax.axis_size(axis)
    return lax.ppermute(a, axis, [(i, i ^ bit) for i in range(size)])


ANY = pl.BlockSpec(memory_space=pl.ANY)


def call(body, grid, in_specs, out_specs, out_shape, scratch=(), us=1.0, after=(), vmem=32):
    count = len(in_specs)

    def run(*refs):
        body(*refs[:count], *refs[count + len(after) :])

    def start(*operands):
        return pl.pallas_call(
            run,
            grid=grid,
            in_specs=list(in_specs) + [ANY] * len(after),
            out_specs=out_specs,
            out_shape=out_shape,
            scratch_shapes=list(scratch),
            cost_estimate=pl.CostEstimate(flops=int(us * 1.15e9), bytes_accessed=2**20, transcendentals=0),
            compiler_params=pltpu.CompilerParams(vmem_limit_bytes=vmem * 2**20),
        )(*operands, *after)

    return start


def whole(shape):
    return pl.BlockSpec(shape, lambda *_: (0,) * len(shape))


SMEM = pl.BlockSpec(memory_space=pltpu.SMEM)


def shard_of():
    return lax.axis_index("seq") * 2 + lax.axis_index("ffn")


def doc_begin_row(starts_ref, length):
    begin = shard_of() * length
    place = lax.broadcasted_iota(jnp.int32, (1, length), 1)
    row = jnp.full((1, length), -(2**30), jnp.int32)
    for j in range(starts_ref.shape[1]):
        s = starts_ref[0, j] - begin
        row = jnp.where(place >= s, jnp.maximum(row, s), row)
    return row


def passes(starts_ref, which, length):
    hit = jnp.int32(0)
    for j in range(starts_ref.shape[1]):
        s = starts_ref[0, j]
        hit = hit | ((s >= which * length) & (s < which * length + length)).astype(jnp.int32)
    return 1.0 - hit.astype(F32)


def visible(doc_row, length):
    i = lax.broadcasted_iota(jnp.int32, (length, length), 0)
    t = lax.broadcasted_iota(jnp.int32, (length, length), 1)
    return jnp.where((i <= t) & (i >= doc_row), 1.0, 0.0).astype(BF)


def tail_row(doc_row, length):
    place = lax.broadcasted_iota(jnp.int32, (1, length), 1)
    last = doc_row[:, length - 1 :]
    return jnp.where(place >= last, 1.0, 0.0)


def pack_totals(pack_ref, totals8):
    base = HEADS * HEAD
    hi = totals8.astype(BF)
    lo = (totals8 - hi.astype(F32)).astype(BF)
    for a in range(4):
        cols = slice(128 * a, 128 * a + 128)
        pack_ref[base + 16 * a : base + 16 * a + 16, :] = jnp.concatenate(
            [hi[:, cols], lo[:, cols]], axis=0
        )


def unpack(rows, totals8_of):
    base = HEADS * HEAD
    out = []
    for a in range(4):
        block = totals8_of(slice(base + 16 * a, base + 16 * a + 16))
        out.append(block[:8] + block[8:])
    return rows(slice(0, base)), jnp.concatenate(out, axis=1)


def combine_body(backward, length, starts_ref, own_ref, partner_ref, out_ref):
    first = 2 * lax.axis_index("seq")
    is_first = (lax.axis_index("ffn") == 0).astype(F32)
    base = HEADS * HEAD
    if backward:
        p = passes(starts_ref, first, length)
        own_by, partner_by = is_first + (1 - is_first) * p, is_first * p + (1 - is_first)
    else:
        p = passes(starts_ref, first + 1, length)
        own_by, partner_by = is_first * p + (1 - is_first), is_first + (1 - is_first) * p

    def sum_of(at):
        return own_ref[at, :].astype(F32) * own_by + partner_ref[at, :].astype(F32) * partner_by

    memory, totals8 = unpack(sum_of, sum_of)
    out_ref[:base, :] = memory.astype(BF)
    pack_totals(out_ref, totals8)


def combine(backward, length, starts, own, partner, after=()):
    return call(
        functools.partial(combine_body, backward, length),
        (),
        [SMEM, whole((PACK, 128)), whole((PACK, 128))],
        whole((PACK, 128)),
        jax.ShapeDtypeStruct((PACK, 128), BF),
        after=after,
    )(starts, own, partner)


def arrived(backward, length, starts_ref, partner_ref, far_ref, mem_ref, totals_ref):
    first = 2 * lax.axis_index("seq")
    is_first = (lax.axis_index("ffn") == 0).astype(F32)
    if backward:
        p = passes(starts_ref, first + 1, length)
        far_by, partner_by = is_first * p + (1 - is_first), is_first
    else:
        p = passes(starts_ref, first, length)
        far_by, partner_by = is_first + (1 - is_first) * p, 1 - is_first

    def sum_of(at):
        return far_ref[at, :].astype(F32) * far_by + partner_ref[at, :].astype(F32) * partner_by

    memory, totals8 = unpack(sum_of, sum_of)
    mem_ref[...] = memory.astype(BF)
    totals_ref[...] = totals8.T


def project_body(x_hbm, gain_hbm, bias_hbm, w_hbm, starts_ref,
                 heads_ref, control_ref, xnt_ref, pack_ref,
                 x_ref, gain_ref, bias_ref, w_ref, sems):
    length, width = x_ref.shape
    copies = [
        pltpu.make_async_copy(x_hbm, x_ref, sems.at[0]),
        pltpu.make_async_copy(gain_hbm, gain_ref, sems.at[1]),
        pltpu.make_async_copy(bias_hbm, bias_ref, sems.at[2]),
    ]
    columns = [
        pltpu.make_async_copy(w_hbm.at[:, pl.ds(j * width, width)], w_ref.at[j], sems.at[3 + j])
        for j in range(4)
    ]
    for copy in copies + columns:
        copy.start()
    for copy in copies:
        copy.wait()
    x = x_ref[...].astype(F32)
    mean = jnp.mean(x, axis=-1, keepdims=True)
    centered = x - mean
    inverse = lax.rsqrt(jnp.mean(centered * centered, axis=-1, keepdims=True) + EPSILON)
    xn = (centered * inverse * gain_ref[...] + bias_ref[...]).astype(BF)
    xnt_ref[...] = xn.T
    for j in range(3):
        columns[j].wait()
        t = nn(xn, w_ref[j]).astype(BF).T
        for h in range(HEADS):
            heads_ref[h, j * HEAD : j * HEAD + HEAD, :] = t[h * HEAD : h * HEAD + HEAD]
    columns[3].wait()
    control = jnp.exp(nn(xn, w_ref[3])).T
    control_ref[...] = control
    c = control.astype(BF)
    tail = tail_row(doc_begin_row(starts_ref, length), length)
    c_tail = c * tail.astype(BF)
    for h in range(HEADS):
        rows = slice(h * HEAD, h * HEAD + HEAD)
        heads_ref[h, 3 * HEAD :, :] = c[rows]
        mem_k = nt(c_tail[rows], heads_ref[h, HEAD : 2 * HEAD, :])
        mem_vt = nt(heads_ref[h, 2 * HEAD : 3 * HEAD, :], c_tail[rows])
        pack_ref[rows, :] = jnp.concatenate([mem_k, mem_vt], axis=1).astype(BF)
    tail8 = jnp.broadcast_to(tail, (8, length)).astype(BF)
    pack_totals(pack_ref, nt(tail8, c))


def project(x, gain, bias, w, starts):
    length, width = x.shape
    hbm = pl.BlockSpec(memory_space=pltpu.MemorySpace.HBM)
    return call(
        project_body,
        (),
        [hbm, hbm, hbm, hbm, SMEM],
        [
            whole((HEADS, 4 * HEAD, length)), whole((width, length)), whole((width, length)),
            whole((PACK, 128)),
        ],
        [
            jax.ShapeDtypeStruct((HEADS, 4 * HEAD, length), BF),
            jax.ShapeDtypeStruct((width, length), F32),
            jax.ShapeDtypeStruct((width, length), BF),
            jax.ShapeDtypeStruct((PACK, 128), BF),
        ],
        [
            pltpu.VMEM((length, width), BF), pltpu.VMEM((1, width), F32), pltpu.VMEM((1, width), F32),
            pltpu.VMEM((4, width, width), BF), pltpu.SemaphoreType.DMA((7,)),
        ],
        us=4.3,
        vmem=57,
    )(x, gain, bias, w, starts)


HEAD_BLOCK = lambda rows, length: pl.BlockSpec((1, rows, length), lambda h: (h, 0, 0))
ROW_BLOCK = lambda length: pl.BlockSpec((HEAD, length), lambda h: (h, 0))


def causal_pairs(left, right, mask_ref):
    half = mask_ref.shape[0] // 2
    rows = left.T
    a = nn(rows[:half], right[:, :half]).astype(BF) * mask_ref[:half, :half]
    b = nn(rows, right[:, half:]).astype(BF) * mask_ref[:, half:]
    return a, b


def causal_sum(left, pairs):
    a, b = pairs
    half = a.shape[0]
    return jnp.concatenate([nn(left[:, :half], a), nn(left, b)], axis=1)


def causal_back(left, pairs):
    a, b = pairs
    half = a.shape[0]
    late = nt(left[:, half:], b)
    return jnp.concatenate([late[:, :half] + nt(left[:, :half], a), late[:, half:]], axis=1)


def mask_pair(mask_ref):
    half = mask_ref.shape[0] // 2
    return mask_ref[:half, :half], mask_ref[:, half:]


def parts(heads_ref):
    return [heads_ref[0, j * HEAD : j * HEAD + HEAD, :] for j in range(4)]


def local_body(starts_ref, heads_ref, number_ref, total_ref, mask_ref):
    length = heads_ref.shape[2]

    @pl.when(pl.program_id(0) == 0)
    def _():
        mask_ref[...] = visible(doc_begin_row(starts_ref, length), length)

    q, k, v, c = parts(heads_ref)
    number_ref[...] = causal_sum(c, causal_pairs(k, q, mask_ref))
    total_ref[...] = causal_sum(c, mask_pair(mask_ref))


def local_sums(starts, heads, begin, count, after=()):
    length = heads.shape[2]
    return call(
        local_body,
        (count,),
        [SMEM, pl.BlockSpec((1, 4 * HEAD, length), lambda h: (h + begin, 0, 0))],
        [ROW_BLOCK(length)] * 2,
        [jax.ShapeDtypeStruct((count * HEAD, length), F32)] * 2,
        [pltpu.VMEM((length, length), BF)],
        us=0.75 * count,
        after=after,
    )(starts, heads)


def enters_row(starts_ref, length):
    return jnp.where(doc_begin_row(starts_ref, length) < 0, 1.0, 0.0)


def softmax(number, inverse):
    score = number * (inverse * SCALE)
    e = jnp.exp(score - jnp.max(score, axis=0, keepdims=True))
    return e / jnp.sum(e, axis=0, keepdims=True)


def mix_body(starts_ref, heads_ref, number_a, number_b, total_a, total_b, partner_ref, far_ref,
             number_out, total_out, mixed_ref, mem_out, mask_ref, mem_ref, totals_ref):
    length = heads_ref.shape[2]
    h = pl.program_id(0)

    @pl.when(h == 0)
    def _():
        mask_ref[...] = visible(doc_begin_row(starts_ref, length), length)
        arrived(False, length, starts_ref, partner_ref, far_ref, mem_ref, totals_ref)
        mem_out[...] = mem_ref[...]

    enters = enters_row(starts_ref, length)
    rows = pl.ds(pl.multiple_of(h * HEAD, HEAD), HEAD)
    q, k, v, c = parts(heads_ref)
    mem = mem_ref[rows, :]
    mem_k, mem_vt = mem[:, :HEAD], mem[:, HEAD:]
    early = h < HEADS // 2
    number = jnp.where(early, number_a[...], number_b[...]) + enters * nn(mem_k, q)
    total = jnp.where(early, total_a[...], total_b[...]) + enters * totals_ref[rows, 0:1]
    number_out[...] = number
    total_out[...] = total
    inverse = 1.0 / total
    spread = (softmax(number, inverse) * inverse).astype(BF)
    links = causal_pairs(c, spread, mask_ref)
    mixed = causal_sum(v, links) + enters * nn(mem_vt, spread)
    mixed_ref[...] = mixed.astype(BF)


def mix(starts, heads, number_a, total_a, number_b, total_b, partner, far):
    length = heads.shape[2]
    width = HEADS * HEAD
    a = pl.BlockSpec((HEAD, length), lambda h: (jnp.minimum(h, HEADS // 2 - 1), 0))
    b = pl.BlockSpec((HEAD, length), lambda h: (jnp.maximum(h - HEADS // 2, 0), 0))
    return call(
        mix_body,
        (HEADS,),
        [SMEM, HEAD_BLOCK(4 * HEAD, length), a, b, a, b,
         whole((PACK, 128)), whole((PACK, 128))],
        [ROW_BLOCK(length), ROW_BLOCK(length), ROW_BLOCK(length), whole((width, 128))],
        [
            jax.ShapeDtypeStruct((width, length), F32),
            jax.ShapeDtypeStruct((width, length), F32),
            jax.ShapeDtypeStruct((width, length), BF),
            jax.ShapeDtypeStruct((width, 128), BF),
        ],
        [pltpu.VMEM((length, length), BF), pltpu.VMEM((width, 128), BF), pltpu.VMEM((width, 8), F32)],
        us=6.0,
    )(starts, heads, number_a, number_b, total_a, total_b, partner, far)


def feed_step(xn_ref, cot_ref, xnt_ref, cott_ref, up_ref, down_ref, gup_ref, gdown_ref):
    up, down = up_ref[...], down_ref[...]
    pre = nn(xn_ref[...], up)
    v2 = pre * pre
    th = jnp.tanh(GELU_A * pre * (1.0 + GELU_B * v2))
    half = 0.5 * (1.0 + th)
    hidden = (pre * half).astype(BF)
    slope = half + 0.5 * pre * (1.0 - th * th) * (GELU_A * (1.0 + 3.0 * GELU_B * v2))
    grad_pre = (nn(cot_ref[...], down) * slope).astype(BF)
    gdown_ref[...] = nn(cott_ref[...], hidden).astype(BF)
    gup_ref[...] = nn(xnt_ref[...], grad_pre).astype(BF)
    return nt(hidden, down), nt(grad_pre, up)


def feed_other_body(x_ref, mixed_ref, cot_ref, w_out_ref, gain_ref, bias_ref, up_ref, down_ref,
                    gup_ref, gdown_ref, hidden1_ref, n_ref, inv_ref, xn_ref, xnt_ref, cott_ref,
                    part_ref, d_ref):
    j = pl.program_id(0)

    @pl.when(j == 0)
    def _():
        hidden1 = x_ref[...].astype(F32) + tn(mixed_ref[...], w_out_ref[...])
        hidden1_ref[...] = hidden1
        mean = jnp.mean(hidden1, axis=-1, keepdims=True)
        centered = hidden1 - mean
        inverse = lax.rsqrt(jnp.mean(centered * centered, axis=-1, keepdims=True) + EPSILON)
        n = centered * inverse
        n_ref[...] = n
        inv_ref[...] = jnp.broadcast_to(inverse, inv_ref.shape)
        xn = (n * gain_ref[...] + bias_ref[...]).astype(BF)
        xn_ref[...] = xn
        xnt_ref[...] = xn.T
        cott_ref[...] = cot_ref[...].T

    part, d = feed_step(xn_ref, cot_ref, xnt_ref, cott_ref, up_ref, down_ref, gup_ref, gdown_ref)

    @pl.when(j == 0)
    def _():
        part_ref[...] = part
        d_ref[...] = d

    @pl.when(j > 0)
    def _():
        part_ref[...] += part
        d_ref[...] += d


def feed_own_body(hidden1_ref, n_ref, inv_ref, xn_ref, xnt_ref, cott_ref, part_ref, d_in_ref,
                  mixed_ref, cot_ref, w_out_ref, gain_ref, up_ref, down_ref,
                  output_ref, d_hidden1_ref, g_ref, out_send_ref, out_keep_ref, norms_ref,
                  gup_ref, gdown_ref, sum_ref, d_ref):
    j = pl.program_id(0)
    part, d = feed_step(xn_ref, cot_ref, xnt_ref, cott_ref, up_ref, down_ref, gup_ref, gdown_ref)

    @pl.when(j == 0)
    def _():
        sum_ref[...] = part_ref[...] + part
        d_ref[...] = d_in_ref[...] + d

    @pl.when(j == 1)
    def _():
        output_ref[...] = (hidden1_ref[...] + (sum_ref[...] + part)).astype(BF)
        dx, n = d_ref[...] + d, n_ref[...]
        norms_ref[...] = jnp.concatenate(
            [jnp.sum(dx * n, axis=0, keepdims=True), jnp.sum(dx, axis=0, keepdims=True)] * 4, axis=0
        )
        d_n = dx * gain_ref[...]
        d_in = (
            d_n
            - jnp.mean(d_n, axis=-1, keepdims=True)
            - n * jnp.mean(d_n * n, axis=-1, keepdims=True)
        ) * inv_ref[:, 0:1]
        d_hidden1 = cot_ref[...].astype(F32) + d_in
        d_hidden1_ref[...] = d_hidden1
        d_branch = d_hidden1.astype(BF)
        grad_out = nn(mixed_ref[...], d_branch).astype(BF)
        half = grad_out.shape[1] // 2
        second = lax.axis_index("ffn") == 1
        out_keep_ref[...] = jnp.where(second, grad_out[:, half:], grad_out[:, :half])
        out_send_ref[...] = jnp.where(second, grad_out[:, :half], grad_out[:, half:])
        g_ref[...] = nt(w_out_ref[...], d_branch).astype(BF)


FEED_COLS = pl.BlockSpec((512, 512), lambda j: (0, j))


def feed_other(x, mixed, cotangent, w_out, gain, bias, up, down):
    length, width = x.shape
    square, row = whole((length, width)), whole((1, width))
    sq = lambda dt: jax.ShapeDtypeStruct((length, width), dt)
    half = jax.ShapeDtypeStruct(up.shape, BF)
    return call(
        feed_other_body,
        (2,),
        [square] * 4 + [row, row, FEED_COLS, FEED_COLS],
        [FEED_COLS, FEED_COLS, square, square, whole((length, 128))] + [square] * 5,
        [half, half, sq(F32), sq(F32), jax.ShapeDtypeStruct((length, 128), F32),
         sq(BF), sq(BF), sq(BF), sq(F32), sq(F32)],
        us=6.5,
    )(x, mixed, cotangent, w_out, gain, bias, up, down)


def feed_own(saved, mixed, cotangent, w_out, gain, up, down, after=()):
    length, width = mixed.shape
    square, row = whole((length, width)), whole((1, width))
    sq = lambda dt: jax.ShapeDtypeStruct((length, width), dt)
    half = jax.ShapeDtypeStruct(up.shape, BF)
    narrow = whole((width, width // 2))
    return call(
        feed_own_body,
        (2,),
        [square, square, whole((length, 128))] + [square] * 5
        + [square] * 3 + [row, FEED_COLS, FEED_COLS],
        [square] * 3 + [narrow, narrow, whole((8, width)), FEED_COLS, FEED_COLS],
        [sq(BF), sq(F32), sq(BF)] + [jax.ShapeDtypeStruct((width, width // 2), BF)] * 2
        + [jax.ShapeDtypeStruct((8, width), F32), half, half],
        [pltpu.VMEM((length, width), F32)] * 2,
        us=6.5,
        after=after,
    )(*saved, mixed, cotangent, w_out, gain, up, down)


def head_of(own_side, h):
    ffn = lax.axis_index("ffn")
    return (ffn if own_side else 1 - ffn) * (HEADS // 2) + h


def scores_back_body(own_side, starts_ref, heads_ref, g_ref, number_ref, total_ref, mem_ref, *refs):
    if own_side:
        pack_in, sums_in, a_ref, spread_ref, d_total_ref, pack_ref, mask_ref, sums_ref = refs
    else:
        a_ref, spread_ref, d_total_ref, pack_ref, sums_ref, mask_ref = refs
    length = heads_ref.shape[2]
    h = pl.program_id(0)

    @pl.when(h == 0)
    def _():
        mask_ref[...] = visible(doc_begin_row(starts_ref, length), length)
        if own_side:
            pack_ref[...] = pack_in[...]
            sums_ref[...] = sums_in[...]

    enters = enters_row(starts_ref, length)
    rows = pl.ds(pl.multiple_of(head_of(own_side, h) * HEAD, HEAD), HEAD)
    q, k, v, c = parts(heads_ref)
    g = g_ref[...]
    mem_vt = mem_ref[:, HEAD:]
    number, inverse = number_ref[...], 1.0 / total_ref[...]
    weight = softmax(number, inverse)
    number_v = causal_sum(c, causal_pairs(v, g, mask_ref)) + enters * tn(mem_vt, g)
    d_weight = number_v * inverse
    d_score = weight * (d_weight - jnp.sum(weight * d_weight, axis=0, keepdims=True))
    a = d_score * (inverse * SCALE)
    spread = weight * inverse
    d_total = -(a * number + spread * number_v) * inverse
    a_ref[...] = a.astype(BF)
    spread_ref[...] = spread.astype(BF)
    d_total_ref[...] = d_total.astype(BF)
    d_k = nt((a * enters).astype(BF), q)
    d_vt = nt(g, (spread * enters).astype(BF))
    pack_ref[rows, :] = jnp.concatenate([d_k, d_vt], axis=1).astype(BF)
    sums_ref[rows, :] = jnp.broadcast_to(jnp.sum(d_total * enters, axis=1, keepdims=True), (HEAD, 128))

    if own_side:

        @pl.when(h == HEADS // 2 - 1)
        def _():
            pack_totals(pack_ref, sums_ref[...].T[0:8])


def scores_back(own_side, starts, heads, g, number, total, mem, packs=(), after=()):
    length = heads.shape[2]
    width, count = HEADS * HEAD, HEADS // 2
    row = pl.BlockSpec((HEAD, length), lambda h: (head_of(own_side, h), 0))
    half = pl.BlockSpec((HEAD, length), lambda h: (h, 0))
    pack, sums = jax.ShapeDtypeStruct((PACK, 128), BF), jax.ShapeDtypeStruct((width, 128), F32)
    scratch = [pltpu.VMEM((length, length), BF)]
    in_specs = [
        SMEM, pl.BlockSpec((1, 4 * HEAD, length), lambda h: (head_of(own_side, h), 0, 0)),
        row, row, row, pl.BlockSpec((HEAD, 128), lambda h: (head_of(own_side, h), 0)),
    ]
    out_specs = [half, half, half, whole((PACK, 128))]
    out_shape = [jax.ShapeDtypeStruct((count * HEAD, length), BF)] * 3 + [pack]
    if own_side:
        in_specs += [whole((PACK, 128)), whole((width, 128))]
        scratch += [pltpu.VMEM((width, 128), F32)]
    else:
        out_specs += [whole((width, 128))]
        out_shape += [sums]
    return call(
        functools.partial(scores_back_body, own_side),
        (count,),
        in_specs,
        out_specs,
        out_shape,
        scratch,
        us=3.0,
        after=after,
    )(starts, heads, g, number, total, mem, *packs)


def heads_back_body(starts_ref, heads_ref, g_ref, a_ref, spread_ref, d_total_ref, mem_ref,
                    d_ref, mask_ref):
    length = heads_ref.shape[2]

    @pl.when(pl.program_id(0) == 0)
    def _():
        mask_ref[...] = visible(doc_begin_row(starts_ref, length), length)

    enters = enters_row(starts_ref, length)
    q, k, v, c = parts(heads_ref)
    g, a, spread, d_total = g_ref[...], a_ref[...], spread_ref[...], d_total_ref[...]
    mem_k = mem_ref[:, :HEAD]
    steps = causal_pairs(c, a, mask_ref)
    d_ref[0, :HEAD, :] = causal_sum(k, steps) + enters * tn(mem_k, a)
    d_ref[0, HEAD : 2 * HEAD, :] = causal_back(q, steps)
    links = causal_pairs(c, spread, mask_ref)
    d_ref[0, 2 * HEAD : 3 * HEAD, :] = causal_back(g, links)
    d_ref[0, 3 * HEAD :, :] = (
        causal_back(a, causal_pairs(k, q, mask_ref))
        + causal_back(spread, causal_pairs(v, g, mask_ref))
        + causal_back(d_total, mask_pair(mask_ref))
    )


def heads_back(own_side, starts, heads, g, a, spread, d_total, mem, after=()):
    length = heads.shape[2]
    count = HEADS // 2
    head = functools.partial(head_of, own_side)
    row = pl.BlockSpec((HEAD, length), lambda h: (head(h), 0))
    half = pl.BlockSpec((HEAD, length), lambda h: (h, 0))
    return call(
        heads_back_body,
        (count,),
        [SMEM, pl.BlockSpec((1, 4 * HEAD, length), lambda h: (head(h), 0, 0)), row, half, half, half,
         pl.BlockSpec((HEAD, 128), lambda h: (head(h), 0))],
        HEAD_BLOCK(4 * HEAD, length),
        jax.ShapeDtypeStruct((count, 4 * HEAD, length), F32),
        [pltpu.VMEM((length, length), BF)],
        us=8.0 if own_side else 3.0,
        after=after,
    )(starts, heads, g, a, spread, d_total, mem)


def project_back_body(own_side, starts_ref, heads_ref, d_ref, control_ref, partner_ref, far_ref, xnt_ref,
                      wq_ref, wk_ref, wv_ref, wc_ref, *refs):
    if own_side:
        (dx_in_ref, x_ref, gain_ref, d_hidden1_ref, norms2_ref,
         grad_ref, grad_x_ref, norms_ref, mem_ref, totals_ref, proj_ref, dx_ref) = refs
    else:
        grad_ref, dx_ref, mem_ref, totals_ref, proj_ref = refs
    j = pl.program_id(0)
    length = xnt_ref.shape[1]
    ffn = lax.axis_index("ffn")

    @pl.when(j == 0)
    def _():
        arrived(True, length, starts_ref, partner_ref, far_ref, mem_ref, totals_ref)

    pair = (ffn if own_side else 1 - ffn) * 2 + j
    tail = tail_row(doc_begin_row(starts_ref, length), length)
    for i in range(2):
        rows = pl.ds(pl.multiple_of((pair * 2 + i) * HEAD, HEAD), HEAD)
        mem = mem_ref[rows, :]
        back_k, back_vt = mem[:, :HEAD], mem[:, HEAD:]
        k, v, c = [heads_ref[i, m * HEAD : m * HEAD + HEAD, :] for m in (1, 2, 3)]
        c_tail = (c.astype(F32) * tail).astype(BF)
        d_q = d_ref[i, :HEAD, :]
        d_k = d_ref[i, HEAD : 2 * HEAD, :] + tn(back_k, c_tail)
        d_v = d_ref[i, 2 * HEAD : 3 * HEAD, :] + nn(back_vt, c_tail)
        d_c = d_ref[i, 3 * HEAD :, :] + tail * (
            nn(back_k, k) + tn(back_vt, v) + totals_ref[rows, 0:1]
        )
        d_c = d_c * control_ref[i * HEAD : i * HEAD + HEAD, :]
        for m, value in enumerate((d_q, d_k, d_v, d_c)):
            proj_ref[m * 128 + i * HEAD : m * 128 + i * HEAD + HEAD, :] = value.astype(BF)
    d_proj = proj_ref[...]
    grad_ref[...] = nt(xnt_ref[...], d_proj).astype(BF)
    w = jnp.concatenate([wq_ref[...], wk_ref[...], wv_ref[...], wc_ref[...]], axis=1)
    dx = nn(w, d_proj)

    @pl.when(j == 0)
    def _():
        dx_ref[...] = dx_in_ref[...] + dx if own_side else dx

    @pl.when(j > 0)
    def _():
        dx_ref[...] += dx

    if own_side:

        @pl.when(j == 1)
        def _():
            x = x_ref[...].astype(F32)
            mean = jnp.mean(x, axis=-1, keepdims=True)
            centered = x - mean
            inverse = lax.rsqrt(jnp.mean(centered * centered, axis=-1, keepdims=True) + EPSILON)
            n = centered * inverse
            d = dx_ref[...].T
            sums = [jnp.sum(d * n, axis=0, keepdims=True), jnp.sum(d, axis=0, keepdims=True)]
            rows8 = jnp.concatenate(sums + [norms2_ref[0:6, :]], axis=0)
            columns = jnp.concatenate([rows8, jnp.zeros((120, length), F32)], axis=0).T
            norms_ref[...] = columns.astype(BF)
            d_n = d * gain_ref[...]
            grad_x_ref[...] = d_hidden1_ref[...] + (
                d_n
                - jnp.mean(d_n, axis=-1, keepdims=True)
                - n * jnp.mean(d_n * n, axis=-1, keepdims=True)
            ) * inverse


def project_back(own_side, starts, heads, d, control, partner, far, xnt, w, rest=(), after=()):
    width, length = xnt.shape
    square, row = whole((length, width)), whole((1, width))

    def pair(j):
        ffn = lax.axis_index("ffn")
        return (ffn if own_side else 1 - ffn) * 2 + j

    weights = [
        pl.BlockSpec((width, 128), functools.partial(lambda m, j: (0, 4 * m + pair(j)), m))
        for m in range(4)
    ]
    in_specs = [
        SMEM,
        pl.BlockSpec((2, 4 * HEAD, length), lambda j: (pair(j), 0, 0)),
        pl.BlockSpec((2, 4 * HEAD, length), lambda j: (j, 0, 0)),
        pl.BlockSpec((128, length), lambda j: (pair(j), 0)),
        whole((PACK, 128)), whole((PACK, 128)), square,
    ] + weights
    f32_square = jax.ShapeDtypeStruct((length, width), F32)
    out_specs, out_shape = [FEED_COLS], [jax.ShapeDtypeStruct((width, 1024), BF)]
    scratch = [pltpu.VMEM((width, 128), BF), pltpu.VMEM((width, 8), F32), pltpu.VMEM((512, length), BF)]
    if own_side:
        in_specs += [square, square, row, square, whole((8, width))]
        out_specs += [square, whole((width, 128))]
        out_shape += [f32_square, jax.ShapeDtypeStruct((width, 128), BF)]
        scratch += [pltpu.VMEM((width, length), F32)]
    else:
        out_specs += [square]
        out_shape += [f32_square]
    return call(
        functools.partial(project_back_body, own_side),
        (2,),
        in_specs,
        out_specs,
        out_shape,
        scratch,
        us=5.0 if own_side else 3.5,
        after=after,
    )(starts, heads, d, control, partner, far, xnt, w, w, w, w, *rest)


def bit_axis(bit):
    return ("seq", 1) if bit == 0 else ("dp", 1 << (bit - 1))


def my_bit(bit):
    axis, step = bit_axis(bit)
    return (lax.axis_index(axis) // step) % 2


def send_across(a, bits):
    seqs, dps = lax.axis_size("seq"), lax.axis_size("dp")
    flip = sum(1 << bit for bit in bits)
    return lax.ppermute(a, ("dp", "seq"), [(i, i ^ flip) for i in range(seqs * dps)])


def place_of(t, places, values):
    index, rest, bit = 0, t, 0
    fixed = dict(zip(places, values))
    while rest or fixed:
        if bit in fixed:
            index = index + fixed.pop(bit) * (1 << bit)
        else:
            index = index + ((rest & 1) << bit)
            rest >>= 1
        bit += 1
    return index


def stage_body(plan, *refs):
    refs = list(refs)
    ins = [[[refs.pop(0) for _ in pieces] for pieces in arrays] for arrays, _, _ in plan]
    for (arrays, split, dtype), sources in zip(plan, ins):
        outs = [refs.pop(0) for _ in range(1 << len(split))]
        blocks = outs[0].shape[0]
        places = [place for _, place in split]
        mine = [my_bit(bit) for bit, _ in split]
        for pattern, out in enumerate(outs):
            values = [
                (1 - m) if (pattern >> n) & 1 else m for n, m in enumerate(mine)
            ]
            for t in range(blocks):
                at = place_of(t, places, values)
                total = None
                for pieces in sources:
                    row = jnp.concatenate([p[at] for p in pieces], axis=1) if len(pieces) > 1 else pieces[0][at]
                    row = row.astype(F32)
                    total = row if total is None else total + row
                out[t] = total.astype(out.dtype)


def stage(groups, after=(), dtype=BF):
    plan, operands, in_specs, out_specs, out_shape = [], [], [], [], []
    rows = groups[0][0][0][0][0].shape[1]
    steps = 2 if rows % 32 == 0 else 1
    for arrays, split in groups:
        for pieces in arrays:
            for array, first, count in pieces:
                operands.append(array)
                in_specs.append(
                    pl.BlockSpec((array.shape[0], rows // steps, count),
                                 functools.partial(lambda at, i: (0, i, at), first // count))
                )
        blocks, width = arrays[0][0][0].shape[0] >> len(split), sum(p[2] for p in arrays[0])
        plan.append(([[None] * len(pieces) for pieces in arrays], split, dtype))
        for _ in range(1 << len(split)):
            out_specs.append(pl.BlockSpec((blocks, rows // steps, width), lambda i: (0, i, 0)))
            out_shape.append(jax.ShapeDtypeStruct((blocks, rows, width), dtype))
    outs = list(
        call(functools.partial(stage_body, plan), (steps,), in_specs, out_specs, out_shape, after=after)(*operands)
    )
    result = []
    for _, split in groups:
        result.append([outs.pop(0) for _ in range(1 << len(split))])
    return result


def all_of(a):
    return [(a, 0, a.shape[2])]


def patterns(bits):
    return [[b for n, b in enumerate(bits) if (p >> n) & 1] for p in range(1, 1 << len(bits))]


def finish_body(a_ref, b_ref, up_ref, down_ref, out_ref):
    total = a_ref[0].astype(F32) + b_ref[0].astype(F32)
    half, part = up_ref.shape[1], out_ref.shape[1] // 2
    up_ref[...] = total[:, :half]
    down_ref[...] = total[:, half + part : 2 * half + part]
    out_ref[:, :part] = total[:, half : half + part].astype(BF)
    out_ref[:, part:] = total[:, 2 * half + part :].astype(BF)


def finish(a, b, half, part, after=()):
    rows = a.shape[1]
    return call(
        finish_body,
        (),
        [whole(a.shape)] * 2,
        [whole((rows, half)), whole((rows, half)), whole((rows, 2 * part))],
        [jax.ShapeDtypeStruct((rows, half), F32)] * 2 + [jax.ShapeDtypeStruct((rows, 2 * part), BF)],
        after=after,
    )(a, b)


def join_body(own_ref, other_ref, out_own, out_other, grad_in_ref, grad_out_ref, *norm_refs):
    second = lax.axis_index("ffn") == 1
    own, other = own_ref[0].astype(F32), other_ref[0].astype(F32)
    for f in range(2):
        keep_own = second if f else jnp.logical_not(second)
        half = jnp.where(keep_own, own[:, :1024], other[:, :1024])
        for p in range(2):
            for m in range(4):
                grad_in_ref[:, m * 512 + f * 256 + p * 128 : m * 512 + f * 256 + p * 128 + 128] = (
                    half[:, p * 512 + m * 128 : p * 512 + m * 128 + 128]
                )
        grad_out_ref[:, f * 256 : f * 256 + 256] = jnp.where(
            keep_own, out_own[...], out_other[...]
        ).astype(F32)
    norms = (own[:, 1024:] + other[:, 1024:]).T
    for n, ref in enumerate(norm_refs):
        ref[...] = norms[n]


def join(own, other, out_own, out_other):
    rows = own.shape[1]
    return call(
        join_body,
        (),
        [whole(own.shape)] * 2 + [whole(out_own.shape)] * 2,
        [whole((rows, 2048)), whole((rows, 512))] + [whole((rows,))] * 4,
        [jax.ShapeDtypeStruct((rows, n), F32) for n in (2048, 512)] + [jax.ShapeDtypeStruct((rows,), F32)] * 4,
    )(own, other, out_own, out_other)


def on_device(tokens, doc_starts, norm1_gain, norm1_bias, in_weight, out_weight,
              norm2_gain, norm2_bias, up_own, down_own, output_cotangent):
    up_other, down_other = swap(up_own, "ffn", 1), swap(down_own, "ffn", 1)
    x, cotangent, starts = tokens[0], output_cotangent[0], doc_starts
    length, width = x.shape
    owners = lax.axis_size("dp") * lax.axis_size("seq")
    bits = owners.bit_length() - 1
    row = lambda a: a.reshape(1, width)
    blocked = lambda a: a.reshape(owners, width // owners, a.shape[1])

    heads, control, xnt, own = project(x, row(norm1_gain), row(norm1_bias), in_weight, starts)
    partner = swap(own, "ffn", 1)
    local_a = local_sums(starts, heads, 0, 4)
    both = combine(False, length, starts, own, partner, after=local_a[:1])
    far = lax.ppermute(both, "seq", [(0, 1)])
    local_b = local_sums(starts, heads, 4, 4, after=[both])
    number, total, mixed, memory = mix(starts, heads, *local_a, *local_b, partner, far)
    gup_send, gdown_send, *saved = feed_other(
        x, mixed, cotangent, out_weight, row(norm2_gain), row(norm2_bias), up_other, down_other)
    gup_got, gdown_got = swap(gup_send, "ffn", 1), swap(gdown_send, "ffn", 1)
    (output, d_hidden1, g, out_send, out_keep, norms2, gup_own, gdown_own) = feed_own(
        saved, mixed, cotangent, out_weight, row(norm2_gain), up_own, down_own)
    out_got = swap(out_send, "ffn", 1)

    out_half = width // 4
    ups, downs, outs = [
        [blocked(a) for a in pair]
        for pair in ((gup_own, gup_got), (gdown_own, gdown_got), (out_keep, out_got))
    ]
    groups = [
        [[*all_of(a), (o, 0, out_half)] for a, o in zip(ups, outs)],
        [[*all_of(a), (o, out_half, out_half)] for a, o in zip(downs, outs)],
    ]
    orders = [[0, 1], [1, 0]]
    left = [list(range(bits)) for _ in groups]

    def advance(groups, n, after):
        if n >= 2:
            if n == 2:
                groups = [[pieces_a + pieces_b for pieces_a, pieces_b in zip(*groups)]]
            bits_now = [n]
            splits = [[(n, 0)]]
        else:
            bits_now = [order[n] for order in orders]
            splits = [[(bit, rest.index(bit))] for bit, rest in zip(bits_now, left)]
            for bit, rest in zip(bits_now, left):
                rest.remove(bit)
        outs = stage(list(zip(groups, splits)), after=after)
        got = [send_across(sent, [bit]) for (_, sent), bit in zip(outs, bits_now)]
        sent = [s for _, s in outs]
        return [[all_of(kept), all_of(r)] for (kept, _), r in zip(outs, got)], sent

    back = (starts, heads, g, number, total, memory)
    *scores_other, pack, sums = scores_back(False, *back)
    groups, sent = advance(groups, 0, [pack])
    *scores_own, d_own = scores_back(True, *back, packs=(pack, sums), after=sent)
    d_partner = swap(d_own, "ffn", 1)
    d_both = combine(True, length, starts, d_own, d_partner)
    d_far = lax.ppermute(d_both, "seq", [(1, 0)])
    side = (control, d_partner, d_far, xnt, in_weight)
    d_other = heads_back(False, starts, heads, g, *scores_other, memory, after=[d_both])
    groups, sent = advance(groups, 1, [d_other])
    in_send, dx = project_back(False, starts, heads, d_other, *side, after=sent)
    in_got = swap(in_send, "ffn", 1)
    d_mine = heads_back(True, starts, heads, g, *scores_own, memory, after=[in_send])
    groups, sent = advance(groups, 2, [d_mine])
    in_keep, grad_tokens, norms = project_back(
        True, starts, heads, d_mine, *side,
        rest=(dx, x, row(norm1_gain), d_hidden1, norms2), after=sent)

    late = [
        all_of(blocked(in_keep)) + all_of(blocked(norms)),
        all_of(blocked(in_got)) + all_of(jnp.zeros_like(blocked(norms))),
    ]
    rest = list(range(bits))
    first = True
    while rest:
        now = rest[:2]
        split = [(b, rest.index(b)) for b in now]
        rest = rest[2:]
        (kept, *sent), = stage([(late, split)])
        late = [all_of(kept)] + [all_of(send_across(s, p)) for s, p in zip(sent, patterns(now))]
        if first:
            first, token = False, [kept]
            for n in range(3, bits):
                groups, token = advance(groups, n, token)
    grad_up, grad_down, out = finish(*(a[0][0] for a in groups[0]), gup_own.shape[1], out_half, after=[kept])
    (final,), = stage([(late, [])], after=[out])
    grad_in, grad_out, *norms = join(final, swap(final, "ffn", 1), out, swap(out, "ffn", 1))
    return (output[None], grad_tokens[None], grad_in, grad_out, grad_up, grad_down, *norms)


def solution(mesh):
    rows = P("dp", ("seq", "ffn"), None)
    owned = P(("dp", "seq"))
    return jax.shard_map(
        on_device,
        mesh=mesh,
        in_specs=(
            rows, P("dp", None), P(), P(), P(), P(), P(), P(),
            P(None, "ffn"), P(None, "ffn"), rows,
        ),
        out_specs=(
            rows, rows, P(("dp", "seq"), None), P(("dp", "seq"), None),
            P(("dp", "seq"), "ffn"), P(("dp", "seq"), "ffn"),
            owned, owned, owned, owned,
        ),
        check_vma=False,
    )
```

```python
import functools

import jax
import jax.numpy as jnp
from jax import lax
from jax.experimental import pallas as pl
from jax.experimental.pallas import tpu as pltpu
from jax.sharding import PartitionSpec as P

HEADS = 8
HEAD = 64
EPSILON = 1e-05
BF = jnp.bfloat16
F32 = jnp.float32
GELU_A = 0.7978845608028654
GELU_B = 0.044715
SCALE = HEAD**-0.5
SIDE = HEADS // 2
PACK = HEADS * HEAD + 64


def nn(a, b):
    return lax.dot_general(a, b, (((1,), (0,)), ((), ())), preferred_element_type=F32)


def nt(a, b):
    return lax.dot_general(a, b, (((1,), (1,)), ((), ())), preferred_element_type=F32)


def tn(a, b):
    return lax.dot_general(a, b, (((0,), (0,)), ((), ())), preferred_element_type=F32)


def swap(a, axis, bit):
    size = lax.axis_size(axis)
    return lax.ppermute(a, axis, [(i, i ^ bit) for i in range(size)])


ANY = pl.BlockSpec(memory_space=pl.ANY)


def call(body, grid, in_specs, out_specs, out_shape, scratch=(), us=1.0, after=(), vmem=20):
    count = len(in_specs)

    def run(*refs):
        body(*refs[:count], *refs[count + len(after) :])

    def start(*operands):
        return pl.pallas_call(
            run,
            grid=grid,
            in_specs=list(in_specs) + [ANY] * len(after),
            out_specs=out_specs,
            out_shape=out_shape,
            scratch_shapes=list(scratch),
            cost_estimate=pl.CostEstimate(flops=int(us * 1.15e9), bytes_accessed=2**20, transcendentals=0),
            compiler_params=pltpu.CompilerParams(vmem_limit_bytes=vmem * 2**20),
        )(*operands, *after)

    return start


def whole(shape):
    return pl.BlockSpec(shape, lambda *_: (0,) * len(shape))


VM = pl.BlockSpec(memory_space=pltpu.MemorySpace.VMEM)


def shape(dtype, *dims):
    return jax.ShapeDtypeStruct(dims, dtype)


SMEM = pl.BlockSpec(memory_space=pltpu.SMEM)


def shard_of():
    return lax.axis_index("seq") * 2 + lax.axis_index("ffn")


def doc_begin_row(starts_ref, length):
    begin = shard_of() * length
    place = lax.broadcasted_iota(jnp.int32, (1, length), 1)
    row = jnp.full((1, length), -(2**30), jnp.int32)
    for j in range(starts_ref.shape[1]):
        s = starts_ref[0, j] - begin
        row = jnp.where(place >= s, jnp.maximum(row, s), row)
    return row


def passes(starts_ref, which, length):
    hit = jnp.int32(0)
    for j in range(starts_ref.shape[1]):
        s = starts_ref[0, j]
        hit = hit | ((s >= which * length) & (s < which * length + length)).astype(jnp.int32)
    return 1.0 - hit.astype(F32)


def visible(doc_row, length):
    i = lax.broadcasted_iota(jnp.int32, (length, length), 0)
    t = lax.broadcasted_iota(jnp.int32, (length, length), 1)
    return jnp.where((i <= t) & (i >= doc_row), 1.0, 0.0).astype(BF)


def tail_row(doc_row, length):
    place = lax.broadcasted_iota(jnp.int32, (1, length), 1)
    last = doc_row[:, length - 1 :]
    return jnp.where(place >= last, 1.0, 0.0)


def pack_totals(pack_ref, totals8):
    base = HEADS * HEAD
    hi = totals8.astype(BF)
    lo = (totals8 - hi.astype(F32)).astype(BF)
    for a in range(4):
        cols = slice(128 * a, 128 * a + 128)
        pack_ref[base + 16 * a : base + 16 * a + 16, :] = jnp.concatenate(
            [hi[:, cols], lo[:, cols]], axis=0
        )


def unpack(rows, totals8_of):
    base = HEADS * HEAD
    out = []
    for a in range(4):
        block = totals8_of(slice(base + 16 * a, base + 16 * a + 16))
        out.append(block[:8] + block[8:])
    return rows(slice(0, base)), jnp.concatenate(out, axis=1)


def combine_body(backward, length, starts_ref, own_ref, partner_ref, out_ref):
    first = 2 * lax.axis_index("seq")
    is_first = (lax.axis_index("ffn") == 0).astype(F32)
    base = HEADS * HEAD
    if backward:
        p = passes(starts_ref, first, length)
        own_by, partner_by = is_first + (1 - is_first) * p, is_first * p + (1 - is_first)
    else:
        p = passes(starts_ref, first + 1, length)
        own_by, partner_by = is_first * p + (1 - is_first), is_first + (1 - is_first) * p

    def sum_of(at):
        return own_ref[at, :].astype(F32) * own_by + partner_ref[at, :].astype(F32) * partner_by

    memory, totals8 = unpack(sum_of, sum_of)
    out_ref[:base, :] = memory.astype(BF)
    pack_totals(out_ref, totals8)


def combine(backward, length, starts, own, partner, after=()):
    return call(
        functools.partial(combine_body, backward, length),
        (),
        [SMEM, VM, VM],
        VM,
        shape(BF, PACK, 128),
        after=after,
    )(starts, own, partner)


def arrived(backward, length, starts_ref, partner_ref, far_ref, mem_ref, totals_ref):
    first = 2 * lax.axis_index("seq")
    is_first = (lax.axis_index("ffn") == 0).astype(F32)
    if backward:
        p = passes(starts_ref, first + 1, length)
        far_by, partner_by = is_first * p + (1 - is_first), is_first
        valid = lax.axis_index("seq") == 0
    else:
        p = passes(starts_ref, first, length)
        far_by, partner_by = is_first + (1 - is_first) * p, 1 - is_first
        valid = lax.axis_index("seq") == 1

    def sum_of(at):
        far = jnp.where(valid, far_ref[at, :].astype(F32), 0.0)
        return far * far_by + partner_ref[at, :].astype(F32) * partner_by

    memory, totals8 = unpack(sum_of, sum_of)
    mem_ref[...] = memory.astype(BF)
    totals_ref[...] = totals8.T


def head_of(own_side, h):
    ffn = lax.axis_index("ffn")
    return (ffn if own_side else 1 - ffn) * SIDE + h


def head_rows(head):
    return pl.ds(pl.multiple_of(head * HEAD, HEAD), HEAD)


def project_body(x_hbm, gain_hbm, bias_hbm, w_hbm, starts_ref,
                 heads_ref, control_ref, xnt_ref, pack_ref, mask_ref,
                 x_ref, gain_ref, bias_ref, w_ref, sems):
    length, width = x_ref.shape
    copies = [
        pltpu.make_async_copy(x_hbm, x_ref, sems.at[0]),
        pltpu.make_async_copy(gain_hbm, gain_ref, sems.at[1]),
        pltpu.make_async_copy(bias_hbm, bias_ref, sems.at[2]),
    ]
    columns = [
        pltpu.make_async_copy(w_hbm.at[:, pl.ds(j * width, width)], w_ref.at[j], sems.at[3 + j])
        for j in range(4)
    ]
    for copy in copies + columns:
        copy.start()
    mask_ref[...] = visible(doc_begin_row(starts_ref, length), length)
    for copy in copies:
        copy.wait()
    x = x_ref[...].astype(F32)
    mean = jnp.mean(x, axis=-1, keepdims=True)
    centered = x - mean
    inverse = lax.rsqrt(jnp.mean(centered * centered, axis=-1, keepdims=True) + EPSILON)
    xn = (centered * inverse * gain_ref[...] + bias_ref[...]).astype(BF)
    xnt_ref[...] = xn.T
    for j in range(3):
        columns[j].wait()
        t = nn(xn, w_ref[j]).astype(BF).T
        for h in range(HEADS):
            heads_ref[h, j * HEAD : j * HEAD + HEAD, :] = t[h * HEAD : h * HEAD + HEAD]
    columns[3].wait()
    control = jnp.exp(nn(xn, w_ref[3])).T
    control_ref[...] = control
    c = control.astype(BF)
    tail = tail_row(doc_begin_row(starts_ref, length), length)
    c_tail = c * tail.astype(BF)
    for h in range(HEADS):
        rows = slice(h * HEAD, h * HEAD + HEAD)
        heads_ref[h, 3 * HEAD :, :] = c[rows]
        mem_k = nt(c_tail[rows], heads_ref[h, HEAD : 2 * HEAD, :])
        mem_vt = nt(heads_ref[h, 2 * HEAD : 3 * HEAD, :], c_tail[rows])
        pack_ref[rows, :] = jnp.concatenate([mem_k, mem_vt], axis=1).astype(BF)
    tail8 = jnp.broadcast_to(tail, (8, length)).astype(BF)
    pack_totals(pack_ref, nt(tail8, c))


def project(x, gain, bias, w, starts):
    length, width = x.shape
    hbm = pl.BlockSpec(memory_space=pltpu.MemorySpace.HBM)
    return call(
        project_body,
        (),
        [hbm, hbm, hbm, hbm, SMEM],
        [VM] * 5,
        [
            shape(BF, HEADS, 4 * HEAD, length), shape(F32, width, length), shape(BF, width, length),
            shape(BF, PACK, 128), shape(BF, length, length),
        ],
        [
            pltpu.VMEM((length, width), BF), pltpu.VMEM((1, width), F32), pltpu.VMEM((1, width), F32),
            pltpu.VMEM((4, width, width), BF), pltpu.SemaphoreType.DMA((7,)),
        ],
        us=4.3,
        vmem=48,
    )(*(pltpu.with_memory_space_constraint(a, pltpu.HBM) for a in (x, gain, bias, w, starts)))


def parts(heads_ref, head):
    return [heads_ref[head, j * HEAD : j * HEAD + HEAD, :] for j in range(4)]


def mask_pair(mask_ref):
    half = mask_ref.shape[0] // 2
    return mask_ref[:half, :half], mask_ref[:, half:]


def causal_pairs(left, right, mask_ref):
    half = mask_ref.shape[0] // 2
    early, late = mask_pair(mask_ref)
    rows = left.T
    return nn(rows[:half], right[:, :half]).astype(BF) * early, nn(rows, right[:, half:]).astype(BF) * late


def causal_sum(left, pairs):
    a, b = pairs
    half = a.shape[0]
    return jnp.concatenate([nn(left[:, :half], a), nn(left, b)], axis=1)


def causal_back(pairs, right):
    a, b = pairs
    half = a.shape[0]
    late = nn(b, right[half:])
    return jnp.concatenate([late[:half] + nn(a, right[:half]), late[half:]], axis=0)


def padded(rows, second):
    zero = jnp.zeros_like(rows)
    return jnp.concatenate([zero, rows] if second else [rows, zero], axis=0).T


def pair_shapes(length, count=SIDE):
    half = length // 2
    return [shape(BF, count, half, half), shape(BF, count, length, half)]


def store_pairs(refs, i, pairs):
    refs[0][i], refs[1][i] = pairs


def load_pairs(refs, i):
    return refs[0][i], refs[1][i]


def local_body(own_side, heads_ref, mask_ref, number_ref, total_ref, *pair_refs):
    for i in range(SIDE):
        q, k, v, c = parts(heads_ref, head_of(own_side, i))
        pairs = causal_pairs(k, q, mask_ref)
        store_pairs(pair_refs, i, pairs)
        number_ref[i * HEAD : i * HEAD + HEAD, :] = causal_sum(c, pairs)
    c = jnp.concatenate([parts(heads_ref, head_of(own_side, i))[3] for i in range(SIDE)], axis=0)
    total_ref[...] = causal_sum(c, mask_pair(mask_ref))


def local_sums(own_side, heads, mask, after=()):
    length = heads.shape[2]
    return call(
        functools.partial(local_body, own_side),
        (),
        [VM, VM],
        [VM] * 4,
        [shape(F32, SIDE * HEAD, length)] * 2 + pair_shapes(length),
        us=3.0,
        after=after,
    )(heads, mask)


def enters_row(starts_ref, length):
    return jnp.where(doc_begin_row(starts_ref, length) < 0, 1.0, 0.0)


def mix_body(starts_ref, heads_ref, mask_ref, partner_ref, far_ref, *refs):
    refs = list(refs)
    take = lambda n: [refs.pop(0) for _ in range(n)]
    ins = [take(2), take(2)]
    mixed_ref, mem_ref = take(2)
    outs = [take(5), take(5)]
    (totals_ref,) = refs
    length = heads_ref.shape[2]
    arrived(False, length, starts_ref, partner_ref, far_ref, mem_ref, totals_ref)
    enters = enters_row(starts_ref, length)
    for own_side in (False, True):
        number_in, total_in = ins[own_side]
        number_ref, inverse_ref, weight_ref, *link_refs = outs[own_side]
        for i in range(SIDE):
            head, at = head_of(own_side, i), slice(i * HEAD, i * HEAD + HEAD)
            q, k, v, c = parts(heads_ref, head)
            mem = mem_ref[head_rows(head), :]
            mem_k, mem_vt = mem[:, :HEAD], mem[:, HEAD:]
            number = number_in[at, :] + enters * nn(mem_k, q)
            inverse = 1.0 / (total_in[at, :] + enters * totals_ref[head_rows(head), 0:1])
            score = number * (inverse * SCALE)
            e = jnp.exp(score - jnp.max(score, axis=0, keepdims=True))
            weight = e / jnp.sum(e, axis=0, keepdims=True)
            number_ref[at, :] = number
            inverse_ref[at, :] = inverse
            weight_ref[at, :] = weight
            spread = (weight * inverse).astype(BF)
            links = causal_pairs(c, spread, mask_ref)
            store_pairs(link_refs, i, links)
            mixed = causal_sum(v, links) + enters * nn(mem_vt, spread)
            mixed_ref[head_rows(head), :] = mixed.astype(BF)


def mix(starts, heads, mask, partner, far, local_other, local_own):
    length, width = heads.shape[2], HEADS * HEAD
    side = [shape(F32, SIDE * HEAD, length)] * 3 + pair_shapes(length)
    mixed, mem, *rest = call(
        mix_body,
        (),
        [SMEM] + [VM] * 8,
        [VM] * 12,
        [shape(BF, width, length), shape(BF, width, 128)] + side + side,
        [pltpu.VMEM((width, 8), F32)],
        us=4.0,
    )(starts, heads, mask, partner, far, *local_other, *local_own)
    return mixed, mem, rest[:5], rest[5:]


def feed_step(j, xn, cot, xnt, cott, up_ref, down_ref, gup_ref, gdown_ref):
    cols = slice(j * 512, j * 512 + 512)
    up, down = up_ref[:, cols], down_ref[:, cols]
    pre = nn(xn, up)
    v2 = pre * pre
    th = jnp.tanh(GELU_A * pre * (1.0 + GELU_B * v2))
    half = 0.5 * (1.0 + th)
    hidden = (pre * half).astype(BF)
    slope = half + 0.5 * pre * (1.0 - th * th) * (GELU_A * (1.0 + 3.0 * GELU_B * v2))
    grad_pre = (nn(cot, down) * slope).astype(BF)
    gdown_ref[:, cols] = nn(cott, hidden).astype(BF)
    gup_ref[:, cols] = nn(xnt, grad_pre).astype(BF)
    return nt(hidden, down), nt(grad_pre, up)


def feed_other_body(x_ref, mixed_ref, cot_ref, w_out_ref, gain_ref, bias_ref, up_ref, down_ref,
                    gup_ref, gdown_ref, hidden1_ref, n_ref, inv_ref, xn_ref, xnt_ref, cott_ref,
                    part_ref, d_ref):
    hidden1 = x_ref[...].astype(F32) + tn(mixed_ref[...], w_out_ref[...])
    hidden1_ref[...] = hidden1
    mean = jnp.mean(hidden1, axis=-1, keepdims=True)
    centered = hidden1 - mean
    inverse = lax.rsqrt(jnp.mean(centered * centered, axis=-1, keepdims=True) + EPSILON)
    n = centered * inverse
    n_ref[...] = n
    inv_ref[...] = jnp.broadcast_to(inverse, inv_ref.shape)
    xn_ref[...] = (n * gain_ref[...] + bias_ref[...]).astype(BF)
    xnt_ref[...] = xn_ref[...].T
    cott_ref[...] = cot_ref[...].T
    for j in range(up_ref.shape[1] // 512):
        part, d = feed_step(j, xn_ref[...], cot_ref[...], xnt_ref[...], cott_ref[...],
                            up_ref, down_ref, gup_ref, gdown_ref)
        part_ref[...] = part if j == 0 else part_ref[...] + part
        d_ref[...] = d if j == 0 else d_ref[...] + d


def feed_own_body(hidden1_ref, n_ref, inv_ref, xn_ref, xnt_ref, cott_ref, part_ref, d_in_ref,
                  mixed_ref, cot_ref, w_out_ref, gain_ref, up_ref, down_ref,
                  output_ref, d_hidden1_ref, g_ref, out_send_ref, out_keep_ref, norms_ref,
                  gup_ref, gdown_ref, sum_ref, d_ref):
    for j in range(up_ref.shape[1] // 512):
        part, d = feed_step(j, xn_ref[...], cot_ref[...], xnt_ref[...], cott_ref[...],
                            up_ref, down_ref, gup_ref, gdown_ref)
        sum_ref[...] = (part_ref[...] if j == 0 else sum_ref[...]) + part
        d_ref[...] = (d_in_ref[...] if j == 0 else d_ref[...]) + d
    output_ref[...] = (hidden1_ref[...] + sum_ref[...]).astype(BF)
    dx, n = d_ref[...], n_ref[...]
    norms_ref[...] = jnp.concatenate(
        [jnp.sum(dx * n, axis=0, keepdims=True), jnp.sum(dx, axis=0, keepdims=True)] * 4, axis=0
    )
    d_n = dx * gain_ref[...]
    d_in = (
        d_n
        - jnp.mean(d_n, axis=-1, keepdims=True)
        - n * jnp.mean(d_n * n, axis=-1, keepdims=True)
    ) * inv_ref[:, 0:1]
    d_hidden1 = cot_ref[...].astype(F32) + d_in
    d_hidden1_ref[...] = d_hidden1
    d_branch = d_hidden1.astype(BF)
    g_ref[...] = nt(w_out_ref[...], d_branch).astype(BF)
    grad_out = nn(mixed_ref[...], d_branch).astype(BF)
    half = grad_out.shape[1] // 2
    second = lax.axis_index("ffn") == 1
    out_keep_ref[...] = jnp.where(second, grad_out[:, half:], grad_out[:, :half])
    out_send_ref[...] = jnp.where(second, grad_out[:, :half], grad_out[:, half:])


def feed_other(x, mixed, cotangent, w_out, gain, bias, up, down):
    length, width = x.shape
    half, sq = shape(BF, *up.shape), lambda dt: shape(dt, length, width)
    return call(
        feed_other_body,
        (),
        [VM] * 8,
        [VM] * 10,
        [half, half, sq(F32), sq(F32), shape(F32, length, 128),
         sq(BF), sq(BF), sq(BF), sq(F32), sq(F32)],
        us=6.0,
    )(x, mixed, cotangent, w_out, gain, bias, up, down)


def feed_own(saved, mixed, cotangent, w_out, gain, up, down, after=()):
    length, width = mixed.shape
    half, sq = shape(BF, *up.shape), lambda dt: shape(dt, length, width)
    return call(
        feed_own_body,
        (),
        [VM] * 14,
        [VM] * 8,
        [sq(BF), sq(F32), sq(BF)] + [shape(BF, width, width // 2)] * 2 + [shape(F32, 8, width), half, half],
        [pltpu.VMEM((length, width), F32)] * 2,
        us=6.0,
        after=after,
    )(*saved, mixed, cotangent, w_out, gain, up, down)


def scores_back_body(own_side, starts_ref, heads_ref, mask_ref, g_ref, mem_ref, number_ref, inverse_ref, weight_ref,
                     *refs):
    if own_side:
        pack_in, sums_in, a_ref, spread_ref, d_total_ref, early_ref, late_ref, pack_ref, sums_ref = refs
        pack_ref[...] = pack_in[...]
        sums_ref[...] = sums_in[...]
    else:
        a_ref, spread_ref, d_total_ref, early_ref, late_ref, pack_ref, sums_ref = refs
    length = heads_ref.shape[2]
    enters = enters_row(starts_ref, length)
    for i in range(SIDE):
        head, at = head_of(own_side, i), slice(i * HEAD, i * HEAD + HEAD)
        rows = head_rows(head)
        q, k, v, c = parts(heads_ref, head)
        g = g_ref[rows, :]
        mem_vt = mem_ref[rows, :][:, HEAD:]
        number, inverse, weight = number_ref[at, :], inverse_ref[at, :], weight_ref[at, :]
        values = causal_pairs(v, g, mask_ref)
        store_pairs((early_ref, late_ref), i, values)
        number_v = causal_sum(c, values) + enters * tn(mem_vt, g)
        d_weight = number_v * inverse
        d_score = weight * (d_weight - jnp.sum(weight * d_weight, axis=0, keepdims=True))
        a = d_score * (inverse * SCALE)
        spread = weight * inverse
        d_total = -(a * number + spread * number_v) * inverse
        a_ref[at, :] = a.astype(BF)
        spread_ref[at, :] = spread.astype(BF)
        d_total_ref[at, :] = d_total.astype(BF)
        d_k = nt((a * enters).astype(BF), q)
        d_vt = nt(g, (spread * enters).astype(BF))
        pack_ref[rows, :] = jnp.concatenate([d_k, d_vt], axis=1).astype(BF)
        sums_ref[rows, :] = jnp.broadcast_to(jnp.sum(d_total * enters, axis=1, keepdims=True), (HEAD, 128))
    if own_side:
        pack_totals(pack_ref, sums_ref[...].T[0:8])


def scores_back(own_side, starts, heads, mask, g, mem, saved, packs=(), after=()):
    length, width = heads.shape[2], HEADS * HEAD
    sums = [] if own_side else [shape(F32, width, 128)]
    outs = [shape(BF, SIDE * HEAD, length)] * 3 + pair_shapes(length) + [shape(BF, PACK, 128)] + sums
    return call(
        functools.partial(scores_back_body, own_side),
        (),
        [SMEM] + [VM] * (7 + len(packs)),
        [VM] * len(outs),
        outs,
        [pltpu.VMEM((width, 128), F32)] if own_side else [],
        us=3.0,
        after=after,
    )(starts, heads, mask, g, mem, *saved[:3], *packs)


def heads_back_body(own_side, starts_ref, heads_ref, mask_ref, g_ref, mem_ref, a_ref, spread_ref, d_total_ref,
                    v_early, v_late, l_early, l_late, p_early, p_late, d_ref):
    length = heads_ref.shape[2]
    enters = enters_row(starts_ref, length)
    from_totals = causal_back(mask_pair(mask_ref), d_total_ref[...].T).T
    held = None
    for i in range(SIDE):
        head, at = head_of(own_side, i), slice(i * HEAD, i * HEAD + HEAD)
        rows = head_rows(head)
        q, k, v, c = parts(heads_ref, head)
        g, a, spread = g_ref[rows, :], a_ref[at, :], spread_ref[at, :]
        mem_k = mem_ref[rows, :][:, :HEAD]
        steps = causal_pairs(c, a, mask_ref)
        d_ref[i, :HEAD, :] = causal_sum(k, steps) + enters * tn(mem_k, a)
        d_ref[i, HEAD : 3 * HEAD, :] = (
            causal_back(steps, padded(q, False)) + causal_back(load_pairs((l_early, l_late), i), padded(g, True))
        ).T
        odd = i % 2 == 1
        d_control = causal_back(load_pairs((p_early, p_late), i), padded(a, odd)) + causal_back(
            load_pairs((v_early, v_late), i), padded(spread, odd)
        )
        if odd:
            two = (held + d_control).T
            for n in range(2):
                total_rows = slice((i - 1 + n) * HEAD, (i + n) * HEAD)
                d_ref[i - 1 + n, 3 * HEAD :, :] = two[n * HEAD : n * HEAD + HEAD] + from_totals[total_rows]
        held = d_control


def heads_back(own_side, starts, heads, mask, g, mem, scores, links, pairs, after=()):
    length = heads.shape[2]
    return call(
        functools.partial(heads_back_body, own_side),
        (),
        [SMEM] + [VM] * 13,
        VM,
        shape(F32, SIDE, 4 * HEAD, length),
        us=8.0 if own_side else 3.0,
        after=after,
    )(starts, heads, mask, g, mem, *scores, *links, *pairs)


def project_back_body(own_side, starts_ref, heads_ref, d_ref, control_ref, partner_ref, far_ref, xnt_ref, w_ref, *refs):
    if own_side:
        (dx_in_ref, x_ref, gain_ref, d_hidden1_ref, norms2_ref,
         grad_ref, grad_x_ref, norms_ref, mem_ref, totals_ref, proj_ref) = refs
    else:
        grad_ref, dx_ref, mem_ref, totals_ref, proj_ref = refs
    length, width = xnt_ref.shape[1], xnt_ref.shape[0]
    arrived(True, length, starts_ref, partner_ref, far_ref, mem_ref, totals_ref)
    tail = tail_row(doc_begin_row(starts_ref, length), length)
    tail_bf = tail.astype(BF)
    dx = None
    for p in range(SIDE // 2):
        for i in range(2):
            n = 2 * p + i
            head = head_of(own_side, n)
            rows = head_rows(head)
            mem = mem_ref[rows, :]
            back_k, back_vt = mem[:, :HEAD], mem[:, HEAD:]
            q, k, v, c = parts(heads_ref, head)
            c_tail = c * tail_bf
            d_q = d_ref[n, :HEAD, :]
            d_k = d_ref[n, HEAD : 2 * HEAD, :] + tn(back_k, c_tail)
            d_v = d_ref[n, 2 * HEAD : 3 * HEAD, :] + nn(back_vt, c_tail)
            d_c = d_ref[n, 3 * HEAD :, :] + tail * (
                nn(back_k, k) + tn(back_vt, v) + totals_ref[rows, 0:1]
            )
            d_c = d_c * control_ref[rows, :]
            for m, value in enumerate((d_q, d_k, d_v, d_c)):
                proj_ref[p, m * 128 + i * HEAD : m * 128 + i * HEAD + HEAD, :] = value.astype(BF)
        d_proj = proj_ref[p]
        grad_ref[:, p * 512 : p * 512 + 512] = nt(xnt_ref[...], d_proj).astype(BF)
        first = head_of(own_side, 2 * p) * HEAD
        w = jnp.concatenate(
            [w_ref[:, pl.ds(pl.multiple_of(m * width + first, 128), 128)] for m in range(4)], axis=1
        )
        dx = nn(w, d_proj) if dx is None else dx + nn(w, d_proj)
    if not own_side:
        dx_ref[...] = dx
        return
    x = x_ref[...].astype(F32)
    mean = jnp.mean(x, axis=-1, keepdims=True)
    centered = x - mean
    inverse = lax.rsqrt(jnp.mean(centered * centered, axis=-1, keepdims=True) + EPSILON)
    n = centered * inverse
    d = (dx_in_ref[...] + dx).T
    sums = [jnp.sum(d * n, axis=0, keepdims=True), jnp.sum(d, axis=0, keepdims=True)]
    rows8 = jnp.concatenate(sums + [norms2_ref[0:6, :]], axis=0)
    norms_ref[...] = jnp.concatenate([rows8, jnp.zeros((120, length), F32)], axis=0).T.astype(BF)
    d_n = d * gain_ref[...]
    grad_x_ref[...] = d_hidden1_ref[...] + (
        d_n
        - jnp.mean(d_n, axis=-1, keepdims=True)
        - n * jnp.mean(d_n * n, axis=-1, keepdims=True)
    ) * inverse


def project_back(own_side, starts, heads, d, control, partner, far, xnt, w, rest=(), after=()):
    width, length = xnt.shape
    outs = [shape(BF, width, 1024), shape(F32, length, width)]
    if own_side:
        outs.append(shape(BF, width, 128))
    return call(
        functools.partial(project_back_body, own_side),
        (),
        [SMEM] + [VM] * (7 + len(rest)),
        [VM] * len(outs),
        outs,
        [pltpu.VMEM((width, 128), BF), pltpu.VMEM((width, 8), F32), pltpu.VMEM((SIDE // 2, 512, length), BF)],
        us=5.0 if own_side else 3.5,
        after=after,
    )(starts, heads, d, control, partner, far, xnt, w, *rest)


def bit_axis(bit):
    return ("seq", 1) if bit == 0 else ("dp", 1 << (bit - 1))


def my_bit(bit):
    axis, step = bit_axis(bit)
    return (lax.axis_index(axis) // step) % 2


def send_across(a, bits):
    seqs, dps = lax.axis_size("seq"), lax.axis_size("dp")
    flip = sum(1 << bit for bit in bits)
    return lax.ppermute(a, ("dp", "seq"), [(i, i ^ flip) for i in range(seqs * dps)])


def place_of(t, places, values):
    index, rest, bit = 0, t, 0
    fixed = dict(zip(places, values))
    while rest or fixed:
        if bit in fixed:
            index = index + fixed.pop(bit) * (1 << bit)
        else:
            index = index + ((rest & 1) << bit)
            rest >>= 1
        bit += 1
    return index


def stage_body(plan, *refs):
    refs = list(refs)
    ins = [[[refs.pop(0) for _ in pieces] for pieces in arrays] for arrays, _, _ in plan]
    for (arrays, split, dtype), sources in zip(plan, ins):
        outs = [refs.pop(0) for _ in range(1 << len(split))]
        blocks = outs[0].shape[0]
        places = [place for _, place in split]
        mine = [my_bit(bit) for bit, _ in split]
        for pattern, out in enumerate(outs):
            values = [
                (1 - m) if (pattern >> n) & 1 else m for n, m in enumerate(mine)
            ]
            for t in range(blocks):
                at = place_of(t, places, values)
                total = None
                for pieces in sources:
                    row = jnp.concatenate([p[at] for p in pieces], axis=1) if len(pieces) > 1 else pieces[0][at]
                    row = row.astype(F32)
                    total = row if total is None else total + row
                out[t] = total.astype(out.dtype)


def stage(groups, after=(), dtype=BF):
    plan, operands, in_specs, out_specs, out_shape = [], [], [], [], []
    rows = groups[0][0][0][0][0].shape[1]
    steps = 2 if rows % 32 == 0 else 1
    for arrays, split in groups:
        for pieces in arrays:
            for array, first, count in pieces:
                operands.append(array)
                in_specs.append(
                    pl.BlockSpec((array.shape[0], rows // steps, count),
                                 functools.partial(lambda at, i: (0, i, at), first // count))
                )
        blocks, width = arrays[0][0][0].shape[0] >> len(split), sum(p[2] for p in arrays[0])
        plan.append(([[None] * len(pieces) for pieces in arrays], split, dtype))
        for _ in range(1 << len(split)):
            out_specs.append(pl.BlockSpec((blocks, rows // steps, width), lambda i: (0, i, 0)))
            out_shape.append(jax.ShapeDtypeStruct((blocks, rows, width), dtype))
    outs = list(
        call(functools.partial(stage_body, plan), (steps,), in_specs, out_specs, out_shape, after=after)(*operands)
    )
    result = []
    for _, split in groups:
        result.append([outs.pop(0) for _ in range(1 << len(split))])
    return result


def all_of(a):
    return [(a, 0, a.shape[2])]


def patterns(bits):
    return [[b for n, b in enumerate(bits) if (p >> n) & 1] for p in range(1, 1 << len(bits))]


def finish_body(a_ref, b_ref, up_ref, down_ref, out_ref):
    total = a_ref[0].astype(F32) + b_ref[0].astype(F32)
    half, part = up_ref.shape[1], out_ref.shape[1] // 2
    up_ref[...] = total[:, :half]
    down_ref[...] = total[:, half + part : 2 * half + part]
    out_ref[:, :part] = total[:, half : half + part].astype(BF)
    out_ref[:, part:] = total[:, 2 * half + part :].astype(BF)


def finish(a, b, half, part, after=()):
    rows = a.shape[1]
    return call(
        finish_body,
        (),
        [VM] * 2,
        [VM] * 3,
        [jax.ShapeDtypeStruct((rows, half), F32)] * 2 + [jax.ShapeDtypeStruct((rows, 2 * part), BF)],
        after=after,
    )(a, b)


def join_body(own_ref, other_ref, out_own, out_other, grad_in_ref, grad_out_ref, *norm_refs):
    second = lax.axis_index("ffn") == 1
    own, other = own_ref[0].astype(F32), other_ref[0].astype(F32)
    for f in range(2):
        keep_own = second if f else jnp.logical_not(second)
        half = jnp.where(keep_own, own[:, :1024], other[:, :1024])
        for p in range(2):
            for m in range(4):
                grad_in_ref[:, m * 512 + f * 256 + p * 128 : m * 512 + f * 256 + p * 128 + 128] = (
                    half[:, p * 512 + m * 128 : p * 512 + m * 128 + 128]
                )
        grad_out_ref[:, f * 256 : f * 256 + 256] = jnp.where(
            keep_own, out_own[...], out_other[...]
        ).astype(F32)
    norms = (own[:, 1024:] + other[:, 1024:]).T
    for n, ref in enumerate(norm_refs):
        ref[...] = norms[n]


def join(own, other, out_own, out_other):
    rows = own.shape[1]
    return call(
        join_body,
        (),
        [VM] * 4,
        [VM] * 6,
        [jax.ShapeDtypeStruct((rows, n), F32) for n in (2048, 512)] + [jax.ShapeDtypeStruct((rows,), F32)] * 4,
    )(own, other, out_own, out_other)


def on_device(tokens, doc_starts, norm1_gain, norm1_bias, in_weight, out_weight,
              norm2_gain, norm2_bias, up_own, down_own, output_cotangent):
    up_other, down_other = swap(up_own, "ffn", 1), swap(down_own, "ffn", 1)
    x, cotangent, starts = tokens[0], output_cotangent[0], doc_starts
    length, width = x.shape
    owners = lax.axis_size("dp") * lax.axis_size("seq")
    bits = owners.bit_length() - 1
    row = lambda a: a.reshape(1, width)
    blocked = lambda a: a.reshape(owners, width // owners, a.shape[1])

    heads, control, xnt, own, mask = project(x, row(norm1_gain), row(norm1_bias), in_weight, starts)
    partner = swap(own, "ffn", 1)
    number_o, total_o, *pairs_other = local_sums(False, heads, mask)
    both = combine(False, length, starts, own, partner, after=[number_o])
    far = swap(both, "seq", 1)
    number, total, *pairs_own = local_sums(True, heads, mask, after=[both])
    mixed, memory, saved_other, saved_own = mix(
        starts, heads, mask, partner, far, (number_o, total_o), (number, total))
    gup_send, gdown_send, *saved = feed_other(
        x, mixed, cotangent, out_weight, row(norm2_gain), row(norm2_bias), up_other, down_other)
    gup_got, gdown_got = swap(gup_send, "ffn", 1), swap(gdown_send, "ffn", 1)
    (output, d_hidden1, g, out_send, out_keep, norms2, gup_own, gdown_own) = feed_own(
        saved, mixed, cotangent, out_weight, row(norm2_gain), up_own, down_own)
    out_got = swap(out_send, "ffn", 1)

    out_half = width // 4
    ups, downs, outs = [
        [blocked(a) for a in pair]
        for pair in ((gup_own, gup_got), (gdown_own, gdown_got), (out_keep, out_got))
    ]
    groups = [
        [[*all_of(a), (o, 0, out_half)] for a, o in zip(ups, outs)],
        [[*all_of(a), (o, out_half, out_half)] for a, o in zip(downs, outs)],
    ]
    orders = [[1, 2], [2, 1]]
    left = [list(range(bits)) for _ in groups]

    def advance(groups, n, after):
        if n >= 2:
            if n == 2:
                groups = [[pieces_a + pieces_b for pieces_a, pieces_b in zip(*groups)]]
            bits_now = left[0][:1]
            splits = [[(bits_now[0], 0)]]
            for rest in left:
                rest.pop(0)
        else:
            bits_now = [order[n] for order in orders]
            splits = [[(bit, rest.index(bit))] for bit, rest in zip(bits_now, left)]
            for bit, rest in zip(bits_now, left):
                rest.remove(bit)
        outs = stage(list(zip(groups, splits)), after=after)
        got = [send_across(sent, [bit]) for (_, sent), bit in zip(outs, bits_now)]
        sent = [s for _, s in outs]
        return [[all_of(kept), all_of(r)] for (kept, _), r in zip(outs, got)], sent

    back = (starts, heads, mask, g, memory)
    *scores_other, pack, sums = scores_back(False, *back, saved_other)
    groups, sent = advance(groups, 0, [pack])
    *scores_own, d_own = scores_back(True, *back, saved_own, packs=(pack, sums), after=sent)
    d_partner = swap(d_own, "ffn", 1)
    d_both = combine(True, length, starts, d_own, d_partner)
    d_far = swap(d_both, "seq", 1)
    side = (control, d_partner, d_far, xnt, in_weight)
    d_other = heads_back(False, *back, scores_other, saved_other[3:], pairs_other, after=[d_both])
    groups, sent = advance(groups, 1, [d_other])
    in_send, dx = project_back(False, starts, heads, d_other, *side, after=sent)
    in_got = swap(in_send, "ffn", 1)
    d_mine = heads_back(True, *back, scores_own, saved_own[3:], pairs_own, after=[in_send])
    groups, sent = advance(groups, 2, [d_mine])
    in_keep, grad_tokens, norms = project_back(
        True, starts, heads, d_mine, *side,
        rest=(dx, x, row(norm1_gain), d_hidden1, norms2), after=sent)

    late = [
        all_of(blocked(in_keep)) + all_of(blocked(norms)),
        all_of(blocked(in_got)) + all_of(jnp.zeros_like(blocked(norms))),
    ]
    rest = list(range(bits))
    first = True
    while rest:
        now = rest[:2]
        split = [(b, rest.index(b)) for b in now]
        rest = rest[2:]
        (kept, *sent), = stage([(late, split)])
        late = [all_of(kept)] + [all_of(send_across(s, p)) for s, p in zip(sent, patterns(now))]
        if first:
            first, token = False, [kept]
            for n in range(3, bits):
                groups, token = advance(groups, n, token)
    grad_up, grad_down, out = finish(*(a[0][0] for a in groups[0]), gup_own.shape[1], out_half, after=[kept])
    (final,), = stage([(late, [])], after=[out])
    grad_in, grad_out, *norms = join(final, swap(final, "ffn", 1), out, swap(out, "ffn", 1))
    return (output[None], grad_tokens[None], grad_in, grad_out, grad_up, grad_down, *norms)


def solution(mesh):
    rows = P("dp", ("seq", "ffn"), None)
    owned = P(("dp", "seq"))
    return jax.shard_map(
        on_device,
        mesh=mesh,
        in_specs=(
            rows, P("dp", None), P(), P(), P(), P(), P(), P(),
            P(None, "ffn"), P(None, "ffn"), rows,
        ),
        out_specs=(
            rows, rows, P(("dp", "seq"), None), P(("dp", "seq"), None),
            P(("dp", "seq"), "ffn"), P(("dp", "seq"), "ffn"),
            owned, owned, owned, owned,
        ),
        check_vma=False,
    )
```

```python
import functools

import jax
import jax.numpy as jnp
from jax import lax
from jax.experimental import pallas as pl
from jax.experimental.pallas import tpu as pltpu
from jax.sharding import PartitionSpec as P

HEADS = 8
HEAD = 64
EPSILON = 1e-05
BF = jnp.bfloat16
F32 = jnp.float32
GELU_A = 0.7978845608028654
GELU_B = 0.044715
SCALE = HEAD**-0.5
SIDE = HEADS // 2
PACK = HEADS * HEAD + 64


def nn(a, b):
    return lax.dot_general(a, b, (((1,), (0,)), ((), ())), preferred_element_type=F32)


def nt(a, b):
    return lax.dot_general(a, b, (((1,), (1,)), ((), ())), preferred_element_type=F32)


def tn(a, b):
    return lax.dot_general(a, b, (((0,), (0,)), ((), ())), preferred_element_type=F32)


def swap(a, axis, bit):
    size = lax.axis_size(axis)
    return lax.ppermute(a, axis, [(i, i ^ bit) for i in range(size)])


ANY = pl.BlockSpec(memory_space=pl.ANY)


def call(body, grid, in_specs, out_specs, out_shape, scratch=(), us=1.0, after=(), vmem=20):
    count = len(in_specs)

    def run(*refs):
        body(*refs[:count], *refs[count + len(after) :])

    def start(*operands):
        return pl.pallas_call(
            run,
            grid=grid,
            in_specs=list(in_specs) + [ANY] * len(after),
            out_specs=out_specs,
            out_shape=out_shape,
            scratch_shapes=list(scratch),
            cost_estimate=pl.CostEstimate(flops=int(us * 1e7), bytes_accessed=2**13, transcendentals=0),
            compiler_params=pltpu.CompilerParams(vmem_limit_bytes=vmem * 2**20),
        )(*operands, *after)

    return start


def whole(shape):
    return pl.BlockSpec(shape, lambda *_: (0,) * len(shape))


VM = pl.BlockSpec(memory_space=pltpu.MemorySpace.VMEM)


def shape(dtype, *dims):
    return jax.ShapeDtypeStruct(dims, dtype)


SMEM = pl.BlockSpec(memory_space=pltpu.SMEM)


def shard_of():
    return lax.axis_index("seq") * 2 + lax.axis_index("ffn")


def doc_begin_row(starts_ref, length):
    begin = shard_of() * length
    place = lax.broadcasted_iota(jnp.int32, (1, length), 1)
    row = jnp.full((1, length), -(2**30), jnp.int32)
    for j in range(starts_ref.shape[1]):
        s = starts_ref[0, j] - begin
        row = jnp.where(place >= s, jnp.maximum(row, s), row)
    return row


def passes(starts_ref, which, length):
    hit = jnp.int32(0)
    for j in range(starts_ref.shape[1]):
        s = starts_ref[0, j]
        hit = hit | ((s >= which * length) & (s < which * length + length)).astype(jnp.int32)
    return 1.0 - hit.astype(F32)


def visible(doc_row, length):
    i = lax.broadcasted_iota(jnp.int32, (length, length), 0)
    t = lax.broadcasted_iota(jnp.int32, (length, length), 1)
    return jnp.where((i <= t) & (i >= doc_row), 1.0, 0.0).astype(BF)


def tail_row(doc_row, length):
    place = lax.broadcasted_iota(jnp.int32, (1, length), 1)
    last = doc_row[:, length - 1 :]
    return jnp.where(place >= last, 1.0, 0.0)


def pack_totals(pack_ref, totals8):
    base = HEADS * HEAD
    hi = totals8.astype(BF)
    lo = (totals8 - hi.astype(F32)).astype(BF)
    for a in range(4):
        cols = slice(128 * a, 128 * a + 128)
        pack_ref[base + 16 * a : base + 16 * a + 16, :] = jnp.concatenate(
            [hi[:, cols], lo[:, cols]], axis=0
        )


def unpack(rows, totals8_of):
    base = HEADS * HEAD
    out = []
    for a in range(4):
        block = totals8_of(slice(base + 16 * a, base + 16 * a + 16))
        out.append(block[:8] + block[8:])
    return rows(slice(0, base)), jnp.concatenate(out, axis=1)


def combine_body(backward, length, starts_ref, own_ref, partner_ref, out_ref):
    first = 2 * lax.axis_index("seq")
    is_first = (lax.axis_index("ffn") == 0).astype(F32)
    base = HEADS * HEAD
    if backward:
        p = passes(starts_ref, first, length)
        own_by, partner_by = is_first + (1 - is_first) * p, is_first * p + (1 - is_first)
    else:
        p = passes(starts_ref, first + 1, length)
        own_by, partner_by = is_first * p + (1 - is_first), is_first + (1 - is_first) * p

    def sum_of(at):
        return own_ref[at, :].astype(F32) * own_by + partner_ref[at, :].astype(F32) * partner_by

    memory, totals8 = unpack(sum_of, sum_of)
    out_ref[:base, :] = memory.astype(BF)
    pack_totals(out_ref, totals8)


def combine(backward, length, starts, own, partner, after=()):
    return call(
        functools.partial(combine_body, backward, length),
        (),
        [SMEM, VM, VM],
        VM,
        shape(BF, PACK, 128),
        after=after,
    )(starts, own, partner)


def arrived(backward, length, starts_ref, partner_ref, far_ref, mem_ref, totals_ref):
    first = 2 * lax.axis_index("seq")
    is_first = (lax.axis_index("ffn") == 0).astype(F32)
    if backward:
        p = passes(starts_ref, first + 1, length)
        far_by, partner_by = is_first * p + (1 - is_first), is_first
        valid = lax.axis_index("seq") == 0
    else:
        p = passes(starts_ref, first, length)
        far_by, partner_by = is_first + (1 - is_first) * p, 1 - is_first
        valid = lax.axis_index("seq") == 1

    def sum_of(at):
        far = jnp.where(valid, far_ref[at, :].astype(F32), 0.0)
        return far * far_by + partner_ref[at, :].astype(F32) * partner_by

    memory, totals8 = unpack(sum_of, sum_of)
    mem_ref[...] = memory.astype(BF)
    totals_ref[...] = totals8.T


def head_of(own_side, h):
    ffn = lax.axis_index("ffn")
    return (ffn if own_side else 1 - ffn) * SIDE + h


def head_rows(head):
    return pl.ds(pl.multiple_of(head * HEAD, HEAD), HEAD)


def project_body(x_hbm, gain_hbm, bias_hbm, w_hbm, starts_ref,
                 heads_ref, control_ref, xnt_ref, pack_ref, mask_ref,
                 x_ref, gain_ref, bias_ref, w_ref, sems):
    length, width = x_ref.shape
    copies = [
        pltpu.make_async_copy(x_hbm, x_ref, sems.at[0]),
        pltpu.make_async_copy(gain_hbm, gain_ref, sems.at[1]),
        pltpu.make_async_copy(bias_hbm, bias_ref, sems.at[2]),
    ]
    columns = [
        pltpu.make_async_copy(w_hbm.at[:, pl.ds(j * width, width)], w_ref.at[j], sems.at[3 + j])
        for j in range(4)
    ]
    for copy in copies + columns:
        copy.start()
    mask_ref[...] = visible(doc_begin_row(starts_ref, length), length)
    for copy in copies:
        copy.wait()
    x = x_ref[...].astype(F32)
    mean = jnp.mean(x, axis=-1, keepdims=True)
    centered = x - mean
    inverse = lax.rsqrt(jnp.mean(centered * centered, axis=-1, keepdims=True) + EPSILON)
    xn = (centered * inverse * gain_ref[...] + bias_ref[...]).astype(BF)
    xnt_ref[...] = xn.T
    projected = []
    for j in range(4):
        columns[j].wait()
        projected.append(nn(xn, w_ref[j]))
    control = jnp.exp(projected[3]).T
    control_ref[...] = control
    c = control.astype(BF)
    for j in range(3):
        t = projected[j].astype(BF).T
        for h in range(HEADS):
            heads_ref[h, j * HEAD : j * HEAD + HEAD, :] = t[h * HEAD : h * HEAD + HEAD]
    tail = tail_row(doc_begin_row(starts_ref, length), length)
    c_tail = c * tail.astype(BF)
    for h in range(HEADS):
        rows = slice(h * HEAD, h * HEAD + HEAD)
        heads_ref[h, 3 * HEAD :, :] = c[rows]
        mem_k = nt(c_tail[rows], heads_ref[h, HEAD : 2 * HEAD, :])
        mem_vt = nt(heads_ref[h, 2 * HEAD : 3 * HEAD, :], c_tail[rows])
        pack_ref[rows, :] = jnp.concatenate([mem_k, mem_vt], axis=1).astype(BF)
    tail8 = jnp.broadcast_to(tail, (8, length)).astype(BF)
    pack_totals(pack_ref, nt(tail8, c))


def project(x, gain, bias, w, starts):
    length, width = x.shape
    hbm = pl.BlockSpec(memory_space=pltpu.MemorySpace.HBM)
    return call(
        project_body,
        (),
        [hbm, hbm, hbm, hbm, SMEM],
        [VM] * 5,
        [
            shape(BF, HEADS, 4 * HEAD, length), shape(F32, width, length), shape(BF, width, length),
            shape(BF, PACK, 128), shape(BF, length, length),
        ],
        [
            pltpu.VMEM((length, width), BF), pltpu.VMEM((1, width), F32), pltpu.VMEM((1, width), F32),
            pltpu.VMEM((4, width, width), BF), pltpu.SemaphoreType.DMA((7,)),
        ],
        us=4.3,
        vmem=48,
    )(*(pltpu.with_memory_space_constraint(a, pltpu.HBM) for a in (x, gain, bias, w, starts)))


def parts(heads_ref, head):
    return [heads_ref[head, j * HEAD : j * HEAD + HEAD, :] for j in range(4)]


def mask_pair(mask_ref):
    half = mask_ref.shape[0] // 2
    return mask_ref[:half, :half], mask_ref[:, half:]


def causal_pairs(left, right, mask_ref):
    half = mask_ref.shape[0] // 2
    early, late = mask_pair(mask_ref)
    rows = left.T
    return nn(rows[:half], right[:, :half]).astype(BF) * early, nn(rows, right[:, half:]).astype(BF) * late


def causal_sum(left, pairs):
    a, b = pairs
    half = a.shape[0]
    return jnp.concatenate([nn(left[:, :half], a), nn(left, b)], axis=1)


def causal_back(pairs, right):
    a, b = pairs
    half = a.shape[0]
    late = nn(b, right[half:])
    return jnp.concatenate([late[:half] + nn(a, right[:half]), late[half:]], axis=0)


def padded(rows, second):
    zero = jnp.zeros_like(rows)
    return jnp.concatenate([zero, rows] if second else [rows, zero], axis=0).T


def pair_shapes(length, count=SIDE):
    half = length // 2
    return [shape(BF, count, half, half), shape(BF, count, length, half)]


def store_pairs(refs, i, pairs):
    refs[0][i], refs[1][i] = pairs


def load_pairs(refs, i):
    return refs[0][i], refs[1][i]


def local_body(own_side, heads_ref, mask_ref, number_ref, total_ref, *pair_refs):
    held = [parts(heads_ref, head_of(own_side, i)) for i in range(SIDE)]
    pairs = [causal_pairs(k, q, mask_ref) for q, k, v, c in held]
    for i in range(SIDE):
        store_pairs(pair_refs, i, pairs[i])
    c = jnp.concatenate([h[3] for h in held], axis=0)
    total_ref[...] = causal_sum(c, mask_pair(mask_ref))
    for i in range(SIDE):
        number_ref[i * HEAD : i * HEAD + HEAD, :] = causal_sum(held[i][3], pairs[i])


def local_sums(own_side, heads, mask, after=()):
    length = heads.shape[2]
    return call(
        functools.partial(local_body, own_side),
        (),
        [VM, VM],
        [VM] * 4,
        [shape(F32, SIDE * HEAD, length)] * 2 + pair_shapes(length),
        us=3.0,
        after=after,
    )(heads, mask)


def enters_row(starts_ref, length):
    return jnp.where(doc_begin_row(starts_ref, length) < 0, 1.0, 0.0)


def mix_body(starts_ref, heads_ref, mask_ref, partner_ref, far_ref, *refs):
    refs = list(refs)
    take = lambda n: [refs.pop(0) for _ in range(n)]
    ins = [take(2), take(2)]
    mixed_ref, mem_ref = take(2)
    outs = [take(5), take(5)]
    (totals_ref,) = refs
    length = heads_ref.shape[2]
    arrived(False, length, starts_ref, partner_ref, far_ref, mem_ref, totals_ref)
    enters = enters_row(starts_ref, length)
    jobs = [(own_side, i) for own_side in (False, True) for i in range(SIDE)]
    spreads, links = [], []
    for own_side, i in jobs:
        number_in, total_in = ins[own_side]
        number_ref, inverse_ref, weight_ref, *_ = outs[own_side]
        head, at = head_of(own_side, i), slice(i * HEAD, i * HEAD + HEAD)
        mem_k = mem_ref[head_rows(head), :][:, :HEAD]
        number = number_in[at, :] + enters * nn(mem_k, parts(heads_ref, head)[0])
        inverse = 1.0 / (total_in[at, :] + enters * totals_ref[head_rows(head), 0:1])
        score = number * (inverse * SCALE)
        e = jnp.exp(score - jnp.max(score, axis=0, keepdims=True))
        weight = e * (1.0 / jnp.sum(e, axis=0, keepdims=True))
        number_ref[at, :] = number
        inverse_ref[at, :] = inverse
        weight_ref[at, :] = weight
        spreads.append((weight * inverse).astype(BF))
    for (own_side, i), spread in zip(jobs, spreads):
        links.append(causal_pairs(parts(heads_ref, head_of(own_side, i))[3], spread, mask_ref))
        store_pairs(outs[own_side][3:], i, links[-1])
    for (own_side, i), spread, link in zip(jobs, spreads, links):
        head = head_of(own_side, i)
        mem_vt = mem_ref[head_rows(head), :][:, HEAD:]
        mixed = causal_sum(parts(heads_ref, head)[2], link) + enters * nn(mem_vt, spread)
        mixed_ref[head_rows(head), :] = mixed.astype(BF)


def mix(starts, heads, mask, partner, far, local_other, local_own, after=()):
    length, width = heads.shape[2], HEADS * HEAD
    side = [shape(F32, SIDE * HEAD, length)] * 3 + pair_shapes(length)
    mixed, mem, *rest = call(
        mix_body,
        (),
        [SMEM] + [VM] * 8,
        [VM] * 12,
        [shape(BF, width, length), shape(BF, width, 128)] + side + side,
        [pltpu.VMEM((width, 8), F32)],
        us=4.0,
        after=after,
    )(starts, heads, mask, partner, far, *local_other, *local_own)
    return mixed, mem, rest[:5], rest[5:]


def prepare_body(cot_ref, down_other, down_own, other_ref, own_ref, cott_ref):
    cot = cot_ref[...]
    cott_ref[...] = cot.T
    other_ref[...] = nn(cot, down_other[...])
    own_ref[...] = nn(cot, down_own[...])


def prepare(cotangent, down_other, down_own, after=()):
    length, width = cotangent.shape
    return call(
        prepare_body,
        (),
        [VM] * 3,
        [VM] * 3,
        [shape(F32, length, down_own.shape[1])] * 2 + [shape(BF, width, length)],
        us=2.0,
        after=after,
    )(cotangent, down_other, down_own)


def activations(xn, d_hidden_ref, up_ref):
    cols = [slice(j, j + 512) for j in range(0, up_ref.shape[1], 512)]
    pres = [nn(xn, up_ref[:, at]) for at in cols]
    hidden, grad_pre = [], []
    for pre, at in zip(pres, cols):
        v2 = pre * pre
        h = 0.5 + 0.5 * jnp.tanh(pre * (GELU_A + (GELU_A * GELU_B) * v2))
        act = pre * h
        hidden.append(act.astype(BF))
        slope = h + act * (1.0 - h) * (2.0 * GELU_A + (6.0 * GELU_A * GELU_B) * v2)
        grad_pre.append((d_hidden_ref[:, at] * slope).astype(BF))
    return jnp.concatenate(hidden, axis=1), jnp.concatenate(grad_pre, axis=1)


def feed_other_body(x_ref, mixed_ref, cott_ref, d_hidden_ref, w_out_ref, gain_ref, bias_ref, up_ref, down_ref,
                    gup_ref, gdown_ref, hidden1_ref, n_ref, inv_ref, xn_ref, xnt_ref,
                    part_ref, d_ref):
    hidden1 = x_ref[...].astype(F32) + tn(mixed_ref[...], w_out_ref[...])
    hidden1_ref[...] = hidden1
    mean = jnp.mean(hidden1, axis=-1, keepdims=True)
    centered = hidden1 - mean
    inverse = lax.rsqrt(jnp.mean(centered * centered, axis=-1, keepdims=True) + EPSILON)
    n = centered * inverse
    n_ref[...] = n
    inv_ref[...] = jnp.broadcast_to(inverse, inv_ref.shape)
    xn = (n * gain_ref[...] + bias_ref[...]).astype(BF)
    xnt = xn.T
    xn_ref[...] = xn
    xnt_ref[...] = xnt
    hidden, grad_pre = activations(xn, d_hidden_ref, up_ref)
    gdown_ref[...] = nn(cott_ref[...], hidden).astype(BF)
    gup_ref[...] = nn(xnt, grad_pre).astype(BF)
    part_ref[...] = nt(hidden, down_ref[...])
    d_ref[...] = nt(grad_pre, up_ref[...])


def feed_own_body(hidden1_ref, n_ref, inv_ref, xn_ref, xnt_ref, part_ref, d_in_ref, cott_ref, d_hidden_ref,
                  mixed_ref, cot_ref, w_out_ref, gain_ref, up_ref, down_ref,
                  output_ref, d_hidden1_ref, g_ref, out_send_ref, out_keep_ref, norms_ref,
                  gup_ref, gdown_ref):
    hidden, grad_pre = activations(xn_ref[...], d_hidden_ref, up_ref)
    dx, n = d_in_ref[...] + nt(grad_pre, up_ref[...]), n_ref[...]
    norms_ref[...] = jnp.concatenate(
        [jnp.sum(dx * n, axis=0, keepdims=True), jnp.sum(dx, axis=0, keepdims=True)] * 4, axis=0
    )
    output_ref[...] = (hidden1_ref[...] + (part_ref[...] + nt(hidden, down_ref[...]))).astype(BF)
    gdown_ref[...] = nn(cott_ref[...], hidden).astype(BF)
    d_n = dx * gain_ref[...]
    d_in = (
        d_n
        - jnp.mean(d_n, axis=-1, keepdims=True)
        - n * jnp.mean(d_n * n, axis=-1, keepdims=True)
    ) * inv_ref[:, 0:1]
    d_hidden1 = cot_ref[...].astype(F32) + d_in
    d_hidden1_ref[...] = d_hidden1
    d_branch = d_hidden1.astype(BF)
    gup_ref[...] = nn(xnt_ref[...], grad_pre).astype(BF)
    g_ref[...] = nt(w_out_ref[...], d_branch).astype(BF)
    grad_out = nn(mixed_ref[...], d_branch).astype(BF)
    half = grad_out.shape[1] // 2
    second = lax.axis_index("ffn") == 1
    out_keep_ref[...] = jnp.where(second, grad_out[:, half:], grad_out[:, :half])
    out_send_ref[...] = jnp.where(second, grad_out[:, :half], grad_out[:, half:])


def feed_other(x, mixed, cott, d_hidden, w_out, gain, bias, up, down):
    length, width = x.shape
    half, sq = shape(BF, *up.shape), lambda dt: shape(dt, length, width)
    return call(
        feed_other_body,
        (),
        [VM] * 9,
        [VM] * 9,
        [half, half, sq(F32), sq(F32), shape(F32, length, 128), sq(BF), sq(BF), sq(F32), sq(F32)],
        us=6.0,
    )(x, mixed, cott, d_hidden, w_out, gain, bias, up, down)


def feed_own(saved, cott, d_hidden, mixed, cotangent, w_out, gain, up, down, after=()):
    length, width = mixed.shape
    half, sq = shape(BF, *up.shape), lambda dt: shape(dt, length, width)
    return call(
        feed_own_body,
        (),
        [VM] * 15,
        [VM] * 8,
        [sq(BF), sq(F32), sq(BF)] + [shape(BF, width, width // 2)] * 2 + [shape(F32, 8, width), half, half],
        us=6.0,
        after=after,
    )(*saved, cott, d_hidden, mixed, cotangent, w_out, gain, up, down)


def scores_back_body(own_side, starts_ref, heads_ref, mask_ref, g_ref, mem_ref, number_ref, inverse_ref, weight_ref,
                     *refs):
    if own_side:
        pack_in, sums_in, a_ref, spread_ref, d_total_ref, early_ref, late_ref, pack_ref, sums_ref = refs
        pack_ref[...] = pack_in[...]
        sums_ref[...] = sums_in[...]
    else:
        a_ref, spread_ref, d_total_ref, early_ref, late_ref, pack_ref, sums_ref = refs
    length = heads_ref.shape[2]
    enters = enters_row(starts_ref, length)
    heads = [head_of(own_side, i) for i in range(SIDE)]
    rows = [head_rows(head) for head in heads]
    held = [parts(heads_ref, head) for head in heads]
    values = [causal_pairs(held[i][2], g_ref[rows[i], :], mask_ref) for i in range(SIDE)]
    for i in range(SIDE):
        store_pairs((early_ref, late_ref), i, values[i])
    numbers = [
        causal_sum(held[i][3], values[i]) + enters * tn(mem_ref[rows[i], :][:, HEAD:], g_ref[rows[i], :])
        for i in range(SIDE)
    ]
    kept = []
    for i, number_v in enumerate(numbers):
        at = slice(i * HEAD, i * HEAD + HEAD)
        number, inverse, weight = number_ref[at, :], inverse_ref[at, :], weight_ref[at, :]
        d_weight = number_v * inverse
        d_score = weight * (d_weight - jnp.sum(weight * d_weight, axis=0, keepdims=True))
        a = d_score * (inverse * SCALE)
        spread = weight * inverse
        d_total = -(a * number + spread * number_v) * inverse
        a_ref[at, :] = a.astype(BF)
        spread_ref[at, :] = spread.astype(BF)
        d_total_ref[at, :] = d_total.astype(BF)
        kept.append(((a * enters).astype(BF), (spread * enters).astype(BF), d_total * enters))
    for i, (a, spread, d_total) in enumerate(kept):
        d_k = nt(a, held[i][0])
        d_vt = nt(g_ref[rows[i], :], spread)
        pack_ref[rows[i], :] = jnp.concatenate([d_k, d_vt], axis=1).astype(BF)
        sums_ref[rows[i], :] = jnp.broadcast_to(jnp.sum(d_total, axis=1, keepdims=True), (HEAD, 128))
    if own_side:
        pack_totals(pack_ref, sums_ref[...].T[0:8])


def scores_back(own_side, starts, heads, mask, g, mem, saved, packs=(), after=()):
    length, width = heads.shape[2], HEADS * HEAD
    sums = [] if own_side else [shape(F32, width, 128)]
    outs = [shape(BF, SIDE * HEAD, length)] * 3 + pair_shapes(length) + [shape(BF, PACK, 128)] + sums
    return call(
        functools.partial(scores_back_body, own_side),
        (),
        [SMEM] + [VM] * (7 + len(packs)),
        [VM] * len(outs),
        outs,
        [pltpu.VMEM((width, 128), F32)] if own_side else [],
        us=3.0,
        after=after,
    )(starts, heads, mask, g, mem, *saved[:3], *packs)


def heads_back_body(own_side, starts_ref, heads_ref, mask_ref, g_ref, mem_ref, a_ref, spread_ref, d_total_ref,
                    v_early, v_late, l_early, l_late, p_early, p_late, d_ref):
    length = heads_ref.shape[2]
    enters = enters_row(starts_ref, length)
    heads = [head_of(own_side, i) for i in range(SIDE)]
    rows = [head_rows(head) for head in heads]
    held = [parts(heads_ref, head) for head in heads]
    ats = [slice(i * HEAD, i * HEAD + HEAD) for i in range(SIDE)]
    steps = [causal_pairs(held[i][3], a_ref[ats[i], :], mask_ref) for i in range(SIDE)]
    from_totals = causal_back(mask_pair(mask_ref), d_total_ref[...].T).T
    controls = []
    for i in range(SIDE):
        odd = i % 2 == 1
        controls.append(
            causal_back(load_pairs((p_early, p_late), i), padded(a_ref[ats[i], :], odd))
            + causal_back(load_pairs((v_early, v_late), i), padded(spread_ref[ats[i], :], odd))
        )
    for i in range(SIDE):
        mem_k = mem_ref[rows[i], :][:, :HEAD]
        d_ref[i, :HEAD, :] = causal_sum(held[i][1], steps[i]) + enters * tn(mem_k, a_ref[ats[i], :])
    for i in range(SIDE):
        d_ref[i, HEAD : 3 * HEAD, :] = (
            causal_back(steps[i], padded(held[i][0], False))
            + causal_back(load_pairs((l_early, l_late), i), padded(g_ref[rows[i], :], True))
        ).T
    for i in range(0, SIDE, 2):
        two = (controls[i] + controls[i + 1]).T
        for n in range(2):
            d_ref[i + n, 3 * HEAD :, :] = two[n * HEAD : n * HEAD + HEAD] + from_totals[ats[i + n]]


def heads_back(own_side, starts, heads, mask, g, mem, scores, links, pairs, after=()):
    length = heads.shape[2]
    return call(
        functools.partial(heads_back_body, own_side),
        (),
        [SMEM] + [VM] * 13,
        VM,
        shape(F32, SIDE, 4 * HEAD, length),
        us=1.0,
        after=after,
    )(starts, heads, mask, g, mem, *scores, *links, *pairs)


def project_back_body(starts_ref, heads_ref, d_other, d_own, control_ref, partner_ref, far_ref, xnt_ref,
                      proj_ref, keep_ref, send_ref, mem_ref, totals_ref):
    length, width = xnt_ref.shape[1], xnt_ref.shape[0]
    arrived(True, length, starts_ref, partner_ref, far_ref, mem_ref, totals_ref)
    tail = tail_row(doc_begin_row(starts_ref, length), length)
    tail_bf = tail.astype(BF)
    jobs = [(d_ref, n, head_of(own_side, n)) for own_side, d_ref in ((False, d_other), (True, d_own)) for n in range(SIDE)]
    more = []
    for d_ref, n, head in jobs:
        mem = mem_ref[head_rows(head), :]
        back_k, back_vt = mem[:, :HEAD], mem[:, HEAD:]
        q, k, v, c = parts(heads_ref, head)
        c_tail = c * tail_bf
        more.append((tn(back_k, c_tail), nn(back_vt, c_tail), nn(back_k, k) + tn(back_vt, v)))
    for (d_ref, n, head), (more_k, more_v, more_c) in zip(jobs, more):
        rows = head_rows(head)
        proj_ref[0, rows, :] = d_ref[n, :HEAD, :].astype(BF)
        proj_ref[1, rows, :] = (d_ref[n, HEAD : 2 * HEAD, :] + more_k).astype(BF)
        proj_ref[2, rows, :] = (d_ref[n, 2 * HEAD : 3 * HEAD, :] + more_v).astype(BF)
        d_control = d_ref[n, 3 * HEAD :, :] + tail * (more_c + totals_ref[rows, 0:1])
        proj_ref[3, rows, :] = (d_control * control_ref[rows, :]).astype(BF)
    for own_side in (False, True):
        first = pl.ds(pl.multiple_of(head_of(own_side, 0) * HEAD, SIDE * HEAD), SIDE * HEAD)
        for m in range(4):
            grad = nt(xnt_ref[...], proj_ref[m, first, :]).astype(BF)
            if own_side:
                keep_ref[:, m * SIDE * HEAD : (m + 1) * SIDE * HEAD] = grad
            else:
                send_ref[:, m * SIDE * HEAD : (m + 1) * SIDE * HEAD] = grad


def project_back(starts, heads, d_other, d_own, control, partner, far, xnt, after=()):
    width, length = xnt.shape
    return call(
        project_back_body,
        (),
        [SMEM] + [VM] * 7,
        [VM] * 3,
        [shape(BF, 4, width, length)] + [shape(BF, width, 4 * SIDE * HEAD)] * 2,
        [pltpu.VMEM((width, 128), BF), pltpu.VMEM((width, 8), F32)],
        us=5.0,
        after=after,
    )(starts, heads, d_other, d_own, control, partner, far, xnt)


def norm_back_body(proj_ref, w_ref, x_ref, gain_ref, d_hidden1_ref, norms2_ref, grad_x_ref, norms_ref):
    length, width = x_ref.shape
    dx = nn(w_ref[...], proj_ref[...].reshape(4 * width, length))
    x = x_ref[...].astype(F32)
    mean = jnp.mean(x, axis=-1, keepdims=True)
    centered = x - mean
    inverse = lax.rsqrt(jnp.mean(centered * centered, axis=-1, keepdims=True) + EPSILON)
    n = centered * inverse
    d = dx.T
    sums = [jnp.sum(d * n, axis=0, keepdims=True), jnp.sum(d, axis=0, keepdims=True)]
    rows8 = jnp.concatenate(sums + [norms2_ref[0:6, :]], axis=0)
    norms_ref[...] = jnp.concatenate([rows8, jnp.zeros((120, length), F32)], axis=0).T.astype(BF)
    d_n = d * gain_ref[...]
    grad_x_ref[...] = d_hidden1_ref[...] + (
        d_n
        - jnp.mean(d_n, axis=-1, keepdims=True)
        - n * jnp.mean(d_n * n, axis=-1, keepdims=True)
    ) * inverse


def norm_back(proj, w, x, gain, d_hidden1, norms2, after=()):
    length, width = x.shape
    return call(
        norm_back_body,
        (),
        [VM] * 6,
        [VM] * 2,
        [shape(F32, length, width), shape(BF, width, 128)],
        us=0.1,
        after=after,
    )(proj, w, x, gain, d_hidden1, norms2)


def bit_axis(bit):
    return ("seq", 1) if bit == 0 else ("dp", 1 << (bit - 1))


def my_bit(bit):
    axis, step = bit_axis(bit)
    return (lax.axis_index(axis) // step) % 2


def send_across(a, bits):
    seqs, dps = lax.axis_size("seq"), lax.axis_size("dp")
    flip = sum(1 << bit for bit in bits)
    return lax.ppermute(a, ("dp", "seq"), [(i, i ^ flip) for i in range(seqs * dps)])


def place_of(t, places, values):
    index, rest, bit = 0, t, 0
    fixed = dict(zip(places, values))
    while rest or fixed:
        if bit in fixed:
            index = index + fixed.pop(bit) * (1 << bit)
        else:
            index = index + ((rest & 1) << bit)
            rest >>= 1
        bit += 1
    return index


def stage_body(plan, *refs):
    refs = list(refs)
    ins = [
        [[refs.pop(0).at[:, :, pl.ds(*piece)] for piece in pieces] for pieces in arrays] for arrays, _ in plan
    ]
    for (arrays, split), sources in zip(plan, ins):
        outs = [refs.pop(0) for _ in range(1 << len(split))]
        blocks = outs[0].shape[0]
        places = [place for _, place in split]
        mine = [my_bit(bit) for bit, _ in split]
        for pattern, out in enumerate(outs):
            values = [
                (1 - m) if (pattern >> n) & 1 else m for n, m in enumerate(mine)
            ]
            for t in range(blocks):
                at = place_of(t, places, values)
                rows = [
                    jnp.concatenate([p[at] for p in pieces], axis=1) if len(pieces) > 1 else pieces[0][at]
                    for pieces in sources
                ]
                if len(rows) == 1 or (len(rows) == 2 and out.dtype == BF):
                    total = sum(rows[1:], rows[0])
                else:
                    total = sum(row.astype(F32) for row in rows)
                out[t] = total.astype(out.dtype)


def stage(groups, after=(), dtype=BF):
    plan, operands, out_shape = [], [], []
    for arrays, split in groups:
        for pieces in arrays:
            operands += [array for array, _, _ in pieces]
        (array, _, _), width = arrays[0][0], sum(p[2] for p in arrays[0])
        plan.append(([[(first, count) for _, first, count in pieces] for pieces in arrays], split))
        out_shape += [shape(dtype, array.shape[0] >> len(split), array.shape[1], width)] * (1 << len(split))
    outs = list(
        call(functools.partial(stage_body, plan), (), [VM] * len(operands), [VM] * len(out_shape), out_shape, after=after)(
            *operands
        )
    )
    return [[outs.pop(0) for _ in range(1 << len(split))] for _, split in groups]


def all_of(a):
    return [(a, 0, a.shape[2])]


def patterns(bits):
    return [[b for n, b in enumerate(bits) if (p >> n) & 1] for p in range(1, 1 << len(bits))]


def finish_body(a_ref, b_ref, up_ref, down_ref, out_ref):
    total = a_ref[0].astype(F32) + b_ref[0].astype(F32)
    half, part = up_ref.shape[1], out_ref.shape[1] // 2
    up_ref[...] = total[:, :half]
    down_ref[...] = total[:, half + part : 2 * half + part]
    out_ref[:, :part] = total[:, half : half + part].astype(BF)
    out_ref[:, part:] = total[:, 2 * half + part :].astype(BF)


def finish(a, b, half, part, after=()):
    rows = a.shape[1]
    return call(
        finish_body,
        (),
        [VM] * 2,
        [VM] * 3,
        [jax.ShapeDtypeStruct((rows, half), F32)] * 2 + [jax.ShapeDtypeStruct((rows, 2 * part), BF)],
        after=after,
    )(a, b)


def join_body(own_ref, other_ref, out_own, out_other, grad_in_ref, grad_out_ref, *norm_refs):
    second = lax.axis_index("ffn") == 1
    own, other = own_ref[0].astype(F32), other_ref[0].astype(F32)
    for f in range(2):
        keep_own = second if f else jnp.logical_not(second)
        half = jnp.where(keep_own, own[:, :1024], other[:, :1024])
        for m in range(4):
            grad_in_ref[:, m * 512 + f * 256 : m * 512 + f * 256 + 256] = half[:, m * 256 : m * 256 + 256]
        grad_out_ref[:, f * 256 : f * 256 + 256] = jnp.where(
            keep_own, out_own[...], out_other[...]
        ).astype(F32)
    norms = (own[:, 1024:] + other[:, 1024:]).T
    for n, ref in enumerate(norm_refs):
        ref[...] = norms[n]


def join(own, other, out_own, out_other):
    rows = own.shape[1]
    return call(
        join_body,
        (),
        [VM] * 4,
        [VM] * 6,
        [jax.ShapeDtypeStruct((rows, n), F32) for n in (2048, 512)] + [jax.ShapeDtypeStruct((rows,), F32)] * 4,
    )(own, other, out_own, out_other)


def on_device(tokens, doc_starts, norm1_gain, norm1_bias, in_weight, out_weight,
              norm2_gain, norm2_bias, up_own, down_own, output_cotangent):
    up_other, down_other = swap(up_own, "ffn", 1), swap(down_own, "ffn", 1)
    x, cotangent, starts = tokens[0], output_cotangent[0], doc_starts
    length, width = x.shape
    owners = lax.axis_size("dp") * lax.axis_size("seq")
    bits = owners.bit_length() - 1
    row = lambda a: a.reshape(1, width)
    blocked = lambda a: a.reshape(owners, width // owners, a.shape[1])

    heads, control, xnt, own, mask = project(x, row(norm1_gain), row(norm1_bias), in_weight, starts)
    partner = swap(own, "ffn", 1)
    number_o, total_o, *pairs_other = local_sums(False, heads, mask)
    both = combine(False, length, starts, own, partner, after=[number_o])
    far = swap(both, "seq", 1)
    number, total, *pairs_own = local_sums(True, heads, mask, after=[both])
    d_hidden_other, d_hidden_own, cott = prepare(cotangent, down_other, down_own, after=[number])
    mixed, memory, saved_other, saved_own = mix(
        starts, heads, mask, partner, far, (number_o, total_o), (number, total), after=[cott])
    gup_send, gdown_send, *saved = feed_other(
        x, mixed, cott, d_hidden_other, out_weight, row(norm2_gain), row(norm2_bias), up_other, down_other)
    gup_got, gdown_got = swap(gup_send, "ffn", 1), swap(gdown_send, "ffn", 1)
    (output, d_hidden1, g, out_send, out_keep, norms2, gup_own, gdown_own) = feed_own(
        saved, cott, d_hidden_own, mixed, cotangent, out_weight, row(norm2_gain), up_own, down_own)
    out_got = swap(out_send, "ffn", 1)

    out_half = width // 4
    ups, downs, outs = [
        [blocked(a) for a in pair]
        for pair in ((gup_own, gup_got), (gdown_own, gdown_got), (out_keep, out_got))
    ]
    groups = [
        [[*all_of(a), (o, 0, out_half)] for a, o in zip(ups, outs)],
        [[*all_of(a), (o, out_half, out_half)] for a, o in zip(downs, outs)],
    ]
    orders = [[1, 2], [2, 1]]
    left = [list(range(bits)) for _ in groups]

    def advance(groups, n, after):
        if n >= 2:
            if n == 2:
                groups = [[pieces_a + pieces_b for pieces_a, pieces_b in zip(*groups)]]
            bits_now = left[0][-1:]
            splits = [[(bits_now[0], len(left[0]) - 1)]]
            for rest in left:
                rest.pop()
        else:
            bits_now = [order[n] for order in orders]
            splits = [[(bit, rest.index(bit))] for bit, rest in zip(bits_now, left)]
            for bit, rest in zip(bits_now, left):
                rest.remove(bit)
        outs = stage(list(zip(groups, splits)), after=after)
        got = [send_across(sent, [bit]) for (_, sent), bit in zip(outs, bits_now)]
        sent = [s for _, s in outs]
        return [[all_of(kept), all_of(r)] for (kept, _), r in zip(outs, got)], sent

    back = (starts, heads, mask, g, memory)
    *scores_other, pack, sums = scores_back(False, *back, saved_other)
    groups, sent = advance(groups, 0, [pack])
    *scores_own, d_own = scores_back(True, *back, saved_own, packs=(pack, sums), after=sent)
    d_partner = swap(d_own, "ffn", 1)
    d_both = combine(True, length, starts, d_own, d_partner)
    d_far = swap(d_both, "seq", 1)
    d_other = heads_back(False, *back, scores_other, saved_other[3:], pairs_other, after=[d_both])
    d_mine = heads_back(True, *back, scores_own, saved_own[3:], pairs_own, after=[d_other])
    groups, sent = advance(groups, 1, [d_mine])
    proj, in_keep, in_send = project_back(
        starts, heads, d_other, d_mine, control, d_partner, d_far, xnt, after=sent)
    in_got = swap(in_send, "ffn", 1)
    grad_tokens, norms = norm_back(
        proj, in_weight, x, row(norm1_gain), d_hidden1, norms2, after=[in_send])

    late = [
        all_of(blocked(in_keep)) + all_of(blocked(norms)),
        all_of(blocked(in_got)) + all_of(jnp.zeros_like(blocked(norms))),
    ]
    rest = list(range(bits))
    stages = list(range(2, bits))
    while rest:
        now = rest[:2]
        split = [(b, rest.index(b)) for b in now]
        rest = rest[2:]
        (kept, *sent), = stage([(late, split)])
        late = [all_of(kept)] + [all_of(send_across(s, p)) for s, p in zip(sent, patterns(now))]
        token = [kept]
        while stages:
            groups, token = advance(groups, stages.pop(0), token)
            if rest:
                break
    grad_up, grad_down, out = finish(*(a[0][0] for a in groups[0]), gup_own.shape[1], out_half, after=[kept])
    (final,), = stage([(late, [])], after=[out])
    grad_in, grad_out, *norms = join(final, swap(final, "ffn", 1), out, swap(out, "ffn", 1))
    return (output[None], grad_tokens[None], grad_in, grad_out, grad_up, grad_down, *norms)


def solution(mesh):
    rows = P("dp", ("seq", "ffn"), None)
    owned = P(("dp", "seq"))
    return jax.shard_map(
        on_device,
        mesh=mesh,
        in_specs=(
            rows, P("dp", None), P(), P(), P(), P(), P(), P(),
            P(None, "ffn"), P(None, "ffn"), rows,
        ),
        out_specs=(
            rows, rows, P(("dp", "seq"), None), P(("dp", "seq"), None),
            P(("dp", "seq"), "ffn"), P(("dp", "seq"), "ffn"),
            owned, owned, owned, owned,
        ),
        check_vma=False,
    )
```

```python
import functools

import jax
import jax.numpy as jnp
from jax import lax
from jax.experimental import pallas as pl
from jax.experimental.pallas import tpu as pltpu
from jax.sharding import PartitionSpec as P

HEADS = 8
HEAD = 64
EPSILON = 1e-05
BF = jnp.bfloat16
F32 = jnp.float32
GELU_A = 0.7978845608028654
GELU_B = 0.044715
SCALE = HEAD**-0.5
K1_VMEM = 48
SPLIT = 2
SIDE = HEADS // 2
PACK = HEADS * HEAD + 64


def nn(a, b):
    return lax.dot_general(a, b, (((1,), (0,)), ((), ())), preferred_element_type=F32)


def nt(a, b):
    return lax.dot_general(a, b, (((1,), (1,)), ((), ())), preferred_element_type=F32)


def tn(a, b):
    return lax.dot_general(a, b, (((0,), (0,)), ((), ())), preferred_element_type=F32)


def swap(a, axis, bit):
    size = lax.axis_size(axis)
    return lax.ppermute(a, axis, [(i, i ^ bit) for i in range(size)])


ANY = pl.BlockSpec(memory_space=pl.ANY)


def call(body, grid, in_specs, out_specs, out_shape, scratch=(), us=1.0, after=(), vmem=20):
    count = len(in_specs)

    def run(*refs):
        body(*refs[:count], *refs[count + len(after) :])

    def start(*operands):
        return pl.pallas_call(
            run,
            grid=grid,
            in_specs=list(in_specs) + [ANY] * len(after),
            out_specs=out_specs,
            out_shape=out_shape,
            scratch_shapes=list(scratch),
            cost_estimate=pl.CostEstimate(flops=int(us * 1e7), bytes_accessed=2**13, transcendentals=0),
            compiler_params=pltpu.CompilerParams(vmem_limit_bytes=vmem * 2**20),
        )(*operands, *after)

    return start


def whole(shape):
    return pl.BlockSpec(shape, lambda *_: (0,) * len(shape))


VM = pl.BlockSpec(memory_space=pltpu.MemorySpace.VMEM)


def shape(dtype, *dims):
    return jax.ShapeDtypeStruct(dims, dtype)


SMEM = pl.BlockSpec(memory_space=pltpu.SMEM)


def shard_of():
    return lax.axis_index("seq") * 2 + lax.axis_index("ffn")


def doc_begin_row(starts_ref, length):
    begin = shard_of() * length
    place = lax.broadcasted_iota(jnp.int32, (1, length), 1)
    row = jnp.full((1, length), -(2**30), jnp.int32)
    for j in range(starts_ref.shape[1]):
        s = starts_ref[0, j] - begin
        row = jnp.where(place >= s, jnp.maximum(row, s), row)
    return row


def passes(starts_ref, which, length):
    hit = jnp.int32(0)
    for j in range(starts_ref.shape[1]):
        s = starts_ref[0, j]
        hit = hit | ((s >= which * length) & (s < which * length + length)).astype(jnp.int32)
    return 1.0 - hit.astype(F32)


def visible(doc_row, length):
    i = lax.broadcasted_iota(jnp.int32, (length, length), 0)
    t = lax.broadcasted_iota(jnp.int32, (length, length), 1)
    return jnp.where((i <= t) & (i >= doc_row), 1.0, 0.0).astype(BF)


def tail_row(doc_row, length):
    place = lax.broadcasted_iota(jnp.int32, (1, length), 1)
    last = doc_row[:, length - 1 :]
    return jnp.where(place >= last, 1.0, 0.0)


def pack_totals(pack_ref, totals8):
    base = HEADS * HEAD
    hi = totals8.astype(BF)
    lo = (totals8 - hi.astype(F32)).astype(BF)
    for a in range(4):
        cols = slice(128 * a, 128 * a + 128)
        pack_ref[base + 16 * a : base + 16 * a + 16, :] = jnp.concatenate(
            [hi[:, cols], lo[:, cols]], axis=0
        )


def unpack(rows, totals8_of):
    base = HEADS * HEAD
    out = []
    for a in range(4):
        block = totals8_of(slice(base + 16 * a, base + 16 * a + 16))
        out.append(block[:8] + block[8:])
    return rows(slice(0, base)), jnp.concatenate(out, axis=1)


def combine_body(backward, rows_ref, own_ref, partner_ref, out_ref):
    is_first = (lax.axis_index("ffn") == 0).astype(F32)
    base = HEADS * HEAD
    if backward:
        p = rows_ref[2:3, :128]
        own_by, partner_by = is_first + (1 - is_first) * p, is_first * p + (1 - is_first)
    else:
        p = rows_ref[3:4, :128]
        own_by, partner_by = is_first * p + (1 - is_first), is_first + (1 - is_first) * p

    def sum_of(at):
        return own_ref[at, :].astype(F32) * own_by + partner_ref[at, :].astype(F32) * partner_by

    memory, totals8 = unpack(sum_of, sum_of)
    out_ref[:base, :] = memory.astype(BF)
    pack_totals(out_ref, totals8)


def combine(backward, rows, own, partner, after=()):
    return call(
        functools.partial(combine_body, backward),
        (),
        [VM] * 3,
        VM,
        shape(BF, PACK, 128),
        after=after,
    )(rows, own, partner)


def arrived(backward, rows_ref, partner_ref, far_ref, mem_ref, totals_ref):
    is_first = (lax.axis_index("ffn") == 0).astype(F32)
    if backward:
        p = rows_ref[3:4, :128]
        far_by, partner_by = is_first * p + (1 - is_first), is_first
        valid = lax.axis_index("seq") == 0
    else:
        p = rows_ref[2:3, :128]
        far_by, partner_by = is_first + (1 - is_first) * p, 1 - is_first
        valid = lax.axis_index("seq") == 1

    def sum_of(at):
        far = jnp.where(valid, far_ref[at, :].astype(F32), 0.0)
        return far * far_by + partner_ref[at, :].astype(F32) * partner_by

    memory, totals8 = unpack(sum_of, sum_of)
    mem_ref[...] = memory.astype(BF)
    totals_ref[...] = totals8.T


def head_of(own_side, h):
    ffn = lax.axis_index("ffn")
    return (ffn if own_side else 1 - ffn) * SIDE + h


def head_rows(head):
    return pl.ds(pl.multiple_of(head * HEAD, HEAD), HEAD)


def project_body(x_hbm, gain_hbm, bias_hbm, w_hbm, starts_ref,
                 heads_ref, raw_ref, xn_ref, pack_ref, mask_ref, rows_ref, n_ref, inv_ref,
                 x_ref, gain_ref, bias_ref, w_ref, sems):
    length, width = x_ref.shape
    copies = [
        pltpu.make_async_copy(x_hbm, x_ref, sems.at[0]),
        pltpu.make_async_copy(gain_hbm, gain_ref, sems.at[1]),
        pltpu.make_async_copy(bias_hbm, bias_ref, sems.at[2]),
    ]
    columns = [
        pltpu.make_async_copy(w_hbm.at[:, pl.ds(j * width, width)], w_ref.at[j], sems.at[3 + j])
        for j in range(4)
    ]
    for copy in copies + columns:
        copy.start()
    doc_row = doc_begin_row(starts_ref, length)
    tail = tail_row(doc_row, length)
    first = 2 * lax.axis_index("seq")
    rows = [jnp.where(doc_row < 0, 1.0, 0.0), tail] + [
        jnp.full((1, length), passes(starts_ref, which, length)) for which in (first, first + 1)
    ]
    rows_ref[...] = jnp.concatenate(rows + rows, axis=0)
    mask_ref[...] = visible(doc_row, length)
    for copy in copies:
        copy.wait()
    x = x_ref[...].astype(F32)
    mean = jnp.mean(x, axis=-1, keepdims=True)
    centered = x - mean
    inverse = lax.rsqrt(jnp.mean(centered * centered, axis=-1, keepdims=True) + EPSILON)
    n = centered * inverse
    n_ref[...] = n
    inv_ref[...] = jnp.broadcast_to(inverse, inv_ref.shape)
    xn = (n * gain_ref[...] + bias_ref[...]).astype(BF)
    xn_ref[...] = xn
    projected = []
    for j in range(4):
        columns[j].wait()
        projected.append(nn(xn, w_ref[j]))
    raw_ref[...] = projected[3]
    c = jnp.exp(projected[3]).astype(BF).T
    for j in range(3):
        t = projected[j].astype(BF).T
        for h in range(HEADS):
            heads_ref[h, j * HEAD : j * HEAD + HEAD, :] = t[h * HEAD : h * HEAD + HEAD]
    c_tail = c * tail.astype(BF)
    for h in range(HEADS):
        rows = slice(h * HEAD, h * HEAD + HEAD)
        heads_ref[h, 3 * HEAD :, :] = c[rows]
        mem_k = nt(c_tail[rows], heads_ref[h, HEAD : 2 * HEAD, :])
        mem_vt = nt(heads_ref[h, 2 * HEAD : 3 * HEAD, :], c_tail[rows])
        pack_ref[rows, :] = jnp.concatenate([mem_k, mem_vt], axis=1).astype(BF)
    tail8 = jnp.broadcast_to(tail, (8, length)).astype(BF)
    pack_totals(pack_ref, nt(tail8, c))


def project(x, gain, bias, w, starts):
    length, width = x.shape
    hbm = pl.BlockSpec(memory_space=pltpu.MemorySpace.HBM)
    pin = lambda a: pltpu.with_memory_space_constraint(a, pltpu.HBM)
    return call(
        project_body,
        (),
        [hbm, hbm, hbm, hbm, SMEM],
        [VM] * 8,
        [
            shape(BF, HEADS, 4 * HEAD, length), shape(F32, length, width), shape(BF, length, width),
            shape(BF, PACK, 128), shape(BF, length, length), shape(F32, 8, length),
            shape(F32, length, width), shape(F32, length, 128),
        ],
        [
            pltpu.VMEM((length, width), BF), pltpu.VMEM((1, width), F32), pltpu.VMEM((1, width), F32),
            pltpu.VMEM((4, width, width), BF), pltpu.SemaphoreType.DMA((7,)),
        ],
        us=4.3,
        vmem=K1_VMEM,
    )(*(pin(a) for a in (x, gain, bias, w, starts)))


def parts(heads_ref, head):
    return [heads_ref[head, j * HEAD : j * HEAD + HEAD, :] for j in range(4)]


def mask_pair(mask_ref):
    half = mask_ref.shape[0] // 2
    return mask_ref[:half, :half], mask_ref[:, half:]


def causal_pairs(left, right, mask_ref):
    half = mask_ref.shape[0] // 2
    early, late = mask_pair(mask_ref)
    rows = left.T
    return nn(rows[:half], right[:, :half]).astype(BF) * early, nn(rows, right[:, half:]).astype(BF) * late


def causal_sum(left, pairs):
    a, b = pairs
    half = a.shape[0]
    return jnp.concatenate([nn(left[:, :half], a), nn(left, b)], axis=1)


def causal_back(pairs, right):
    a, b = pairs
    half = a.shape[0]
    late = nn(b, right[half:])
    return jnp.concatenate([late[:half] + nn(a, right[:half]), late[half:]], axis=0)


def padded(rows, second):
    zero = jnp.zeros_like(rows)
    return jnp.concatenate([zero, rows] if second else [rows, zero], axis=0).T


def pair_shapes(length, count=SIDE):
    half = length // 2
    return [shape(BF, count, half, half), shape(BF, count, length, half)]


def store_pairs(refs, i, pairs):
    refs[0][i], refs[1][i] = pairs


def load_pairs(refs, i):
    return refs[0][i], refs[1][i]


def local_body(own_side, heads_ref, mask_ref, number_ref, total_ref, *pair_refs):
    held = [parts(heads_ref, head_of(own_side, i)) for i in range(SIDE)]
    pairs = [causal_pairs(k, q, mask_ref) for q, k, v, c in held]
    for i in range(SIDE):
        store_pairs(pair_refs, i, pairs[i])
    c = jnp.concatenate([h[3] for h in held], axis=0)
    total_ref[...] = causal_sum(c, mask_pair(mask_ref))
    for i in range(SIDE):
        number_ref[i * HEAD : i * HEAD + HEAD, :] = causal_sum(held[i][3], pairs[i])


def local_sums(own_side, heads, mask, after=()):
    length = heads.shape[2]
    return call(
        functools.partial(local_body, own_side),
        (),
        [VM, VM],
        [VM] * 4,
        [shape(F32, SIDE * HEAD, length)] * 2 + pair_shapes(length),
        us=3.0,
        after=after,
    )(heads, mask)


def mix_body(rows_ref, heads_ref, mask_ref, partner_ref, far_ref, *refs):
    refs = list(refs)
    take = lambda n: [refs.pop(0) for _ in range(n)]
    ins = [take(2), take(2)]
    mixed_ref, mem_ref = take(2)
    outs = [take(5), take(5)]
    (totals_ref,) = refs
    arrived(False, rows_ref, partner_ref, far_ref, mem_ref, totals_ref)
    enters = rows_ref[0:1, :]
    jobs = [(own_side, i) for own_side in (False, True) for i in range(SIDE)]
    spreads, links = [], []
    for own_side, i in jobs:
        number_in, total_in = ins[own_side]
        number_ref, inverse_ref, weight_ref, *_ = outs[own_side]
        head, at = head_of(own_side, i), slice(i * HEAD, i * HEAD + HEAD)
        mem_k = mem_ref[head_rows(head), :][:, :HEAD]
        number = number_in[at, :] + enters * nn(mem_k, parts(heads_ref, head)[0])
        inverse = 1.0 / (total_in[at, :] + enters * totals_ref[head_rows(head), 0:1])
        score = number * (inverse * SCALE)
        e = jnp.exp(score - jnp.max(score, axis=0, keepdims=True))
        weight = e * (1.0 / jnp.sum(e, axis=0, keepdims=True))
        number_ref[at, :] = number
        inverse_ref[at, :] = inverse
        weight_ref[at, :] = weight
        spreads.append((weight * inverse).astype(BF))
    for (own_side, i), spread in zip(jobs, spreads):
        links.append(causal_pairs(parts(heads_ref, head_of(own_side, i))[3], spread, mask_ref))
        store_pairs(outs[own_side][3:], i, links[-1])
    for (own_side, i), spread, link in zip(jobs, spreads, links):
        head = head_of(own_side, i)
        mem_vt = mem_ref[head_rows(head), :][:, HEAD:]
        mixed = causal_sum(parts(heads_ref, head)[2], link) + enters * nn(mem_vt, spread)
        mixed_ref[head_rows(head), :] = mixed.astype(BF)


def mix(rows, heads, mask, partner, far, local_other, local_own, after=()):
    length, width = heads.shape[2], HEADS * HEAD
    side = [shape(F32, SIDE * HEAD, length)] * 3 + pair_shapes(length)
    mixed, mem, *rest = call(
        mix_body,
        (),
        [VM] * 9,
        [VM] * 12,
        [shape(BF, width, length), shape(BF, width, 128)] + side + side,
        [pltpu.VMEM((width, 8), F32)],
        us=4.0,
        after=after,
    )(rows, heads, mask, partner, far, *local_other, *local_own)
    return mixed, mem, rest[:5], rest[5:]


def prepare_body(cot_ref, down_ref, down_other_ref, raw_ref, xn_ref, other_ref, own_ref, cott_ref, control_ref, xnt_ref):
    cot = cot_ref[...]
    other_ref[...] = nn(cot, down_other_ref[...])
    own_ref[...] = nn(cot, down_ref[...])
    cott_ref[...] = cot.T
    xnt_ref[...] = xn_ref[...].T
    control_ref[...] = jnp.exp(raw_ref[...]).T


def prepare(cotangent, down, down_other, raw, xn, after=()):
    length, width = cotangent.shape
    return call(
        prepare_body,
        (),
        [VM] * 5,
        [VM] * 5,
        [shape(F32, length, down.shape[1])] * 2
        + [shape(BF, width, length), shape(F32, width, length), shape(BF, width, length)],
        us=2.0,
        after=after,
    )(cotangent, down, down_other, raw, xn)


def activations(xn, d_hidden_ref, up_ref):
    cols = [slice(j, j + 512) for j in range(0, up_ref.shape[1], 512)]
    pres = [nn(xn, up_ref[:, at]) for at in cols]
    hidden, grad_pre = [], []
    for pre, at in zip(pres, cols):
        v2 = pre * pre
        h = 0.5 + 0.5 * jnp.tanh(pre * (GELU_A + (GELU_A * GELU_B) * v2))
        act = pre * h
        hidden.append(act.astype(BF))
        slope = h + act * (1.0 - h) * (2.0 * GELU_A + (6.0 * GELU_A * GELU_B) * v2)
        grad_pre.append((d_hidden_ref[:, at] * slope).astype(BF))
    return jnp.concatenate(hidden, axis=1), jnp.concatenate(grad_pre, axis=1)


def feed_other_body(x_ref, mixed_ref, cott_ref, d_hidden_ref, w_out_ref, gain_ref, bias_ref, up_ref, down_ref,
                    gup_ref, gdown_ref, hidden1_ref, n_ref, inv_ref, xn_ref, xnt_ref,
                    part_ref, d_ref):
    hidden1 = x_ref[...].astype(F32) + tn(mixed_ref[...], w_out_ref[...])
    hidden1_ref[...] = hidden1
    mean = jnp.mean(hidden1, axis=-1, keepdims=True)
    centered = hidden1 - mean
    inverse = lax.rsqrt(jnp.mean(centered * centered, axis=-1, keepdims=True) + EPSILON)
    n = centered * inverse
    n_ref[...] = n
    inv_ref[...] = jnp.broadcast_to(inverse, inv_ref.shape)
    xn = (n * gain_ref[...] + bias_ref[...]).astype(BF)
    xnt = xn.T
    xn_ref[...] = xn
    xnt_ref[...] = xnt
    hidden, grad_pre = activations(xn, d_hidden_ref, up_ref)
    gdown_ref[...] = nn(cott_ref[...], hidden).astype(BF)
    gup_ref[...] = nn(xnt, grad_pre).astype(BF)
    part_ref[...] = nt(hidden, down_ref[...])
    d_ref[...] = nt(grad_pre, up_ref[...])


def feed_own_body(hidden1_ref, n_ref, inv_ref, xn_ref, xnt_ref, part_ref, d_in_ref, cott_ref, d_hidden_ref,
                  mixed_ref, cot_ref, w_out_ref, gain_ref, up_ref, down_ref,
                  output_ref, d_hidden1_ref, g_ref, out_send_ref, out_keep_ref, norms_ref,
                  gup_ref, gdown_ref):
    hidden, grad_pre = activations(xn_ref[...], d_hidden_ref, up_ref)
    dx, n = d_in_ref[...] + nt(grad_pre, up_ref[...]), n_ref[...]
    norms_ref[...] = jnp.concatenate(
        [jnp.sum(dx * n, axis=0, keepdims=True), jnp.sum(dx, axis=0, keepdims=True)] * 4, axis=0
    )
    output_ref[...] = (hidden1_ref[...] + (part_ref[...] + nt(hidden, down_ref[...]))).astype(BF)
    gdown_ref[...] = nn(cott_ref[...], hidden).astype(BF)
    d_n = dx * gain_ref[...]
    d_in = (
        d_n
        - jnp.mean(d_n, axis=-1, keepdims=True)
        - n * jnp.mean(d_n * n, axis=-1, keepdims=True)
    ) * inv_ref[:, 0:1]
    d_hidden1 = cot_ref[...].astype(F32) + d_in
    d_hidden1_ref[...] = d_hidden1
    d_branch = d_hidden1.astype(BF)
    gup_ref[...] = nn(xnt_ref[...], grad_pre).astype(BF)
    g_ref[...] = nt(w_out_ref[...], d_branch).astype(BF)
    grad_out = nn(mixed_ref[...], d_branch).astype(BF)
    half = grad_out.shape[1] // 2
    second = lax.axis_index("ffn") == 1
    out_keep_ref[...] = jnp.where(second, grad_out[:, half:], grad_out[:, :half])
    out_send_ref[...] = jnp.where(second, grad_out[:, :half], grad_out[:, half:])


def feed_other(x, mixed, cott, d_hidden, w_out, gain, bias, up, down):
    length, width = x.shape
    half, sq = shape(BF, *up.shape), lambda dt: shape(dt, length, width)
    return call(
        feed_other_body,
        (),
        [VM] * 9,
        [VM] * 9,
        [half, half, sq(F32), sq(F32), shape(F32, length, 128), sq(BF), sq(BF), sq(F32), sq(F32)],
        us=6.0,
    )(x, mixed, cott, d_hidden, w_out, gain, bias, up, down)


def feed_own(saved, cott, d_hidden, mixed, cotangent, w_out, gain, up, down, after=()):
    length, width = mixed.shape
    half, sq = shape(BF, *up.shape), lambda dt: shape(dt, length, width)
    return call(
        feed_own_body,
        (),
        [VM] * 15,
        [VM] * 8,
        [sq(BF), sq(F32), sq(BF)] + [shape(BF, width, width // 2)] * 2 + [shape(F32, 8, width), half, half],
        us=6.0,
        after=after,
    )(*saved, cott, d_hidden, mixed, cotangent, w_out, gain, up, down)


def scores_back_body(own_side, rows_ref, heads_ref, mask_ref, g_ref, mem_ref, number_ref, inverse_ref, weight_ref,
                     *refs):
    if own_side:
        pack_in, sums_in, a_ref, spread_ref, d_total_ref, early_ref, late_ref, pack_ref, sums_ref = refs
        pack_ref[...] = pack_in[...]
        sums_ref[...] = sums_in[...]
    else:
        a_ref, spread_ref, d_total_ref, early_ref, late_ref, pack_ref, sums_ref = refs
    enters = rows_ref[0:1, :]
    heads = [head_of(own_side, i) for i in range(SIDE)]
    rows = [head_rows(head) for head in heads]
    held = [parts(heads_ref, head) for head in heads]
    values = [causal_pairs(held[i][2], g_ref[rows[i], :], mask_ref) for i in range(SIDE)]
    for i in range(SIDE):
        store_pairs((early_ref, late_ref), i, values[i])
    numbers = [
        causal_sum(held[i][3], values[i]) + enters * tn(mem_ref[rows[i], :][:, HEAD:], g_ref[rows[i], :])
        for i in range(SIDE)
    ]
    kept = []
    for i, number_v in enumerate(numbers):
        at = slice(i * HEAD, i * HEAD + HEAD)
        number, inverse, weight = number_ref[at, :], inverse_ref[at, :], weight_ref[at, :]
        d_weight = number_v * inverse
        d_score = weight * (d_weight - jnp.sum(weight * d_weight, axis=0, keepdims=True))
        a = d_score * (inverse * SCALE)
        spread = weight * inverse
        d_total = -(a * number + spread * number_v) * inverse
        a_ref[at, :] = a.astype(BF)
        spread_ref[at, :] = spread.astype(BF)
        d_total_ref[at, :] = d_total.astype(BF)
        kept.append(((a * enters).astype(BF), (spread * enters).astype(BF), d_total * enters))
    for i, (a, spread, d_total) in enumerate(kept):
        d_k = nt(a, held[i][0])
        d_vt = nt(g_ref[rows[i], :], spread)
        pack_ref[rows[i], :] = jnp.concatenate([d_k, d_vt], axis=1).astype(BF)
        sums_ref[rows[i], :] = jnp.broadcast_to(jnp.sum(d_total, axis=1, keepdims=True), (HEAD, 128))
    if own_side:
        pack_totals(pack_ref, sums_ref[...].T[0:8])


def scores_back(own_side, rows, heads, mask, g, mem, saved, packs=(), after=()):
    length, width = heads.shape[2], HEADS * HEAD
    sums = [] if own_side else [shape(F32, width, 128)]
    outs = [shape(BF, SIDE * HEAD, length)] * 3 + pair_shapes(length) + [shape(BF, PACK, 128)] + sums
    return call(
        functools.partial(scores_back_body, own_side),
        (),
        [VM] * (8 + len(packs)),
        [VM] * len(outs),
        outs,
        [pltpu.VMEM((width, 128), F32)] if own_side else [],
        us=3.0,
        after=after,
    )(rows, heads, mask, g, mem, *saved[:3], *packs)


def heads_back_body(own_side, begin, rows_ref, heads_ref, mask_ref, g_ref, mem_ref, a_ref, spread_ref, d_total_ref,
                    v_early, v_late, l_early, l_late, p_early, p_late, d_ref):
    enters = rows_ref[0:1, :]
    count = d_ref.shape[0]
    order = range(begin, begin + count)
    heads = [head_of(own_side, i) for i in order]
    rows = [head_rows(head) for head in heads]
    held = [parts(heads_ref, head) for head in heads]
    ats = [slice(i * HEAD, i * HEAD + HEAD) for i in order]
    steps = [causal_pairs(h[3], a_ref[at, :], mask_ref) for h, at in zip(held, ats)]
    totals = d_total_ref[begin * HEAD : (begin + count) * HEAD, :]
    from_totals = causal_back(mask_pair(mask_ref), totals.T).T
    controls = []
    for i, at in zip(order, ats):
        odd = i % 2 == 1
        controls.append(
            causal_back(load_pairs((p_early, p_late), i), padded(a_ref[at, :], odd))
            + causal_back(load_pairs((v_early, v_late), i), padded(spread_ref[at, :], odd))
        )
    for n in range(count):
        mem_k = mem_ref[rows[n], :][:, :HEAD]
        d_ref[n, :HEAD, :] = causal_sum(held[n][1], steps[n]) + enters * tn(mem_k, a_ref[ats[n], :])
    for n, i in enumerate(order):
        d_ref[n, HEAD : 3 * HEAD, :] = (
            causal_back(steps[n], padded(held[n][0], False))
            + causal_back(load_pairs((l_early, l_late), i), padded(g_ref[rows[n], :], True))
        ).T
    for n in range(0, count, 2):
        two = (controls[n] + controls[n + 1]).T
        for m in range(2):
            d_ref[n + m, 3 * HEAD :, :] = (
                two[m * HEAD : m * HEAD + HEAD] + from_totals[(n + m) * HEAD : (n + m) * HEAD + HEAD]
            )


def heads_back(own_side, begin, count, rows, heads, mask, g, mem, scores, links, pairs, after=()):
    length = heads.shape[2]
    return call(
        functools.partial(heads_back_body, own_side, begin),
        (),
        [VM] * 14,
        VM,
        shape(F32, count, 4 * HEAD, length),
        us=1.0,
        after=after,
    )(rows, heads, mask, g, mem, *scores, *links, *pairs)


def project_back_body(counts, rows_ref, heads_ref, control_ref, partner_ref, far_ref, xnt_ref, *refs):
    d_refs, (proj_ref, keep_ref, send_ref, mem_ref, totals_ref) = refs[: len(counts)], refs[len(counts) :]
    arrived(True, rows_ref, partner_ref, far_ref, mem_ref, totals_ref)
    tail = rows_ref[1:2, :]
    tail_bf = tail.astype(BF)
    places = [(d_ref, n) for d_ref, count in zip(d_refs, counts) for n in range(count)]
    jobs = [(d_ref, n, head_of(i >= SIDE, i % SIDE)) for i, (d_ref, n) in enumerate(places)]
    more = []
    for d_ref, n, head in jobs:
        mem = mem_ref[head_rows(head), :]
        back_k, back_vt = mem[:, :HEAD], mem[:, HEAD:]
        q, k, v, c = parts(heads_ref, head)
        c_tail = c * tail_bf
        more.append((tn(back_k, c_tail), nn(back_vt, c_tail), nn(back_k, k) + tn(back_vt, v)))
    for (d_ref, n, head), (more_k, more_v, more_c) in zip(jobs, more):
        rows = head_rows(head)
        proj_ref[0, rows, :] = d_ref[n, :HEAD, :].astype(BF)
        proj_ref[1, rows, :] = (d_ref[n, HEAD : 2 * HEAD, :] + more_k).astype(BF)
        proj_ref[2, rows, :] = (d_ref[n, 2 * HEAD : 3 * HEAD, :] + more_v).astype(BF)
        d_control = d_ref[n, 3 * HEAD :, :] + tail * (more_c + totals_ref[rows, 0:1])
        proj_ref[3, rows, :] = (d_control * control_ref[rows, :]).astype(BF)
    for own_side in (False, True):
        first = pl.ds(pl.multiple_of(head_of(own_side, 0) * HEAD, SIDE * HEAD), SIDE * HEAD)
        for m in range(4):
            grad = nt(xnt_ref[...], proj_ref[m, first, :]).astype(BF)
            if own_side:
                keep_ref[:, m * SIDE * HEAD : (m + 1) * SIDE * HEAD] = grad
            else:
                send_ref[:, m * SIDE * HEAD : (m + 1) * SIDE * HEAD] = grad


def project_back(rows, heads, ds, control, partner, far, xnt, after=()):
    width, length = xnt.shape
    return call(
        functools.partial(project_back_body, [d.shape[0] for d in ds]),
        (),
        [VM] * (6 + len(ds)),
        [VM] * 3,
        [shape(BF, 4, width, length)] + [shape(BF, width, 4 * SIDE * HEAD)] * 2,
        [pltpu.VMEM((width, 128), BF), pltpu.VMEM((width, 8), F32)],
        us=5.0,
        after=after,
    )(rows, heads, control, partner, far, xnt, *ds)


def norm_back_body(proj_ref, w_ref, n_ref, inv_ref, gain_ref, d_hidden1_ref, norms2_ref, grad_x_ref, norms_ref):
    length, width = n_ref.shape
    dx = nn(w_ref[...], proj_ref[...].reshape(4 * width, length))
    n, d = n_ref[...], dx.T
    sums = [jnp.sum(d * n, axis=0, keepdims=True), jnp.sum(d, axis=0, keepdims=True)]
    rows8 = jnp.concatenate(sums + [norms2_ref[0:6, :]], axis=0)
    norms_ref[...] = jnp.concatenate([rows8, jnp.zeros((120, length), F32)], axis=0).T.astype(BF)
    d_n = d * gain_ref[...]
    grad_x_ref[...] = d_hidden1_ref[...] + (
        d_n
        - jnp.mean(d_n, axis=-1, keepdims=True)
        - n * jnp.mean(d_n * n, axis=-1, keepdims=True)
    ) * inv_ref[:, 0:1]


def norm_back(proj, w, n, inv, gain, d_hidden1, norms2, after=()):
    length, width = n.shape
    return call(
        norm_back_body,
        (),
        [VM] * 7,
        [VM] * 2,
        [shape(F32, length, width), shape(BF, width, 128)],
        us=1e3,
        after=after,
    )(proj, w, n, inv, gain, d_hidden1, norms2)


def bit_axis(bit):
    return ("seq", 1) if bit == 0 else ("dp", 1 << (bit - 1))


def my_bit(bit):
    axis, step = bit_axis(bit)
    return (lax.axis_index(axis) // step) % 2


def send_across(a, bits):
    seqs, dps = lax.axis_size("seq"), lax.axis_size("dp")
    flip = sum(1 << bit for bit in bits)
    return lax.ppermute(a, ("dp", "seq"), [(i, i ^ flip) for i in range(seqs * dps)])


def place_of(t, places, values):
    index, rest, bit = 0, t, 0
    fixed = dict(zip(places, values))
    while rest or fixed:
        if bit in fixed:
            index = index + fixed.pop(bit) * (1 << bit)
        else:
            index = index + ((rest & 1) << bit)
            rest >>= 1
        bit += 1
    return index


def stage_body(plan, *refs):
    refs = list(refs)
    ins = [
        [[refs.pop(0).at[:, :, pl.ds(*piece)] for piece in pieces] for pieces in arrays] for arrays, _ in plan
    ]
    for (arrays, split), sources in zip(plan, ins):
        outs = [refs.pop(0) for _ in range(1 << len(split))]
        blocks = outs[0].shape[0]
        places = [place for _, place in split]
        mine = [my_bit(bit) for bit, _ in split]
        for pattern, out in enumerate(outs):
            values = [
                (1 - m) if (pattern >> n) & 1 else m for n, m in enumerate(mine)
            ]
            for t in range(blocks):
                at = place_of(t, places, values)
                rows = [
                    jnp.concatenate([p[at] for p in pieces], axis=1) if len(pieces) > 1 else pieces[0][at]
                    for pieces in sources
                ]
                if len(rows) == 1 or (len(rows) == 2 and out.dtype == BF):
                    total = sum(rows[1:], rows[0])
                else:
                    total = sum(row.astype(F32) for row in rows)
                out[t] = total.astype(out.dtype)


def stage(groups, after=(), dtype=BF, us=1.0):
    plan, operands, out_shape = [], [], []
    for arrays, split in groups:
        for pieces in arrays:
            operands += [array for array, _, _ in pieces]
        (array, _, _), width = arrays[0][0], sum(p[2] for p in arrays[0])
        plan.append(([[(first, count) for _, first, count in pieces] for pieces in arrays], split))
        out_shape += [shape(dtype, array.shape[0] >> len(split), array.shape[1], width)] * (1 << len(split))
    outs = list(
        call(functools.partial(stage_body, plan), (), [VM] * len(operands), [VM] * len(out_shape), out_shape, us=us, after=after)(
            *operands
        )
    )
    return [[outs.pop(0) for _ in range(1 << len(split))] for _, split in groups]


def all_of(a):
    return [(a, 0, a.shape[2])]


def patterns(bits):
    return [[b for n, b in enumerate(bits) if (p >> n) & 1] for p in range(1, 1 << len(bits))]


def last_body(late_count, columns, *refs):
    *ins, out_ref = refs
    sums = [
        sum(ref[0].astype(F32) for ref in ins[:late_count]),
        *(sum(ref[0][:, at].astype(F32) for ref in ins[late_count:]) for at in columns),
    ]
    out_ref[...] = jnp.concatenate(sums, axis=1).astype(BF)


def last(late, early, columns):
    rows = late[0].shape[1]
    width = late[0].shape[2] + sum(at.stop - at.start for at in columns)
    return call(
        functools.partial(last_body, len(late), columns),
        (),
        [VM] * (len(late) + len(early)),
        VM,
        shape(BF, rows, width),
    )(*late, *early)


def join_body(up_at, down_at, own_ref, other_ref, a_ref, b_ref,
              grad_in_ref, grad_out_ref, grad_up_ref, grad_down_ref, *norm_refs):
    second = lax.axis_index("ffn") == 1
    own, other = own_ref[...].astype(F32), other_ref[...].astype(F32)
    for f in range(2):
        keep_own = second if f else jnp.logical_not(second)
        half = jnp.where(keep_own, own, other)
        for m in range(4):
            grad_in_ref[:, m * 512 + f * 256 : m * 512 + f * 256 + 256] = half[:, m * 256 : m * 256 + 256]
        grad_out_ref[:, f * 256 : f * 256 + 256] = half[:, 1152:]
    for at, ref in ((up_at, grad_up_ref), (down_at, grad_down_ref)):
        ref[...] = a_ref[0][:, at].astype(F32) + b_ref[0][:, at].astype(F32)
    norms = (own[:, 1024:1152] + other[:, 1024:1152]).T
    for n, ref in enumerate(norm_refs):
        ref[...] = norms[n]


def join(own, other, early, up_at, down_at):
    rows = own.shape[0]
    half = up_at.stop - up_at.start
    return call(
        functools.partial(join_body, up_at, down_at),
        (),
        [VM] * 4,
        [VM] * 8,
        [shape(F32, rows, n) for n in (2048, 512, half, half)] + [shape(F32, rows)] * 4,
    )(own, other, *early)


def on_device(tokens, doc_starts, norm1_gain, norm1_bias, in_weight, out_weight,
              norm2_gain, norm2_bias, up_own, down_own, output_cotangent):
    x, cotangent, starts = tokens[0], output_cotangent[0], doc_starts
    length, width = x.shape
    owners = lax.axis_size("dp") * lax.axis_size("seq")
    bits = owners.bit_length() - 1
    row = lambda a: a.reshape(1, width)
    blocked = lambda a: a.reshape(owners, width // owners, a.shape[1])

    heads, raw, xn, own, mask, rows, n1, inv1 = project(
        x, row(norm1_gain), row(norm1_bias), in_weight, starts)
    up_other, down_other = swap(up_own, "ffn", 1), swap(down_own, "ffn", 1)
    partner = swap(own, "ffn", 1)
    number_o, total_o, *pairs_other = local_sums(False, heads, mask)
    both = combine(False, rows, own, partner, after=[number_o])
    far = swap(both, "seq", 1)
    number, total, *pairs_own = local_sums(True, heads, mask, after=[both])
    d_hidden_other, d_hidden_own, cott, control, xnt = prepare(
        cotangent, down_own, down_other, raw, xn, after=[number])
    mixed, memory, saved_other, saved_own = mix(
        rows, heads, mask, partner, far, (number_o, total_o), (number, total), after=[cott])
    gup_send, gdown_send, *saved = feed_other(
        x, mixed, cott, d_hidden_other, out_weight, row(norm2_gain), row(norm2_bias), up_other, down_other)
    gup_got, gdown_got = swap(gup_send, "ffn", 1), swap(gdown_send, "ffn", 1)
    (output, d_hidden1, g, out_send, out_keep, norms2, gup_own, gdown_own) = feed_own(
        saved, cott, d_hidden_own, mixed, cotangent, out_weight, row(norm2_gain), up_own, down_own)
    out_got = swap(out_send, "ffn", 1)

    out_half = width // 4
    ups, downs, outs = [
        [blocked(a) for a in pair]
        for pair in ((gup_own, gup_got), (gdown_own, gdown_got), (out_keep, out_got))
    ]
    groups = [
        [[*all_of(a), (o, 0, out_half)] for a, o in zip(ups, outs)],
        [[*all_of(a), (o, out_half, out_half)] for a, o in zip(downs, outs)],
    ]
    orders = [[1, 2], [2, 1]]
    left = [list(range(bits)) for _ in groups]

    def advance(groups, n, after):
        if n >= 2:
            if n == 2:
                groups = [[pieces_a + pieces_b for pieces_a, pieces_b in zip(*groups)]]
            bits_now = left[0][-1:]
            splits = [[(bits_now[0], len(left[0]) - 1)]]
            for rest in left:
                rest.pop()
        else:
            bits_now = [order[n] for order in orders]
            splits = [[(bit, rest.index(bit))] for bit, rest in zip(bits_now, left)]
            for bit, rest in zip(bits_now, left):
                rest.remove(bit)
        outs = stage(list(zip(groups, splits)), after=after)
        got = [send_across(sent, [bit]) for (_, sent), bit in zip(outs, bits_now)]
        sent = [s for _, s in outs]
        return [[all_of(kept), all_of(r)] for (kept, _), r in zip(outs, got)], sent

    back = (rows, heads, mask, g, memory)
    *scores_other, pack, sums = scores_back(False, *back, saved_other)
    groups, sent = advance(groups, 0, [pack])
    *scores_own, d_own = scores_back(True, *back, saved_own, packs=(pack, sums), after=sent)
    d_partner = swap(d_own, "ffn", 1)
    other_side, own_side = (scores_other, saved_other[3:], pairs_other), (scores_own, saved_own[3:], pairs_own)
    ds = []
    if SPLIT:
        ds.append(heads_back(False, 0, SPLIT, *back, *other_side, after=[d_own]))
    d_both = combine(True, rows, d_own, d_partner, after=ds)
    d_far = swap(d_both, "seq", 1)
    ds.append(heads_back(False, SPLIT, SIDE - SPLIT, *back, *other_side, after=[d_both]))
    ds.append(heads_back(True, 0, SIDE, *back, *own_side, after=ds[-1:]))
    proj, in_keep, in_send = project_back(rows, heads, ds, control, d_partner, d_far, xnt)
    in_got = swap(in_send, "ffn", 1)
    groups, sent = advance(groups, 1, [in_send])
    grad_tokens, norms = norm_back(
        proj, in_weight, n1, inv1, row(norm1_gain), d_hidden1, norms2, after=sent)

    late = [
        all_of(blocked(in_keep)) + all_of(blocked(norms)),
        all_of(blocked(in_got)) + all_of(jnp.zeros_like(blocked(norms))),
    ]
    rest = list(range(bits))
    stages = list(range(2, bits))
    while rest:
        now = rest[:2]
        split = [(b, rest.index(b)) for b in now]
        rest = rest[2:]
        (kept, *sent), = stage([(late, split)])
        late = [all_of(kept)] + [all_of(send_across(s, p)) for s, p in zip(sent, patterns(now))]
        token = [kept]
        while stages:
            groups, token = advance(groups, stages.pop(0), token)
            if rest:
                break
    early = [arrays[0][0] for arrays in groups[0]]
    half = gup_own.shape[1]
    down_at = half + out_half
    outs_at = [slice(half, down_at), slice(down_at + half, down_at + half + out_half)]
    (total,), = stage([(late, [])], us=1e3)
    final = last([total], early, outs_at)
    grad_in, grad_out, grad_up, grad_down, *norms = join(
        final, swap(final, "ffn", 1), early, slice(0, half), slice(down_at, down_at + half))
    return (output[None], grad_tokens[None], grad_in, grad_out, grad_up, grad_down, *norms)


def solution(mesh):
    rows = P("dp", ("seq", "ffn"), None)
    owned = P(("dp", "seq"))
    return jax.shard_map(
        on_device,
        mesh=mesh,
        in_specs=(
            rows, P("dp", None), P(), P(), P(), P(), P(), P(),
            P(None, "ffn"), P(None, "ffn"), rows,
        ),
        out_specs=(
            rows, rows, P(("dp", "seq"), None), P(("dp", "seq"), None),
            P(("dp", "seq"), "ffn"), P(("dp", "seq"), "ffn"),
            owned, owned, owned, owned,
        ),
        check_vma=False,
    )
```

```python
import functools

import jax
import jax.numpy as jnp
from jax import lax
from jax.experimental import pallas as pl
from jax.experimental.pallas import tpu as pltpu
from jax.sharding import PartitionSpec as P

HEADS = 8
HEAD = 64
EPSILON = 1e-05
BF = jnp.bfloat16
F32 = jnp.float32
GELU_A = 0.7978845608028654
GELU_B = 0.044715
SCALE = HEAD**-0.5
K1_VMEM = 48
SPLIT = 2
SIDE = HEADS // 2
PACK = HEADS * HEAD + 64


def nn(a, b):
    return lax.dot_general(a, b, (((1,), (0,)), ((), ())), preferred_element_type=F32)


def nt(a, b):
    return lax.dot_general(a, b, (((1,), (1,)), ((), ())), preferred_element_type=F32)


def tn(a, b):
    return lax.dot_general(a, b, (((0,), (0,)), ((), ())), preferred_element_type=F32)


def swap(a, axis, bit):
    size = lax.axis_size(axis)
    return lax.ppermute(a, axis, [(i, i ^ bit) for i in range(size)])


ANY = pl.BlockSpec(memory_space=pl.ANY)


def call(body, grid, in_specs, out_specs, out_shape, scratch=(), us=1.0, after=(), vmem=20):
    count = len(in_specs)

    def run(*refs):
        body(*refs[:count], *refs[count + len(after) :])

    def start(*operands):
        return pl.pallas_call(
            run,
            grid=grid,
            in_specs=list(in_specs) + [ANY] * len(after),
            out_specs=out_specs,
            out_shape=out_shape,
            scratch_shapes=list(scratch),
            cost_estimate=pl.CostEstimate(flops=int(us * 1e7), bytes_accessed=2**13, transcendentals=0),
            compiler_params=pltpu.CompilerParams(vmem_limit_bytes=vmem * 2**20),
        )(*operands, *after)

    return start


def whole(shape):
    return pl.BlockSpec(shape, lambda *_: (0,) * len(shape))


VM = pl.BlockSpec(memory_space=pltpu.MemorySpace.VMEM)


def shape(dtype, *dims):
    return jax.ShapeDtypeStruct(dims, dtype)


SMEM = pl.BlockSpec(memory_space=pltpu.SMEM)


def shard_of():
    return lax.axis_index("seq") * 2 + lax.axis_index("ffn")


def doc_begin_row(starts_ref, length):
    begin = shard_of() * length
    place = lax.broadcasted_iota(jnp.int32, (1, length), 1)
    row = jnp.full((1, length), -(2**30), jnp.int32)
    for j in range(starts_ref.shape[1]):
        s = starts_ref[0, j] - begin
        row = jnp.where(place >= s, jnp.maximum(row, s), row)
    return row


def passes(starts_ref, which, length):
    hit = jnp.int32(0)
    for j in range(starts_ref.shape[1]):
        s = starts_ref[0, j]
        hit = hit | ((s >= which * length) & (s < which * length + length)).astype(jnp.int32)
    return 1.0 - hit.astype(F32)


def visible(doc_row, length):
    i = lax.broadcasted_iota(jnp.int32, (length, length), 0)
    t = lax.broadcasted_iota(jnp.int32, (length, length), 1)
    return jnp.where((i <= t) & (i >= doc_row), 1.0, 0.0).astype(BF)


def tail_row(doc_row, length):
    place = lax.broadcasted_iota(jnp.int32, (1, length), 1)
    last = doc_row[:, length - 1 :]
    return jnp.where(place >= last, 1.0, 0.0)


def pack_totals(pack_ref, totals8):
    base = HEADS * HEAD
    hi = totals8.astype(BF)
    lo = (totals8 - hi.astype(F32)).astype(BF)
    for a in range(4):
        cols = slice(128 * a, 128 * a + 128)
        pack_ref[base + 16 * a : base + 16 * a + 16, :] = jnp.concatenate(
            [hi[:, cols], lo[:, cols]], axis=0
        )


def unpack(rows, totals8_of):
    base = HEADS * HEAD
    out = []
    for a in range(4):
        block = totals8_of(slice(base + 16 * a, base + 16 * a + 16))
        out.append(block[:8] + block[8:])
    return rows(slice(0, base)), jnp.concatenate(out, axis=1)


def combine_body(backward, rows_ref, own_ref, partner_ref, out_ref):
    is_first = (lax.axis_index("ffn") == 0).astype(F32)
    base = HEADS * HEAD
    if backward:
        p = rows_ref[2:3, :128]
        own_by, partner_by = is_first + (1 - is_first) * p, is_first * p + (1 - is_first)
    else:
        p = rows_ref[3:4, :128]
        own_by, partner_by = is_first * p + (1 - is_first), is_first + (1 - is_first) * p

    def sum_of(at):
        return own_ref[at, :].astype(F32) * own_by + partner_ref[at, :].astype(F32) * partner_by

    memory, totals8 = unpack(sum_of, sum_of)
    out_ref[:base, :] = memory.astype(BF)
    pack_totals(out_ref, totals8)


def combine(backward, rows, own, partner, after=()):
    return call(
        functools.partial(combine_body, backward),
        (),
        [VM] * 3,
        VM,
        shape(BF, PACK, 128),
        after=after,
    )(rows, own, partner)


def arrived(backward, rows_ref, partner_ref, far_ref, mem_ref, totals_ref):
    is_first = (lax.axis_index("ffn") == 0).astype(F32)
    if backward:
        p = rows_ref[3:4, :128]
        far_by, partner_by = is_first * p + (1 - is_first), is_first
        valid = lax.axis_index("seq") == 0
    else:
        p = rows_ref[2:3, :128]
        far_by, partner_by = is_first + (1 - is_first) * p, 1 - is_first
        valid = lax.axis_index("seq") == 1

    def sum_of(at):
        far = jnp.where(valid, far_ref[at, :].astype(F32), 0.0)
        return far * far_by + partner_ref[at, :].astype(F32) * partner_by

    memory, totals8 = unpack(sum_of, sum_of)
    mem_ref[...] = memory.astype(BF)
    totals_ref[...] = totals8.T


def head_of(own_side, h):
    ffn = lax.axis_index("ffn")
    return (ffn if own_side else 1 - ffn) * SIDE + h


def head_rows(head):
    return pl.ds(pl.multiple_of(head * HEAD, HEAD), HEAD)


def project_body(x_hbm, gain_hbm, bias_hbm, w_hbm, starts_ref,
                 heads_ref, raw_ref, xn_ref, pack_ref, mask_ref, rows_ref, n_ref, inv_ref,
                 x_ref, gain_ref, bias_ref, w_ref, sems):
    length, width = x_ref.shape
    copies = [
        pltpu.make_async_copy(x_hbm, x_ref, sems.at[0]),
        pltpu.make_async_copy(gain_hbm, gain_ref, sems.at[1]),
        pltpu.make_async_copy(bias_hbm, bias_ref, sems.at[2]),
    ]
    columns = [
        pltpu.make_async_copy(w_hbm.at[:, pl.ds((j + 1) * width, width)], w_ref.at[j], sems.at[3 + j])
        for j in range(3)
    ]
    for copy in copies + columns:
        copy.start()
    doc_row = doc_begin_row(starts_ref, length)
    tail = tail_row(doc_row, length)
    first = 2 * lax.axis_index("seq")
    rows = [jnp.where(doc_row < 0, 1.0, 0.0), tail] + [
        jnp.full((1, length), passes(starts_ref, which, length)) for which in (first, first + 1)
    ]
    rows_ref[...] = jnp.concatenate(rows + rows, axis=0)
    mask_ref[...] = visible(doc_row, length)
    for copy in copies:
        copy.wait()
    x = x_ref[...].astype(F32)
    mean = jnp.mean(x, axis=-1, keepdims=True)
    centered = x - mean
    inverse = lax.rsqrt(jnp.mean(centered * centered, axis=-1, keepdims=True) + EPSILON)
    n = centered * inverse
    n_ref[...] = n
    inv_ref[...] = jnp.broadcast_to(inverse, inv_ref.shape)
    xn = (n * gain_ref[...] + bias_ref[...]).astype(BF)
    xn_ref[...] = xn
    projected = []
    for j in range(3):
        columns[j].wait()
        projected.append(nn(xn, w_ref[j]))
    raw_ref[...] = projected[2]
    c = jnp.exp(projected[2]).astype(BF).T
    for j in range(2):
        t = projected[j].astype(BF).T
        for h in range(HEADS):
            heads_ref[h, j * HEAD : j * HEAD + HEAD, :] = t[h * HEAD : h * HEAD + HEAD]
    c_tail = c * tail.astype(BF)
    for h in range(HEADS):
        rows = slice(h * HEAD, h * HEAD + HEAD)
        heads_ref[h, 2 * HEAD :, :] = c[rows]
        mem_k = nt(c_tail[rows], heads_ref[h, :HEAD, :])
        mem_vt = nt(heads_ref[h, HEAD : 2 * HEAD, :], c_tail[rows])
        pack_ref[rows, :] = jnp.concatenate([mem_k, mem_vt], axis=1).astype(BF)
    tail8 = jnp.broadcast_to(tail, (8, length)).astype(BF)
    pack_totals(pack_ref, nt(tail8, c))


def project(x, gain, bias, w, starts):
    length, width = x.shape
    hbm = pl.BlockSpec(memory_space=pltpu.MemorySpace.HBM)
    pin = lambda a: pltpu.with_memory_space_constraint(a, pltpu.HBM)
    return call(
        project_body,
        (),
        [hbm, hbm, hbm, hbm, SMEM],
        [VM] * 8,
        [
            shape(BF, HEADS, 3 * HEAD, length), shape(F32, length, width), shape(BF, length, width),
            shape(BF, PACK, 128), shape(BF, length, length), shape(F32, 8, length),
            shape(F32, length, width), shape(F32, length, 128),
        ],
        [
            pltpu.VMEM((length, width), BF), pltpu.VMEM((1, width), F32), pltpu.VMEM((1, width), F32),
            pltpu.VMEM((3, width, width), BF), pltpu.SemaphoreType.DMA((6,)),
        ],
        us=4.3,
        vmem=K1_VMEM,
    )(*(pin(a) for a in (x, gain, bias, w, starts)))


def query_body(xn_ref, w_ref, q_ref):
    t = nn(xn_ref[...], w_ref[:, : xn_ref.shape[1]]).astype(BF).T
    for h in range(HEADS):
        q_ref[h] = t[h * HEAD : h * HEAD + HEAD]


def query(xn, w, after=()):
    return call(query_body, (), [VM] * 2, VM, shape(BF, HEADS, HEAD, xn.shape[0]), us=0.5, after=after)(xn, w)


def parts(refs, head):
    q_ref, heads_ref = refs
    return [q_ref[head]] + [heads_ref[head, j * HEAD : j * HEAD + HEAD, :] for j in range(3)]


def mask_pair(mask_ref):
    half = mask_ref.shape[0] // 2
    return mask_ref[:half, :half], mask_ref[:, half:]


def causal_pairs(left, right, mask_ref):
    half = mask_ref.shape[0] // 2
    early, late = mask_pair(mask_ref)
    rows = left.T
    return nn(rows[:half], right[:, :half]).astype(BF) * early, nn(rows, right[:, half:]).astype(BF) * late


def causal_sum(left, pairs):
    a, b = pairs
    half = a.shape[0]
    return jnp.concatenate([nn(left[:, :half], a), nn(left, b)], axis=1)


def causal_back(pairs, right):
    a, b = pairs
    half = a.shape[0]
    late = nn(b, right[half:])
    return jnp.concatenate([late[:half] + nn(a, right[:half]), late[half:]], axis=0)


def padded(rows, second):
    zero = jnp.zeros_like(rows)
    return jnp.concatenate([zero, rows] if second else [rows, zero], axis=0).T


def pair_shapes(length, count=SIDE):
    half = length // 2
    return [shape(BF, count, half, half), shape(BF, count, length, half)]


def store_pairs(refs, i, pairs):
    refs[0][i], refs[1][i] = pairs


def load_pairs(refs, i):
    return refs[0][i], refs[1][i]


def local_body(own_side, q_ref, heads_ref, mask_ref, number_ref, total_ref, *pair_refs):
    held = [parts((q_ref, heads_ref), head_of(own_side, i)) for i in range(SIDE)]
    pairs = [causal_pairs(k, q, mask_ref) for q, k, v, c in held]
    for i in range(SIDE):
        store_pairs(pair_refs, i, pairs[i])
    c = jnp.concatenate([h[3] for h in held], axis=0)
    total_ref[...] = causal_sum(c, mask_pair(mask_ref))
    for i in range(SIDE):
        number_ref[i * HEAD : i * HEAD + HEAD, :] = causal_sum(held[i][3], pairs[i])


def local_sums(own_side, heads, mask, after=()):
    length = heads[0].shape[2]
    return call(
        functools.partial(local_body, own_side),
        (),
        [VM] * 3,
        [VM] * 4,
        [shape(F32, SIDE * HEAD, length)] * 2 + pair_shapes(length),
        us=3.0,
        after=after,
    )(*heads, mask)


def mix_body(rows_ref, q_ref, heads_ref, mask_ref, partner_ref, far_ref, *refs):
    refs = list(refs)
    take = lambda n: [refs.pop(0) for _ in range(n)]
    ins = [take(2), take(2)]
    mixed_ref, mem_ref = take(2)
    outs = [take(5), take(5)]
    (totals_ref,) = refs
    arrived(False, rows_ref, partner_ref, far_ref, mem_ref, totals_ref)
    enters = rows_ref[0:1, :]
    jobs = [(own_side, i) for own_side in (False, True) for i in range(SIDE)]
    spreads, links = [], []
    for own_side, i in jobs:
        number_in, total_in = ins[own_side]
        number_ref, inverse_ref, weight_ref, *_ = outs[own_side]
        head, at = head_of(own_side, i), slice(i * HEAD, i * HEAD + HEAD)
        mem_k = mem_ref[head_rows(head), :][:, :HEAD]
        number = number_in[at, :] + enters * nn(mem_k, parts((q_ref, heads_ref), head)[0])
        inverse = 1.0 / (total_in[at, :] + enters * totals_ref[head_rows(head), 0:1])
        score = number * (inverse * SCALE)
        e = jnp.exp(score - jnp.max(score, axis=0, keepdims=True))
        weight = e * (1.0 / jnp.sum(e, axis=0, keepdims=True))
        number_ref[at, :] = number
        inverse_ref[at, :] = inverse
        weight_ref[at, :] = weight
        spreads.append((weight * inverse).astype(BF))
    for (own_side, i), spread in zip(jobs, spreads):
        links.append(causal_pairs(parts((q_ref, heads_ref), head_of(own_side, i))[3], spread, mask_ref))
        store_pairs(outs[own_side][3:], i, links[-1])
    for (own_side, i), spread, link in zip(jobs, spreads, links):
        head = head_of(own_side, i)
        mem_vt = mem_ref[head_rows(head), :][:, HEAD:]
        mixed = causal_sum(parts((q_ref, heads_ref), head)[2], link) + enters * nn(mem_vt, spread)
        mixed_ref[head_rows(head), :] = mixed.astype(BF)


def mix(rows, heads, mask, partner, far, local_other, local_own, after=()):
    length, width = heads[0].shape[2], HEADS * HEAD
    side = [shape(F32, SIDE * HEAD, length)] * 3 + pair_shapes(length)
    mixed, mem, *rest = call(
        mix_body,
        (),
        [VM] * 10,
        [VM] * 12,
        [shape(BF, width, length), shape(BF, width, 128)] + side + side,
        [pltpu.VMEM((width, 8), F32)],
        us=4.0,
        after=after,
    )(rows, *heads, mask, partner, far, *local_other, *local_own)
    return mixed, mem, rest[:5], rest[5:]


def prepare_body(cot_ref, down_ref, down_other_ref, raw_ref, xn_ref, other_ref, own_ref, cott_ref, control_ref, xnt_ref):
    cot = cot_ref[...]
    other_ref[...] = nn(cot, down_other_ref[...])
    own_ref[...] = nn(cot, down_ref[...])
    cott_ref[...] = cot.T
    xnt_ref[...] = xn_ref[...].T
    control_ref[...] = jnp.exp(raw_ref[...]).T


def prepare(cotangent, down, down_other, raw, xn, after=()):
    length, width = cotangent.shape
    return call(
        prepare_body,
        (),
        [VM] * 5,
        [VM] * 5,
        [shape(F32, length, down.shape[1])] * 2
        + [shape(BF, width, length), shape(F32, width, length), shape(BF, width, length)],
        us=2.0,
        after=after,
    )(cotangent, down, down_other, raw, xn)


def activations(xn, d_hidden_ref, up_ref):
    cols = [slice(j, j + 512) for j in range(0, up_ref.shape[1], 512)]
    pres = [nn(xn, up_ref[:, at]) for at in cols]
    hidden, grad_pre = [], []
    for pre, at in zip(pres, cols):
        v2 = pre * pre
        h = 0.5 + 0.5 * jnp.tanh(pre * (GELU_A + (GELU_A * GELU_B) * v2))
        act = pre * h
        hidden.append(act.astype(BF))
        slope = h + act * (1.0 - h) * (2.0 * GELU_A + (6.0 * GELU_A * GELU_B) * v2)
        grad_pre.append((d_hidden_ref[:, at] * slope).astype(BF))
    return jnp.concatenate(hidden, axis=1), jnp.concatenate(grad_pre, axis=1)


def feed_other_body(x_ref, mixed_ref, cott_ref, d_hidden_ref, w_out_ref, gain_ref, bias_ref, up_ref, down_ref,
                    gup_ref, gdown_ref, hidden1_ref, n_ref, inv_ref, xn_ref, xnt_ref,
                    part_ref, d_ref):
    hidden1 = x_ref[...].astype(F32) + tn(mixed_ref[...], w_out_ref[...])
    hidden1_ref[...] = hidden1
    mean = jnp.mean(hidden1, axis=-1, keepdims=True)
    centered = hidden1 - mean
    inverse = lax.rsqrt(jnp.mean(centered * centered, axis=-1, keepdims=True) + EPSILON)
    n = centered * inverse
    n_ref[...] = n
    inv_ref[...] = jnp.broadcast_to(inverse, inv_ref.shape)
    xn = (n * gain_ref[...] + bias_ref[...]).astype(BF)
    xnt = xn.T
    xn_ref[...] = xn
    xnt_ref[...] = xnt
    hidden, grad_pre = activations(xn, d_hidden_ref, up_ref)
    gdown_ref[...] = nn(cott_ref[...], hidden).astype(BF)
    gup_ref[...] = nn(xnt, grad_pre).astype(BF)
    part_ref[...] = nt(hidden, down_ref[...])
    d_ref[...] = nt(grad_pre, up_ref[...])


def feed_own_body(hidden1_ref, n_ref, inv_ref, xn_ref, xnt_ref, part_ref, d_in_ref, cott_ref, d_hidden_ref,
                  mixed_ref, cot_ref, w_out_ref, gain_ref, up_ref, down_ref,
                  output_ref, d_hidden1_ref, g_ref, out_send_ref, out_keep_ref, norms_ref,
                  gup_ref, gdown_ref):
    hidden, grad_pre = activations(xn_ref[...], d_hidden_ref, up_ref)
    dx, n = d_in_ref[...] + nt(grad_pre, up_ref[...]), n_ref[...]
    norms_ref[...] = jnp.concatenate(
        [jnp.sum(dx * n, axis=0, keepdims=True), jnp.sum(dx, axis=0, keepdims=True)] * 4, axis=0
    )
    output_ref[...] = (hidden1_ref[...] + (part_ref[...] + nt(hidden, down_ref[...]))).astype(BF)
    gdown_ref[...] = nn(cott_ref[...], hidden).astype(BF)
    d_n = dx * gain_ref[...]
    d_in = (
        d_n
        - jnp.mean(d_n, axis=-1, keepdims=True)
        - n * jnp.mean(d_n * n, axis=-1, keepdims=True)
    ) * inv_ref[:, 0:1]
    d_hidden1 = cot_ref[...].astype(F32) + d_in
    d_hidden1_ref[...] = d_hidden1
    d_branch = d_hidden1.astype(BF)
    gup_ref[...] = nn(xnt_ref[...], grad_pre).astype(BF)
    g_ref[...] = nt(w_out_ref[...], d_branch).astype(BF)
    grad_out = nn(mixed_ref[...], d_branch).astype(BF)
    half = grad_out.shape[1] // 2
    second = lax.axis_index("ffn") == 1
    out_keep_ref[...] = jnp.where(second, grad_out[:, half:], grad_out[:, :half])
    out_send_ref[...] = jnp.where(second, grad_out[:, :half], grad_out[:, half:])


def feed_other(x, mixed, cott, d_hidden, w_out, gain, bias, up, down):
    length, width = x.shape
    half, sq = shape(BF, *up.shape), lambda dt: shape(dt, length, width)
    return call(
        feed_other_body,
        (),
        [VM] * 9,
        [VM] * 9,
        [half, half, sq(F32), sq(F32), shape(F32, length, 128), sq(BF), sq(BF), sq(F32), sq(F32)],
        us=6.0,
    )(x, mixed, cott, d_hidden, w_out, gain, bias, up, down)


def feed_own(saved, cott, d_hidden, mixed, cotangent, w_out, gain, up, down, after=()):
    length, width = mixed.shape
    half, sq = shape(BF, *up.shape), lambda dt: shape(dt, length, width)
    return call(
        feed_own_body,
        (),
        [VM] * 15,
        [VM] * 8,
        [sq(BF), sq(F32), sq(BF)] + [shape(BF, width, width // 2)] * 2 + [shape(F32, 8, width), half, half],
        us=6.0,
        after=after,
    )(*saved, cott, d_hidden, mixed, cotangent, w_out, gain, up, down)


def scores_back_body(own_side, rows_ref, q_ref, heads_ref, mask_ref, g_ref, mem_ref, number_ref, inverse_ref, weight_ref,
                     *refs):
    if own_side:
        pack_in, sums_in, a_ref, spread_ref, d_total_ref, early_ref, late_ref, pack_ref, sums_ref = refs
        pack_ref[...] = pack_in[...]
        sums_ref[...] = sums_in[...]
    else:
        a_ref, spread_ref, d_total_ref, early_ref, late_ref, pack_ref, sums_ref = refs
    enters = rows_ref[0:1, :]
    heads = [head_of(own_side, i) for i in range(SIDE)]
    rows = [head_rows(head) for head in heads]
    held = [parts((q_ref, heads_ref), head) for head in heads]
    values = [causal_pairs(held[i][2], g_ref[rows[i], :], mask_ref) for i in range(SIDE)]
    for i in range(SIDE):
        store_pairs((early_ref, late_ref), i, values[i])
    numbers = [
        causal_sum(held[i][3], values[i]) + enters * tn(mem_ref[rows[i], :][:, HEAD:], g_ref[rows[i], :])
        for i in range(SIDE)
    ]
    kept = []
    for i, number_v in enumerate(numbers):
        at = slice(i * HEAD, i * HEAD + HEAD)
        number, inverse, weight = number_ref[at, :], inverse_ref[at, :], weight_ref[at, :]
        d_weight = number_v * inverse
        d_score = weight * (d_weight - jnp.sum(weight * d_weight, axis=0, keepdims=True))
        a = d_score * (inverse * SCALE)
        spread = weight * inverse
        d_total = -(a * number + spread * number_v) * inverse
        a_ref[at, :] = a.astype(BF)
        spread_ref[at, :] = spread.astype(BF)
        d_total_ref[at, :] = d_total.astype(BF)
        kept.append(((a * enters).astype(BF), (spread * enters).astype(BF), d_total * enters))
    for i, (a, spread, d_total) in enumerate(kept):
        d_k = nt(a, held[i][0])
        d_vt = nt(g_ref[rows[i], :], spread)
        pack_ref[rows[i], :] = jnp.concatenate([d_k, d_vt], axis=1).astype(BF)
        sums_ref[rows[i], :] = jnp.broadcast_to(jnp.sum(d_total, axis=1, keepdims=True), (HEAD, 128))
    if own_side:
        pack_totals(pack_ref, sums_ref[...].T[0:8])


def scores_back(own_side, rows, heads, mask, g, mem, saved, packs=(), after=()):
    length, width = heads[0].shape[2], HEADS * HEAD
    sums = [] if own_side else [shape(F32, width, 128)]
    outs = [shape(BF, SIDE * HEAD, length)] * 3 + pair_shapes(length) + [shape(BF, PACK, 128)] + sums
    return call(
        functools.partial(scores_back_body, own_side),
        (),
        [VM] * (9 + len(packs)),
        [VM] * len(outs),
        outs,
        [pltpu.VMEM((width, 128), F32)] if own_side else [],
        us=3.0,
        after=after,
    )(rows, *heads, mask, g, mem, *saved[:3], *packs)


def heads_back_body(own_side, begin, rows_ref, q_ref, heads_ref, mask_ref, g_ref, mem_ref, a_ref, spread_ref, d_total_ref,
                    v_early, v_late, l_early, l_late, p_early, p_late, d_ref):
    enters = rows_ref[0:1, :]
    count = d_ref.shape[0]
    order = range(begin, begin + count)
    heads = [head_of(own_side, i) for i in order]
    rows = [head_rows(head) for head in heads]
    held = [parts((q_ref, heads_ref), head) for head in heads]
    ats = [slice(i * HEAD, i * HEAD + HEAD) for i in order]
    steps = [causal_pairs(h[3], a_ref[at, :], mask_ref) for h, at in zip(held, ats)]
    totals = d_total_ref[begin * HEAD : (begin + count) * HEAD, :]
    from_totals = causal_back(mask_pair(mask_ref), totals.T).T
    controls = []
    for i, at in zip(order, ats):
        odd = i % 2 == 1
        controls.append(
            causal_back(load_pairs((p_early, p_late), i), padded(a_ref[at, :], odd))
            + causal_back(load_pairs((v_early, v_late), i), padded(spread_ref[at, :], odd))
        )
    for n in range(count):
        mem_k = mem_ref[rows[n], :][:, :HEAD]
        d_ref[n, :HEAD, :] = causal_sum(held[n][1], steps[n]) + enters * tn(mem_k, a_ref[ats[n], :])
    for n, i in enumerate(order):
        d_ref[n, HEAD : 3 * HEAD, :] = (
            causal_back(steps[n], padded(held[n][0], False))
            + causal_back(load_pairs((l_early, l_late), i), padded(g_ref[rows[n], :], True))
        ).T
    for n in range(0, count, 2):
        two = (controls[n] + controls[n + 1]).T
        for m in range(2):
            d_ref[n + m, 3 * HEAD :, :] = (
                two[m * HEAD : m * HEAD + HEAD] + from_totals[(n + m) * HEAD : (n + m) * HEAD + HEAD]
            )


def heads_back(own_side, begin, count, rows, heads, mask, g, mem, scores, links, pairs, after=()):
    length = heads[0].shape[2]
    return call(
        functools.partial(heads_back_body, own_side, begin),
        (),
        [VM] * 15,
        VM,
        shape(F32, count, 4 * HEAD, length),
        us=1.0,
        after=after,
    )(rows, *heads, mask, g, mem, *scores, *links, *pairs)


def project_back_body(counts, rows_ref, q_ref, heads_ref, control_ref, partner_ref, far_ref, xnt_ref, *refs):
    d_refs, (proj_ref, keep_ref, send_ref, mem_ref, totals_ref) = refs[: len(counts)], refs[len(counts) :]
    arrived(True, rows_ref, partner_ref, far_ref, mem_ref, totals_ref)
    tail = rows_ref[1:2, :]
    tail_bf = tail.astype(BF)
    places = [(d_ref, n) for d_ref, count in zip(d_refs, counts) for n in range(count)]
    jobs = [(d_ref, n, head_of(i >= SIDE, i % SIDE)) for i, (d_ref, n) in enumerate(places)]
    more = []
    for d_ref, n, head in jobs:
        mem = mem_ref[head_rows(head), :]
        back_k, back_vt = mem[:, :HEAD], mem[:, HEAD:]
        q, k, v, c = parts((q_ref, heads_ref), head)
        c_tail = c * tail_bf
        more.append((tn(back_k, c_tail), nn(back_vt, c_tail), nn(back_k, k) + tn(back_vt, v)))
    for (d_ref, n, head), (more_k, more_v, more_c) in zip(jobs, more):
        rows = head_rows(head)
        proj_ref[0, rows, :] = d_ref[n, :HEAD, :].astype(BF)
        proj_ref[1, rows, :] = (d_ref[n, HEAD : 2 * HEAD, :] + more_k).astype(BF)
        proj_ref[2, rows, :] = (d_ref[n, 2 * HEAD : 3 * HEAD, :] + more_v).astype(BF)
        d_control = d_ref[n, 3 * HEAD :, :] + tail * (more_c + totals_ref[rows, 0:1])
        proj_ref[3, rows, :] = (d_control * control_ref[rows, :]).astype(BF)
    for own_side in (False, True):
        first = pl.ds(pl.multiple_of(head_of(own_side, 0) * HEAD, SIDE * HEAD), SIDE * HEAD)
        for m in range(4):
            grad = nt(xnt_ref[...], proj_ref[m, first, :]).astype(BF)
            if own_side:
                keep_ref[:, m * SIDE * HEAD : (m + 1) * SIDE * HEAD] = grad
            else:
                send_ref[:, m * SIDE * HEAD : (m + 1) * SIDE * HEAD] = grad


def project_back(rows, heads, ds, control, partner, far, xnt, after=()):
    width, length = xnt.shape
    return call(
        functools.partial(project_back_body, [d.shape[0] for d in ds]),
        (),
        [VM] * (7 + len(ds)),
        [VM] * 3,
        [shape(BF, 4, width, length)] + [shape(BF, width, 4 * SIDE * HEAD)] * 2,
        [pltpu.VMEM((width, 128), BF), pltpu.VMEM((width, 8), F32)],
        us=5.0,
        after=after,
    )(rows, *heads, control, partner, far, xnt, *ds)


def norm_back_body(proj_ref, w_ref, n_ref, inv_ref, gain_ref, d_hidden1_ref, norms2_ref, grad_x_ref, norms_ref):
    length, width = n_ref.shape
    proj = proj_ref[...].reshape(4 * width, length)
    halves = [slice(0, length // 2), slice(length // 2, length)]
    ds = [
        lax.dot_general(proj[:, at], w_ref[...], (((0,), (1,)), ((), ())), preferred_element_type=F32)
        for at in halves
    ]
    sums = []
    for at, d in zip(halves, ds):
        n = n_ref[at, :]
        sums.append([jnp.sum(d * n, axis=0, keepdims=True), jnp.sum(d, axis=0, keepdims=True)])
        d_n = d * gain_ref[...]
        grad_x_ref[at, :] = d_hidden1_ref[at, :] + (
            d_n
            - jnp.mean(d_n, axis=-1, keepdims=True)
            - n * jnp.mean(d_n * n, axis=-1, keepdims=True)
        ) * inv_ref[at, 0:1]
    rows8 = jnp.concatenate([a + b for a, b in zip(*sums)] + [norms2_ref[0:6, :]], axis=0)
    norms_ref[...] = jnp.concatenate([rows8, jnp.zeros((120, length), F32)], axis=0).T.astype(BF)


def norm_back(proj, w, n, inv, gain, d_hidden1, norms2, after=()):
    length, width = n.shape
    return call(
        norm_back_body,
        (),
        [VM] * 7,
        [VM] * 2,
        [shape(F32, length, width), shape(BF, width, 128)],
        us=1e3,
        after=after,
    )(proj, w, n, inv, gain, d_hidden1, norms2)


def bit_axis(bit):
    return ("seq", 1) if bit == 0 else ("dp", 1 << (bit - 1))


def my_bit(bit):
    axis, step = bit_axis(bit)
    return (lax.axis_index(axis) // step) % 2


def send_across(a, bits):
    seqs, dps = lax.axis_size("seq"), lax.axis_size("dp")
    flip = sum(1 << bit for bit in bits)
    return lax.ppermute(a, ("dp", "seq"), [(i, i ^ flip) for i in range(seqs * dps)])


def place_of(t, places, values):
    index, rest, bit = 0, t, 0
    fixed = dict(zip(places, values))
    while rest or fixed:
        if bit in fixed:
            index = index + fixed.pop(bit) * (1 << bit)
        else:
            index = index + ((rest & 1) << bit)
            rest >>= 1
        bit += 1
    return index


def stage_body(plan, *refs):
    refs = list(refs)
    ins = [
        [[refs.pop(0).at[:, :, pl.ds(*piece)] for piece in pieces] for pieces in arrays] for arrays, _ in plan
    ]
    for (arrays, split), sources in zip(plan, ins):
        outs = [refs.pop(0) for _ in range(1 << len(split))]
        blocks = outs[0].shape[0]
        places = [place for _, place in split]
        mine = [my_bit(bit) for bit, _ in split]
        for pattern, out in enumerate(outs):
            values = [
                (1 - m) if (pattern >> n) & 1 else m for n, m in enumerate(mine)
            ]
            for t in range(blocks):
                at = place_of(t, places, values)
                rows = [
                    jnp.concatenate([p[at] for p in pieces], axis=1) if len(pieces) > 1 else pieces[0][at]
                    for pieces in sources
                ]
                if len(rows) == 1 or (len(rows) == 2 and out.dtype == BF):
                    total = sum(rows[1:], rows[0])
                else:
                    total = sum(row.astype(F32) for row in rows)
                out[t] = total.astype(out.dtype)


def stage(groups, after=(), dtype=BF, us=1.0):
    plan, operands, out_shape = [], [], []
    for arrays, split in groups:
        for pieces in arrays:
            operands += [array for array, _, _ in pieces]
        (array, _, _), width = arrays[0][0], sum(p[2] for p in arrays[0])
        plan.append(([[(first, count) for _, first, count in pieces] for pieces in arrays], split))
        out_shape += [shape(dtype, array.shape[0] >> len(split), array.shape[1], width)] * (1 << len(split))
    outs = list(
        call(functools.partial(stage_body, plan), (), [VM] * len(operands), [VM] * len(out_shape), out_shape, us=us, after=after)(
            *operands
        )
    )
    return [[outs.pop(0) for _ in range(1 << len(split))] for _, split in groups]


def all_of(a):
    return [(a, 0, a.shape[2])]


def patterns(bits):
    return [[b for n, b in enumerate(bits) if (p >> n) & 1] for p in range(1, 1 << len(bits))]


def last_body(late_count, columns, *refs):
    *ins, out_ref = refs
    sums = [
        sum(ref[0].astype(F32) for ref in ins[:late_count]),
        *(sum(ref[0][:, at].astype(F32) for ref in ins[late_count:]) for at in columns),
    ]
    out_ref[...] = jnp.concatenate(sums, axis=1).astype(BF)


def last(late, early, columns):
    rows = late[0].shape[1]
    width = late[0].shape[2] + sum(at.stop - at.start for at in columns)
    return call(
        functools.partial(last_body, len(late), columns),
        (),
        [VM] * (len(late) + len(early)),
        VM,
        shape(BF, rows, width),
    )(*late, *early)


def join_body(up_at, down_at, own_ref, other_ref, a_ref, b_ref,
              grad_in_ref, grad_out_ref, grad_up_ref, grad_down_ref, *norm_refs):
    second = lax.axis_index("ffn") == 1
    own, other = own_ref[...].astype(F32), other_ref[...].astype(F32)
    for f in range(2):
        keep_own = second if f else jnp.logical_not(second)
        half = jnp.where(keep_own, own, other)
        for m in range(4):
            grad_in_ref[:, m * 512 + f * 256 : m * 512 + f * 256 + 256] = half[:, m * 256 : m * 256 + 256]
        grad_out_ref[:, f * 256 : f * 256 + 256] = half[:, 1152:]
    for at, ref in ((up_at, grad_up_ref), (down_at, grad_down_ref)):
        ref[...] = a_ref[0][:, at].astype(F32) + b_ref[0][:, at].astype(F32)
    norms = (own[:, 1024:1152] + other[:, 1024:1152]).T
    for n, ref in enumerate(norm_refs):
        ref[...] = norms[n]


def join(own, other, early, up_at, down_at):
    rows = own.shape[0]
    half = up_at.stop - up_at.start
    return call(
        functools.partial(join_body, up_at, down_at),
        (),
        [VM] * 4,
        [VM] * 8,
        [shape(F32, rows, n) for n in (2048, 512, half, half)] + [shape(F32, rows)] * 4,
    )(own, other, *early)


def on_device(tokens, doc_starts, norm1_gain, norm1_bias, in_weight, out_weight,
              norm2_gain, norm2_bias, up_own, down_own, output_cotangent):
    x, cotangent, starts = tokens[0], output_cotangent[0], doc_starts
    length, width = x.shape
    owners = lax.axis_size("dp") * lax.axis_size("seq")
    bits = owners.bit_length() - 1
    row = lambda a: a.reshape(1, width)
    blocked = lambda a: a.reshape(owners, width // owners, a.shape[1])

    kvc, raw, xn, own, mask, rows, n1, inv1 = project(
        x, row(norm1_gain), row(norm1_bias), in_weight, starts)
    up_other, down_other = swap(up_own, "ffn", 1), swap(down_own, "ffn", 1)
    partner = swap(own, "ffn", 1)
    heads = (query(xn, in_weight), kvc)
    both = combine(False, rows, own, partner, after=heads[:1])
    far = swap(both, "seq", 1)
    number_o, total_o, *pairs_other = local_sums(False, heads, mask, after=[both])
    number, total, *pairs_own = local_sums(True, heads, mask, after=[both])
    d_hidden_other, d_hidden_own, cott, control, xnt = prepare(
        cotangent, down_own, down_other, raw, xn, after=[number])
    mixed, memory, saved_other, saved_own = mix(
        rows, heads, mask, partner, far, (number_o, total_o), (number, total), after=[cott])
    gup_send, gdown_send, *saved = feed_other(
        x, mixed, cott, d_hidden_other, out_weight, row(norm2_gain), row(norm2_bias), up_other, down_other)
    gup_got, gdown_got = swap(gup_send, "ffn", 1), swap(gdown_send, "ffn", 1)
    (output, d_hidden1, g, out_send, out_keep, norms2, gup_own, gdown_own) = feed_own(
        saved, cott, d_hidden_own, mixed, cotangent, out_weight, row(norm2_gain), up_own, down_own)
    out_got = swap(out_send, "ffn", 1)

    out_half = width // 4
    ups, downs, outs = [
        [blocked(a) for a in pair]
        for pair in ((gup_own, gup_got), (gdown_own, gdown_got), (out_keep, out_got))
    ]
    groups = [
        [[*all_of(a), (o, 0, out_half)] for a, o in zip(ups, outs)],
        [[*all_of(a), (o, out_half, out_half)] for a, o in zip(downs, outs)],
    ]
    orders = [[1, 2], [2, 1]]
    left = [list(range(bits)) for _ in groups]

    def advance(groups, n, after):
        if n >= 2:
            if n == 2:
                groups = [[pieces_a + pieces_b for pieces_a, pieces_b in zip(*groups)]]
            bits_now = left[0][-1:]
            splits = [[(bits_now[0], len(left[0]) - 1)]]
            for rest in left:
                rest.pop()
        else:
            bits_now = [order[n] for order in orders]
            splits = [[(bit, rest.index(bit))] for bit, rest in zip(bits_now, left)]
            for bit, rest in zip(bits_now, left):
                rest.remove(bit)
        outs = stage(list(zip(groups, splits)), after=after)
        got = [send_across(sent, [bit]) for (_, sent), bit in zip(outs, bits_now)]
        sent = [s for _, s in outs]
        return [[all_of(kept), all_of(r)] for (kept, _), r in zip(outs, got)], sent

    back = (rows, heads, mask, g, memory)
    *scores_other, pack, sums = scores_back(False, *back, saved_other)
    groups, sent = advance(groups, 0, [pack])
    *scores_own, d_own = scores_back(True, *back, saved_own, packs=(pack, sums), after=sent)
    d_partner = swap(d_own, "ffn", 1)
    other_side, own_side = (scores_other, saved_other[3:], pairs_other), (scores_own, saved_own[3:], pairs_own)
    ds = []
    if SPLIT:
        ds.append(heads_back(False, 0, SPLIT, *back, *other_side, after=[d_own]))
    d_both = combine(True, rows, d_own, d_partner, after=ds)
    d_far = swap(d_both, "seq", 1)
    ds.append(heads_back(False, SPLIT, SIDE - SPLIT, *back, *other_side, after=[d_both]))
    ds.append(heads_back(True, 0, SIDE, *back, *own_side, after=ds[-1:]))
    proj, in_keep, in_send = project_back(rows, heads, ds, control, d_partner, d_far, xnt)
    in_got = swap(in_send, "ffn", 1)
    groups, sent = advance(groups, 1, [in_send])
    grad_tokens, norms = norm_back(
        proj, in_weight, n1, inv1, row(norm1_gain), d_hidden1, norms2, after=sent)

    late = [
        all_of(blocked(in_keep)) + all_of(blocked(norms)),
        all_of(blocked(in_got)) + all_of(jnp.zeros_like(blocked(norms))),
    ]
    rest = list(range(bits))
    stages = list(range(2, bits))
    while rest:
        now = rest[:2]
        split = [(b, rest.index(b)) for b in now]
        rest = rest[2:]
        (kept, *sent), = stage([(late, split)])
        pairs = list(zip(sent, patterns(now)))
        if now[0]:
            pairs = pairs[1:] + pairs[:1]
        late = [all_of(kept)] + [all_of(send_across(s, p)) for s, p in pairs]
        token = [kept]
        while stages:
            groups, token = advance(groups, stages.pop(0), token)
            if rest:
                break
    early = [arrays[0][0] for arrays in groups[0]]
    half = gup_own.shape[1]
    down_at = half + out_half
    outs_at = [slice(half, down_at), slice(down_at + half, down_at + half + out_half)]
    (total,), = stage([(late, [])], us=1e3)
    final = last([total], early, outs_at)
    grad_in, grad_out, grad_up, grad_down, *norms = join(
        final, swap(final, "ffn", 1), early, slice(0, half), slice(down_at, down_at + half))
    return (output[None], grad_tokens[None], grad_in, grad_out, grad_up, grad_down, *norms)


def solution(mesh):
    rows = P("dp", ("seq", "ffn"), None)
    owned = P(("dp", "seq"))
    return jax.shard_map(
        on_device,
        mesh=mesh,
        in_specs=(
            rows, P("dp", None), P(), P(), P(), P(), P(), P(),
            P(None, "ffn"), P(None, "ffn"), rows,
        ),
        out_specs=(
            rows, rows, P(("dp", "seq"), None), P(("dp", "seq"), None),
            P(("dp", "seq"), "ffn"), P(("dp", "seq"), "ffn"),
            owned, owned, owned, owned,
        ),
        check_vma=False,
    )
```

```python
import functools

import jax
import jax.numpy as jnp
from jax import lax
from jax.experimental import pallas as pl
from jax.experimental.pallas import tpu as pltpu
from jax.sharding import PartitionSpec as P

HEADS = 8
HEAD = 64
EPSILON = 1e-05
BF = jnp.bfloat16
F32 = jnp.float32
GELU_A = 0.7978845608028654
GELU_B = 0.044715
SCALE = HEAD**-0.5
K1_VMEM = 48
SPLIT = 2
SIDE = HEADS // 2
PACK = HEADS * HEAD + 64


def nn(a, b):
    return lax.dot_general(a, b, (((1,), (0,)), ((), ())), preferred_element_type=F32)


def nt(a, b):
    return lax.dot_general(a, b, (((1,), (1,)), ((), ())), preferred_element_type=F32)


def tn(a, b):
    return lax.dot_general(a, b, (((0,), (0,)), ((), ())), preferred_element_type=F32)


def swap(a, axis, bit):
    size = lax.axis_size(axis)
    return lax.ppermute(a, axis, [(i, i ^ bit) for i in range(size)])


ANY = pl.BlockSpec(memory_space=pl.ANY)


def call(body, grid, in_specs, out_specs, out_shape, scratch=(), us=1.0, after=(), vmem=20):
    count = len(in_specs)

    def run(*refs):
        body(*refs[:count], *refs[count + len(after) :])

    def start(*operands):
        return pl.pallas_call(
            run,
            grid=grid,
            in_specs=list(in_specs) + [ANY] * len(after),
            out_specs=out_specs,
            out_shape=out_shape,
            scratch_shapes=list(scratch),
            cost_estimate=pl.CostEstimate(flops=int(us * 1e7), bytes_accessed=2**13, transcendentals=0),
            compiler_params=pltpu.CompilerParams(vmem_limit_bytes=vmem * 2**20),
        )(*operands, *after)

    return start


def whole(shape):
    return pl.BlockSpec(shape, lambda *_: (0,) * len(shape))


VM = pl.BlockSpec(memory_space=pltpu.MemorySpace.VMEM)


def shape(dtype, *dims):
    return jax.ShapeDtypeStruct(dims, dtype)


SMEM = pl.BlockSpec(memory_space=pltpu.SMEM)


def shard_of():
    return lax.axis_index("seq") * 2 + lax.axis_index("ffn")


def doc_begin_row(starts_ref, length):
    begin = shard_of() * length
    place = lax.broadcasted_iota(jnp.int32, (1, length), 1)
    row = jnp.full((1, length), -(2**30), jnp.int32)
    for j in range(starts_ref.shape[1]):
        s = starts_ref[0, j] - begin
        row = jnp.where(place >= s, jnp.maximum(row, s), row)
    return row


def passes(starts_ref, which, length):
    hit = jnp.int32(0)
    for j in range(starts_ref.shape[1]):
        s = starts_ref[0, j]
        hit = hit | ((s >= which * length) & (s < which * length + length)).astype(jnp.int32)
    return 1.0 - hit.astype(F32)


def visible(doc_row, length):
    i = lax.broadcasted_iota(jnp.int32, (length, length), 0)
    t = lax.broadcasted_iota(jnp.int32, (length, length), 1)
    return jnp.where((i <= t) & (i >= doc_row), 1.0, 0.0).astype(BF)


def tail_row(doc_row, length):
    place = lax.broadcasted_iota(jnp.int32, (1, length), 1)
    last = doc_row[:, length - 1 :]
    return jnp.where(place >= last, 1.0, 0.0)


def pack_totals(pack_ref, totals8):
    base = HEADS * HEAD
    hi = totals8.astype(BF)
    lo = (totals8 - hi.astype(F32)).astype(BF)
    for a in range(4):
        cols = slice(128 * a, 128 * a + 128)
        pack_ref[base + 16 * a : base + 16 * a + 16, :] = jnp.concatenate(
            [hi[:, cols], lo[:, cols]], axis=0
        )


def unpack(rows, totals8_of):
    base = HEADS * HEAD
    out = []
    for a in range(4):
        block = totals8_of(slice(base + 16 * a, base + 16 * a + 16))
        out.append(block[:8] + block[8:])
    return rows(slice(0, base)), jnp.concatenate(out, axis=1)


def combine_body(backward, rows_ref, own_ref, partner_ref, out_ref):
    is_first = (lax.axis_index("ffn") == 0).astype(F32)
    base = HEADS * HEAD
    if backward:
        p = rows_ref[2:3, :128]
        own_by, partner_by = is_first + (1 - is_first) * p, is_first * p + (1 - is_first)
    else:
        p = rows_ref[3:4, :128]
        own_by, partner_by = is_first * p + (1 - is_first), is_first + (1 - is_first) * p

    def sum_of(at):
        return own_ref[at, :].astype(F32) * own_by + partner_ref[at, :].astype(F32) * partner_by

    memory, totals8 = unpack(sum_of, sum_of)
    out_ref[:base, :] = memory.astype(BF)
    pack_totals(out_ref, totals8)


def combine(backward, rows, own, partner, after=()):
    return call(
        functools.partial(combine_body, backward),
        (),
        [VM] * 3,
        VM,
        shape(BF, PACK, 128),
        after=after,
    )(rows, own, partner)


def arrived(backward, rows_ref, partner_ref, far_ref, mem_ref, totals_ref):
    is_first = (lax.axis_index("ffn") == 0).astype(F32)
    if backward:
        p = rows_ref[3:4, :128]
        far_by, partner_by = is_first * p + (1 - is_first), is_first
        valid = lax.axis_index("seq") == 0
    else:
        p = rows_ref[2:3, :128]
        far_by, partner_by = is_first + (1 - is_first) * p, 1 - is_first
        valid = lax.axis_index("seq") == 1

    def sum_of(at):
        far = jnp.where(valid, far_ref[at, :].astype(F32), 0.0)
        return far * far_by + partner_ref[at, :].astype(F32) * partner_by

    memory, totals8 = unpack(sum_of, sum_of)
    mem_ref[...] = memory.astype(BF)
    totals_ref[...] = totals8.T


def head_of(own_side, h):
    ffn = lax.axis_index("ffn")
    return (ffn if own_side else 1 - ffn) * SIDE + h


def head_rows(head):
    return pl.ds(pl.multiple_of(head * HEAD, HEAD), HEAD)


def project_body(x_hbm, gain_hbm, bias_hbm, w_hbm, starts_ref,
                 heads_ref, raw_ref, xn_ref, pack_ref, mask_ref, rows_ref, n_ref, inv_ref, wq_ref,
                 x_ref, gain_ref, bias_ref, w_ref, sems):
    length, width = x_ref.shape
    copies = [
        pltpu.make_async_copy(x_hbm, x_ref, sems.at[0]),
        pltpu.make_async_copy(gain_hbm, gain_ref, sems.at[1]),
        pltpu.make_async_copy(bias_hbm, bias_ref, sems.at[2]),
    ]
    columns = [
        pltpu.make_async_copy(w_hbm.at[:, pl.ds((j + 1) * width, width)], w_ref.at[j], sems.at[3 + j])
        for j in range(3)
    ]
    later = pltpu.make_async_copy(w_hbm.at[:, pl.ds(0, width)], wq_ref, sems.at[6])
    for copy in copies + columns + [later]:
        copy.start()
    doc_row = doc_begin_row(starts_ref, length)
    tail = tail_row(doc_row, length)
    first = 2 * lax.axis_index("seq")
    rows = [jnp.where(doc_row < 0, 1.0, 0.0), tail] + [
        jnp.full((1, length), passes(starts_ref, which, length)) for which in (first, first + 1)
    ]
    rows_ref[...] = jnp.concatenate(rows + rows, axis=0)
    mask_ref[...] = visible(doc_row, length)
    for copy in copies:
        copy.wait()
    x = x_ref[...].astype(F32)
    mean = jnp.mean(x, axis=-1, keepdims=True)
    centered = x - mean
    inverse = lax.rsqrt(jnp.mean(centered * centered, axis=-1, keepdims=True) + EPSILON)
    n = centered * inverse
    n_ref[...] = n
    inv_ref[...] = jnp.broadcast_to(inverse, inv_ref.shape)
    xn = (n * gain_ref[...] + bias_ref[...]).astype(BF)
    xn_ref[...] = xn
    projected = []
    for j in range(3):
        columns[j].wait()
        projected.append(nn(xn, w_ref[j]))
    raw_ref[...] = projected[2]
    c = jnp.exp(projected[2]).astype(BF).T
    for j in range(2):
        t = projected[j].astype(BF).T
        for h in range(HEADS):
            heads_ref[h, j * HEAD : j * HEAD + HEAD, :] = t[h * HEAD : h * HEAD + HEAD]
    c_tail = c * tail.astype(BF)
    for h in range(HEADS):
        rows = slice(h * HEAD, h * HEAD + HEAD)
        heads_ref[h, 2 * HEAD :, :] = c[rows]
        mem_k = nt(c_tail[rows], heads_ref[h, :HEAD, :])
        mem_vt = nt(heads_ref[h, HEAD : 2 * HEAD, :], c_tail[rows])
        pack_ref[rows, :] = jnp.concatenate([mem_k, mem_vt], axis=1).astype(BF)
    tail8 = jnp.broadcast_to(tail, (8, length)).astype(BF)
    pack_totals(pack_ref, nt(tail8, c))
    later.wait()


def project(x, gain, bias, w, starts):
    length, width = x.shape
    hbm = pl.BlockSpec(memory_space=pltpu.MemorySpace.HBM)
    pin = lambda a: pltpu.with_memory_space_constraint(a, pltpu.HBM)
    return call(
        project_body,
        (),
        [hbm, hbm, hbm, hbm, SMEM],
        [VM] * 9,
        [
            shape(BF, HEADS, 3 * HEAD, length), shape(F32, length, width), shape(BF, length, width),
            shape(BF, PACK, 128), shape(BF, length, length), shape(F32, 8, length),
            shape(F32, length, width), shape(F32, length, 128), shape(BF, width, width),
        ],
        [
            pltpu.VMEM((length, width), BF), pltpu.VMEM((1, width), F32), pltpu.VMEM((1, width), F32),
            pltpu.VMEM((3, width, width), BF), pltpu.SemaphoreType.DMA((7,)),
        ],
        us=4.3,
        vmem=K1_VMEM,
    )(*(pin(a) for a in (x, gain, bias, w, starts)))


def query_body(xn_ref, w_ref, q_ref):
    t = nn(xn_ref[...], w_ref[...]).astype(BF).T
    for h in range(HEADS):
        q_ref[h] = t[h * HEAD : h * HEAD + HEAD]


def query(xn, w, after=()):
    return call(query_body, (), [VM] * 2, VM, shape(BF, HEADS, HEAD, xn.shape[0]), us=1e3, after=after)(xn, w)


def parts(refs, head):
    q_ref, heads_ref = refs
    return [q_ref[head]] + [heads_ref[head, j * HEAD : j * HEAD + HEAD, :] for j in range(3)]


def mask_pair(mask_ref):
    half = mask_ref.shape[0] // 2
    return mask_ref[:half, :half], mask_ref[:, half:]


def causal_pairs(left, right, mask_ref):
    half = mask_ref.shape[0] // 2
    early, late = mask_pair(mask_ref)
    rows = left.T
    return nn(rows[:half], right[:, :half]).astype(BF) * early, nn(rows, right[:, half:]).astype(BF) * late


def causal_sum(left, pairs):
    a, b = pairs
    half = a.shape[0]
    return jnp.concatenate([nn(left[:, :half], a), nn(left, b)], axis=1)


def causal_back(pairs, right):
    a, b = pairs
    half = a.shape[0]
    late = nn(b, right[half:])
    return jnp.concatenate([late[:half] + nn(a, right[:half]), late[half:]], axis=0)


def padded(rows, second):
    zero = jnp.zeros_like(rows)
    return jnp.concatenate([zero, rows] if second else [rows, zero], axis=0).T


def pair_shapes(length, count=SIDE):
    half = length // 2
    return [shape(BF, count, half, half), shape(BF, count, length, half)]


def store_pairs(refs, i, pairs):
    refs[0][i], refs[1][i] = pairs


def load_pairs(refs, i):
    return refs[0][i], refs[1][i]


def local_body(own_side, q_ref, heads_ref, mask_ref, number_ref, total_ref, *pair_refs):
    held = [parts((q_ref, heads_ref), head_of(own_side, i)) for i in range(SIDE)]
    pairs = [causal_pairs(k, q, mask_ref) for q, k, v, c in held]
    for i in range(SIDE):
        store_pairs(pair_refs, i, pairs[i])
    c = jnp.concatenate([h[3] for h in held], axis=0)
    total_ref[...] = causal_sum(c, mask_pair(mask_ref))
    for i in range(SIDE):
        number_ref[i * HEAD : i * HEAD + HEAD, :] = causal_sum(held[i][3], pairs[i])


def local_sums(own_side, heads, mask, after=()):
    length = heads[0].shape[2]
    return call(
        functools.partial(local_body, own_side),
        (),
        [VM] * 3,
        [VM] * 4,
        [shape(F32, SIDE * HEAD, length)] * 2 + pair_shapes(length),
        us=3.0,
        after=after,
    )(*heads, mask)


def mix_body(rows_ref, q_ref, heads_ref, mask_ref, partner_ref, far_ref, *refs):
    refs = list(refs)
    take = lambda n: [refs.pop(0) for _ in range(n)]
    ins = [take(2), take(2)]
    mixed_ref, mem_ref = take(2)
    outs = [take(5), take(5)]
    (totals_ref,) = refs
    arrived(False, rows_ref, partner_ref, far_ref, mem_ref, totals_ref)
    enters = rows_ref[0:1, :]
    jobs = [(own_side, i) for own_side in (False, True) for i in range(SIDE)]
    spreads, links = [], []
    for own_side, i in jobs:
        number_in, total_in = ins[own_side]
        number_ref, inverse_ref, weight_ref, *_ = outs[own_side]
        head, at = head_of(own_side, i), slice(i * HEAD, i * HEAD + HEAD)
        mem_k = mem_ref[head_rows(head), :][:, :HEAD]
        number = number_in[at, :] + enters * nn(mem_k, parts((q_ref, heads_ref), head)[0])
        inverse = 1.0 / (total_in[at, :] + enters * totals_ref[head_rows(head), 0:1])
        score = number * (inverse * SCALE)
        e = jnp.exp(score - jnp.max(score, axis=0, keepdims=True))
        weight = e * (1.0 / jnp.sum(e, axis=0, keepdims=True))
        number_ref[at, :] = number
        inverse_ref[at, :] = inverse
        weight_ref[at, :] = weight
        spreads.append((weight * inverse).astype(BF))
    for (own_side, i), spread in zip(jobs, spreads):
        links.append(causal_pairs(parts((q_ref, heads_ref), head_of(own_side, i))[3], spread, mask_ref))
        store_pairs(outs[own_side][3:], i, links[-1])
    for (own_side, i), spread, link in zip(jobs, spreads, links):
        head = head_of(own_side, i)
        mem_vt = mem_ref[head_rows(head), :][:, HEAD:]
        mixed = causal_sum(parts((q_ref, heads_ref), head)[2], link) + enters * nn(mem_vt, spread)
        mixed_ref[head_rows(head), :] = mixed.astype(BF)


def mix(rows, heads, mask, partner, far, local_other, local_own, after=()):
    length, width = heads[0].shape[2], HEADS * HEAD
    side = [shape(F32, SIDE * HEAD, length)] * 3 + pair_shapes(length)
    mixed, mem, *rest = call(
        mix_body,
        (),
        [VM] * 10,
        [VM] * 12,
        [shape(BF, width, length), shape(BF, width, 128)] + side + side,
        [pltpu.VMEM((width, 8), F32)],
        us=4.0,
        after=after,
    )(rows, *heads, mask, partner, far, *local_other, *local_own)
    return mixed, mem, rest[:5], rest[5:]


def prepare_body(cot_ref, down_ref, down_other_ref, raw_ref, xn_ref, other_ref, own_ref, cott_ref, control_ref, xnt_ref):
    cot = cot_ref[...]
    other_ref[...] = nn(cot, down_other_ref[...])
    own_ref[...] = nn(cot, down_ref[...])
    cott_ref[...] = cot.T
    xnt_ref[...] = xn_ref[...].T
    control_ref[...] = jnp.exp(raw_ref[...]).T


def prepare(cotangent, down, down_other, raw, xn, after=()):
    length, width = cotangent.shape
    return call(
        prepare_body,
        (),
        [VM] * 5,
        [VM] * 5,
        [shape(F32, length, down.shape[1])] * 2
        + [shape(BF, width, length), shape(F32, width, length), shape(BF, width, length)],
        us=2.0,
        after=after,
    )(cotangent, down, down_other, raw, xn)


def activations(xn, d_hidden_ref, up_ref):
    cols = [slice(j, j + 512) for j in range(0, up_ref.shape[1], 512)]
    pres = [nn(xn, up_ref[:, at]) for at in cols]
    hidden, grad_pre = [], []
    for pre, at in zip(pres, cols):
        v2 = pre * pre
        h = 0.5 + 0.5 * jnp.tanh(pre * (GELU_A + (GELU_A * GELU_B) * v2))
        act = pre * h
        hidden.append(act.astype(BF))
        slope = h + act * (1.0 - h) * (2.0 * GELU_A + (6.0 * GELU_A * GELU_B) * v2)
        grad_pre.append((d_hidden_ref[:, at] * slope).astype(BF))
    return jnp.concatenate(hidden, axis=1), jnp.concatenate(grad_pre, axis=1)


def feed_other_body(x_ref, mixed_ref, cott_ref, d_hidden_ref, w_out_ref, gain_ref, bias_ref, up_ref, down_ref,
                    gup_ref, gdown_ref, hidden1_ref, n_ref, inv_ref, xn_ref, xnt_ref,
                    part_ref, d_ref):
    hidden1 = x_ref[...].astype(F32) + tn(mixed_ref[...], w_out_ref[...])
    hidden1_ref[...] = hidden1
    mean = jnp.mean(hidden1, axis=-1, keepdims=True)
    centered = hidden1 - mean
    inverse = lax.rsqrt(jnp.mean(centered * centered, axis=-1, keepdims=True) + EPSILON)
    n = centered * inverse
    n_ref[...] = n
    inv_ref[...] = jnp.broadcast_to(inverse, inv_ref.shape)
    xn = (n * gain_ref[...] + bias_ref[...]).astype(BF)
    xnt = xn.T
    xn_ref[...] = xn
    xnt_ref[...] = xnt
    hidden, grad_pre = activations(xn, d_hidden_ref, up_ref)
    gdown_ref[...] = nn(cott_ref[...], hidden).astype(BF)
    gup_ref[...] = nn(xnt, grad_pre).astype(BF)
    part_ref[...] = nt(hidden, down_ref[...])
    d_ref[...] = nt(grad_pre, up_ref[...])


def feed_own_body(hidden1_ref, n_ref, inv_ref, xn_ref, xnt_ref, part_ref, d_in_ref, cott_ref, d_hidden_ref,
                  mixed_ref, cot_ref, w_out_ref, gain_ref, up_ref, down_ref,
                  output_ref, d_hidden1_ref, g_ref, out_send_ref, out_keep_ref, norms_ref,
                  gup_ref, gdown_ref):
    hidden, grad_pre = activations(xn_ref[...], d_hidden_ref, up_ref)
    dx, n = d_in_ref[...] + nt(grad_pre, up_ref[...]), n_ref[...]
    norms_ref[...] = jnp.concatenate(
        [jnp.sum(dx * n, axis=0, keepdims=True), jnp.sum(dx, axis=0, keepdims=True)] * 4, axis=0
    )
    output_ref[...] = (hidden1_ref[...] + (part_ref[...] + nt(hidden, down_ref[...]))).astype(BF)
    gdown_ref[...] = nn(cott_ref[...], hidden).astype(BF)
    d_n = dx * gain_ref[...]
    d_in = (
        d_n
        - jnp.mean(d_n, axis=-1, keepdims=True)
        - n * jnp.mean(d_n * n, axis=-1, keepdims=True)
    ) * inv_ref[:, 0:1]
    d_hidden1 = cot_ref[...].astype(F32) + d_in
    d_hidden1_ref[...] = d_hidden1
    d_branch = d_hidden1.astype(BF)
    gup_ref[...] = nn(xnt_ref[...], grad_pre).astype(BF)
    g_ref[...] = nt(w_out_ref[...], d_branch).astype(BF)
    grad_out = nn(mixed_ref[...], d_branch).astype(BF)
    half = grad_out.shape[1] // 2
    second = lax.axis_index("ffn") == 1
    out_keep_ref[...] = jnp.where(second, grad_out[:, half:], grad_out[:, :half])
    out_send_ref[...] = jnp.where(second, grad_out[:, :half], grad_out[:, half:])


def feed_other(x, mixed, cott, d_hidden, w_out, gain, bias, up, down):
    length, width = x.shape
    half, sq = shape(BF, *up.shape), lambda dt: shape(dt, length, width)
    return call(
        feed_other_body,
        (),
        [VM] * 9,
        [VM] * 9,
        [half, half, sq(F32), sq(F32), shape(F32, length, 128), sq(BF), sq(BF), sq(F32), sq(F32)],
        us=6.0,
    )(x, mixed, cott, d_hidden, w_out, gain, bias, up, down)


def feed_own(saved, cott, d_hidden, mixed, cotangent, w_out, gain, up, down, after=()):
    length, width = mixed.shape
    half, sq = shape(BF, *up.shape), lambda dt: shape(dt, length, width)
    return call(
        feed_own_body,
        (),
        [VM] * 15,
        [VM] * 8,
        [sq(BF), sq(F32), sq(BF)] + [shape(BF, width, width // 2)] * 2 + [shape(F32, 8, width), half, half],
        us=6.0,
        after=after,
    )(*saved, cott, d_hidden, mixed, cotangent, w_out, gain, up, down)


def scores_back_body(own_side, rows_ref, q_ref, heads_ref, mask_ref, g_ref, mem_ref, number_ref, inverse_ref, weight_ref,
                     *refs):
    if own_side:
        pack_in, sums_in, a_ref, spread_ref, d_total_ref, early_ref, late_ref, pack_ref, sums_ref = refs
        pack_ref[...] = pack_in[...]
        sums_ref[...] = sums_in[...]
    else:
        a_ref, spread_ref, d_total_ref, early_ref, late_ref, pack_ref, sums_ref = refs
    enters = rows_ref[0:1, :]
    heads = [head_of(own_side, i) for i in range(SIDE)]
    rows = [head_rows(head) for head in heads]
    held = [parts((q_ref, heads_ref), head) for head in heads]
    values = [causal_pairs(held[i][2], g_ref[rows[i], :], mask_ref) for i in range(SIDE)]
    for i in range(SIDE):
        store_pairs((early_ref, late_ref), i, values[i])
    numbers = [
        causal_sum(held[i][3], values[i]) + enters * tn(mem_ref[rows[i], :][:, HEAD:], g_ref[rows[i], :])
        for i in range(SIDE)
    ]
    kept = []
    for i, number_v in enumerate(numbers):
        at = slice(i * HEAD, i * HEAD + HEAD)
        number, inverse, weight = number_ref[at, :], inverse_ref[at, :], weight_ref[at, :]
        d_weight = number_v * inverse
        d_score = weight * (d_weight - jnp.sum(weight * d_weight, axis=0, keepdims=True))
        a = d_score * (inverse * SCALE)
        spread = weight * inverse
        d_total = -(a * number + spread * number_v) * inverse
        a_ref[at, :] = a.astype(BF)
        spread_ref[at, :] = spread.astype(BF)
        d_total_ref[at, :] = d_total.astype(BF)
        kept.append(((a * enters).astype(BF), (spread * enters).astype(BF), d_total * enters))
    for i, (a, spread, d_total) in enumerate(kept):
        d_k = nt(a, held[i][0])
        d_vt = nt(g_ref[rows[i], :], spread)
        pack_ref[rows[i], :] = jnp.concatenate([d_k, d_vt], axis=1).astype(BF)
        sums_ref[rows[i], :] = jnp.broadcast_to(jnp.sum(d_total, axis=1, keepdims=True), (HEAD, 128))
    if own_side:
        pack_totals(pack_ref, sums_ref[...].T[0:8])


def scores_back(own_side, rows, heads, mask, g, mem, saved, packs=(), after=()):
    length, width = heads[0].shape[2], HEADS * HEAD
    sums = [] if own_side else [shape(F32, width, 128)]
    outs = [shape(BF, SIDE * HEAD, length)] * 3 + pair_shapes(length) + [shape(BF, PACK, 128)] + sums
    return call(
        functools.partial(scores_back_body, own_side),
        (),
        [VM] * (9 + len(packs)),
        [VM] * len(outs),
        outs,
        [pltpu.VMEM((width, 128), F32)] if own_side else [],
        us=3.0,
        after=after,
    )(rows, *heads, mask, g, mem, *saved[:3], *packs)


def heads_back_body(own_side, begin, rows_ref, q_ref, heads_ref, mask_ref, g_ref, mem_ref, a_ref, spread_ref, d_total_ref,
                    v_early, v_late, l_early, l_late, p_early, p_late, d_ref):
    enters = rows_ref[0:1, :]
    count = d_ref.shape[0]
    order = range(begin, begin + count)
    heads = [head_of(own_side, i) for i in order]
    rows = [head_rows(head) for head in heads]
    held = [parts((q_ref, heads_ref), head) for head in heads]
    ats = [slice(i * HEAD, i * HEAD + HEAD) for i in order]
    steps = [causal_pairs(h[3], a_ref[at, :], mask_ref) for h, at in zip(held, ats)]
    totals = d_total_ref[begin * HEAD : (begin + count) * HEAD, :]
    from_totals = causal_back(mask_pair(mask_ref), totals.T).T
    controls = []
    for i, at in zip(order, ats):
        odd = i % 2 == 1
        controls.append(
            causal_back(load_pairs((p_early, p_late), i), padded(a_ref[at, :], odd))
            + causal_back(load_pairs((v_early, v_late), i), padded(spread_ref[at, :], odd))
        )
    for n in range(count):
        mem_k = mem_ref[rows[n], :][:, :HEAD]
        d_ref[n, :HEAD, :] = causal_sum(held[n][1], steps[n]) + enters * tn(mem_k, a_ref[ats[n], :])
    for n, i in enumerate(order):
        d_ref[n, HEAD : 3 * HEAD, :] = (
            causal_back(steps[n], padded(held[n][0], False))
            + causal_back(load_pairs((l_early, l_late), i), padded(g_ref[rows[n], :], True))
        ).T
    for n in range(0, count, 2):
        two = (controls[n] + controls[n + 1]).T
        for m in range(2):
            d_ref[n + m, 3 * HEAD :, :] = (
                two[m * HEAD : m * HEAD + HEAD] + from_totals[(n + m) * HEAD : (n + m) * HEAD + HEAD]
            )


def heads_back(own_side, begin, count, rows, heads, mask, g, mem, scores, links, pairs, after=()):
    length = heads[0].shape[2]
    return call(
        functools.partial(heads_back_body, own_side, begin),
        (),
        [VM] * 15,
        VM,
        shape(F32, count, 4 * HEAD, length),
        us=1.0,
        after=after,
    )(rows, *heads, mask, g, mem, *scores, *links, *pairs)


def project_back_body(counts, rows_ref, q_ref, heads_ref, control_ref, partner_ref, far_ref, xnt_ref, *refs):
    d_refs, (proj_ref, keep_ref, send_ref, mem_ref, totals_ref) = refs[: len(counts)], refs[len(counts) :]
    arrived(True, rows_ref, partner_ref, far_ref, mem_ref, totals_ref)
    tail = rows_ref[1:2, :]
    tail_bf = tail.astype(BF)
    places = [(d_ref, n) for d_ref, count in zip(d_refs, counts) for n in range(count)]
    jobs = [(d_ref, n, head_of(i >= SIDE, i % SIDE)) for i, (d_ref, n) in enumerate(places)]
    more = []
    for d_ref, n, head in jobs:
        mem = mem_ref[head_rows(head), :]
        back_k, back_vt = mem[:, :HEAD], mem[:, HEAD:]
        q, k, v, c = parts((q_ref, heads_ref), head)
        c_tail = c * tail_bf
        more.append((tn(back_k, c_tail), nn(back_vt, c_tail), nn(back_k, k) + tn(back_vt, v)))
    for (d_ref, n, head), (more_k, more_v, more_c) in zip(jobs, more):
        rows = head_rows(head)
        proj_ref[0, rows, :] = d_ref[n, :HEAD, :].astype(BF)
        proj_ref[1, rows, :] = (d_ref[n, HEAD : 2 * HEAD, :] + more_k).astype(BF)
        proj_ref[2, rows, :] = (d_ref[n, 2 * HEAD : 3 * HEAD, :] + more_v).astype(BF)
        d_control = d_ref[n, 3 * HEAD :, :] + tail * (more_c + totals_ref[rows, 0:1])
        proj_ref[3, rows, :] = (d_control * control_ref[rows, :]).astype(BF)
    for own_side in (False, True):
        first = pl.ds(pl.multiple_of(head_of(own_side, 0) * HEAD, SIDE * HEAD), SIDE * HEAD)
        for m in range(4):
            grad = nt(xnt_ref[...], proj_ref[m, first, :]).astype(BF)
            if own_side:
                keep_ref[:, m * SIDE * HEAD : (m + 1) * SIDE * HEAD] = grad
            else:
                send_ref[:, m * SIDE * HEAD : (m + 1) * SIDE * HEAD] = grad


def project_back(rows, heads, ds, control, partner, far, xnt, after=()):
    width, length = xnt.shape
    return call(
        functools.partial(project_back_body, [d.shape[0] for d in ds]),
        (),
        [VM] * (7 + len(ds)),
        [VM] * 3,
        [shape(BF, 4, width, length)] + [shape(BF, width, 4 * SIDE * HEAD)] * 2,
        [pltpu.VMEM((width, 128), BF), pltpu.VMEM((width, 8), F32)],
        us=5.0,
        after=after,
    )(rows, *heads, control, partner, far, xnt, *ds)


def norm_back_body(proj_ref, w_ref, n_ref, inv_ref, gain_ref, d_hidden1_ref, norms2_ref, grad_x_ref, norms_ref):
    length, width = n_ref.shape
    proj = proj_ref[...].reshape(4 * width, length)
    halves = [slice(0, length // 2), slice(length // 2, length)]
    ds = [
        lax.dot_general(proj[:, at], w_ref[...], (((0,), (1,)), ((), ())), preferred_element_type=F32)
        for at in halves
    ]
    sums = []
    for at, d in zip(halves, ds):
        n = n_ref[at, :]
        sums.append([jnp.sum(d * n, axis=0, keepdims=True), jnp.sum(d, axis=0, keepdims=True)])
        d_n = d * gain_ref[...]
        grad_x_ref[at, :] = d_hidden1_ref[at, :] + (
            d_n
            - jnp.mean(d_n, axis=-1, keepdims=True)
            - n * jnp.mean(d_n * n, axis=-1, keepdims=True)
        ) * inv_ref[at, 0:1]
    rows8 = jnp.concatenate([a + b for a, b in zip(*sums)] + [norms2_ref[0:6, :]], axis=0)
    norms_ref[...] = jnp.concatenate([rows8, jnp.zeros((120, length), F32)], axis=0).T.astype(BF)


def norm_back(proj, w, n, inv, gain, d_hidden1, norms2, after=()):
    length, width = n.shape
    return call(
        norm_back_body,
        (),
        [VM] * 7,
        [VM] * 2,
        [shape(F32, length, width), shape(BF, width, 128)],
        us=1e3,
        after=after,
    )(proj, w, n, inv, gain, d_hidden1, norms2)


def bit_axis(bit):
    return ("seq", 1) if bit == 0 else ("dp", 1 << (bit - 1))


def my_bit(bit):
    axis, step = bit_axis(bit)
    return (lax.axis_index(axis) // step) % 2


def send_across(a, bits):
    seqs, dps = lax.axis_size("seq"), lax.axis_size("dp")
    flip = sum(1 << bit for bit in bits)
    return lax.ppermute(a, ("dp", "seq"), [(i, i ^ flip) for i in range(seqs * dps)])


def place_of(t, places, values):
    index, rest, bit = 0, t, 0
    fixed = dict(zip(places, values))
    while rest or fixed:
        if bit in fixed:
            index = index + fixed.pop(bit) * (1 << bit)
        else:
            index = index + ((rest & 1) << bit)
            rest >>= 1
        bit += 1
    return index


def stage_body(plan, *refs):
    refs = list(refs)
    ins = [
        [[refs.pop(0).at[:, :, pl.ds(*piece)] for piece in pieces] for pieces in arrays] for arrays, _ in plan
    ]
    for (arrays, split), sources in zip(plan, ins):
        outs = [refs.pop(0) for _ in range(1 << len(split))]
        blocks = outs[0].shape[0]
        places = [place for _, place in split]
        mine = [my_bit(bit) for bit, _ in split]
        for pattern, out in enumerate(outs):
            values = [
                (1 - m) if (pattern >> n) & 1 else m for n, m in enumerate(mine)
            ]
            for t in range(blocks):
                at = place_of(t, places, values)
                rows = [
                    jnp.concatenate([p[at] for p in pieces], axis=1) if len(pieces) > 1 else pieces[0][at]
                    for pieces in sources
                ]
                if len(rows) == 1 or (len(rows) == 2 and out.dtype == BF):
                    total = sum(rows[1:], rows[0])
                else:
                    total = sum(row.astype(F32) for row in rows)
                out[t] = total.astype(out.dtype)


def stage(groups, after=(), dtype=BF, us=1.0):
    plan, operands, out_shape = [], [], []
    for arrays, split in groups:
        for pieces in arrays:
            operands += [array for array, _, _ in pieces]
        (array, _, _), width = arrays[0][0], sum(p[2] for p in arrays[0])
        plan.append(([[(first, count) for _, first, count in pieces] for pieces in arrays], split))
        out_shape += [shape(dtype, array.shape[0] >> len(split), array.shape[1], width)] * (1 << len(split))
    outs = list(
        call(functools.partial(stage_body, plan), (), [VM] * len(operands), [VM] * len(out_shape), out_shape, us=us, after=after)(
            *operands
        )
    )
    return [[outs.pop(0) for _ in range(1 << len(split))] for _, split in groups]


def all_of(a):
    return [(a, 0, a.shape[2])]


def patterns(bits):
    return [[b for n, b in enumerate(bits) if (p >> n) & 1] for p in range(1, 1 << len(bits))]


def last_body(late_count, columns, *refs):
    *ins, out_ref = refs
    sums = [
        sum(ref[0].astype(F32) for ref in ins[:late_count]),
        *(sum(ref[0][:, at].astype(F32) for ref in ins[late_count:]) for at in columns),
    ]
    out_ref[...] = jnp.concatenate(sums, axis=1).astype(BF)


def last(late, early, columns):
    rows = late[0].shape[1]
    width = late[0].shape[2] + sum(at.stop - at.start for at in columns)
    return call(
        functools.partial(last_body, len(late), columns),
        (),
        [VM] * (len(late) + len(early)),
        VM,
        shape(BF, rows, width),
    )(*late, *early)


def join_body(up_at, down_at, own_ref, other_ref, a_ref, b_ref,
              grad_in_ref, grad_out_ref, grad_up_ref, grad_down_ref, *norm_refs):
    second = lax.axis_index("ffn") == 1
    own, other = own_ref[...].astype(F32), other_ref[...].astype(F32)
    for f in range(2):
        keep_own = second if f else jnp.logical_not(second)
        half = jnp.where(keep_own, own, other)
        for m in range(4):
            grad_in_ref[:, m * 512 + f * 256 : m * 512 + f * 256 + 256] = half[:, m * 256 : m * 256 + 256]
        grad_out_ref[:, f * 256 : f * 256 + 256] = half[:, 1152:]
    for at, ref in ((up_at, grad_up_ref), (down_at, grad_down_ref)):
        ref[...] = a_ref[0][:, at].astype(F32) + b_ref[0][:, at].astype(F32)
    norms = (own[:, 1024:1152] + other[:, 1024:1152]).T
    for n, ref in enumerate(norm_refs):
        ref[...] = norms[n]


def join(own, other, early, up_at, down_at):
    rows = own.shape[0]
    half = up_at.stop - up_at.start
    return call(
        functools.partial(join_body, up_at, down_at),
        (),
        [VM] * 4,
        [VM] * 8,
        [shape(F32, rows, n) for n in (2048, 512, half, half)] + [shape(F32, rows)] * 4,
    )(own, other, *early)


def on_device(tokens, doc_starts, norm1_gain, norm1_bias, in_weight, out_weight,
              norm2_gain, norm2_bias, up_own, down_own, output_cotangent):
    x, cotangent, starts = tokens[0], output_cotangent[0], doc_starts
    length, width = x.shape
    owners = lax.axis_size("dp") * lax.axis_size("seq")
    bits = owners.bit_length() - 1
    row = lambda a: a.reshape(1, width)
    blocked = lambda a: a.reshape(owners, width // owners, a.shape[1])

    kvc, raw, xn, own, mask, rows, n1, inv1, wq = project(
        x, row(norm1_gain), row(norm1_bias), in_weight, starts)
    up_other, down_other = swap(up_own, "ffn", 1), swap(down_own, "ffn", 1)
    partner = swap(own, "ffn", 1)
    heads = (query(xn, wq), kvc)
    both = combine(False, rows, own, partner, after=heads[:1])
    far = swap(both, "seq", 1)
    number_o, total_o, *pairs_other = local_sums(False, heads, mask, after=[both])
    number, total, *pairs_own = local_sums(True, heads, mask, after=[both])
    d_hidden_other, d_hidden_own, cott, control, xnt = prepare(
        cotangent, down_own, down_other, raw, xn, after=[number])
    mixed, memory, saved_other, saved_own = mix(
        rows, heads, mask, partner, far, (number_o, total_o), (number, total), after=[cott])
    gup_send, gdown_send, *saved = feed_other(
        x, mixed, cott, d_hidden_other, out_weight, row(norm2_gain), row(norm2_bias), up_other, down_other)
    gup_got, gdown_got = swap(gup_send, "ffn", 1), swap(gdown_send, "ffn", 1)
    (output, d_hidden1, g, out_send, out_keep, norms2, gup_own, gdown_own) = feed_own(
        saved, cott, d_hidden_own, mixed, cotangent, out_weight, row(norm2_gain), up_own, down_own)
    out_got = swap(out_send, "ffn", 1)

    out_half = width // 4
    ups, downs, outs = [
        [blocked(a) for a in pair]
        for pair in ((gup_own, gup_got), (gdown_own, gdown_got), (out_keep, out_got))
    ]
    groups = [
        [[*all_of(a), (o, 0, out_half)] for a, o in zip(ups, outs)],
        [[*all_of(a), (o, out_half, out_half)] for a, o in zip(downs, outs)],
    ]
    orders = [[1, 2], [2, 1]]
    left = [list(range(bits)) for _ in groups]

    def advance(groups, n, after):
        if n >= 2:
            if n == 2:
                groups = [[pieces_a + pieces_b for pieces_a, pieces_b in zip(*groups)]]
            bits_now = left[0][-1:]
            splits = [[(bits_now[0], len(left[0]) - 1)]]
            for rest in left:
                rest.pop()
        else:
            bits_now = [order[n] for order in orders]
            splits = [[(bit, rest.index(bit))] for bit, rest in zip(bits_now, left)]
            for bit, rest in zip(bits_now, left):
                rest.remove(bit)
        outs = stage(list(zip(groups, splits)), after=after)
        got = [send_across(sent, [bit]) for (_, sent), bit in zip(outs, bits_now)]
        sent = [s for _, s in outs]
        return [[all_of(kept), all_of(r)] for (kept, _), r in zip(outs, got)], sent

    back = (rows, heads, mask, g, memory)
    *scores_other, pack, sums = scores_back(False, *back, saved_other)
    groups, sent = advance(groups, 0, [pack])
    *scores_own, d_own = scores_back(True, *back, saved_own, packs=(pack, sums), after=sent)
    d_partner = swap(d_own, "ffn", 1)
    other_side, own_side = (scores_other, saved_other[3:], pairs_other), (scores_own, saved_own[3:], pairs_own)
    ds = []
    if SPLIT:
        ds.append(heads_back(False, 0, SPLIT, *back, *other_side, after=[d_own]))
    d_both = combine(True, rows, d_own, d_partner, after=ds)
    d_far = swap(d_both, "seq", 1)
    ds.append(heads_back(False, SPLIT, SIDE - SPLIT, *back, *other_side, after=[d_both]))
    ds.append(heads_back(True, 0, SIDE, *back, *own_side, after=ds[-1:]))
    proj, in_keep, in_send = project_back(rows, heads, ds, control, d_partner, d_far, xnt)
    in_got = swap(in_send, "ffn", 1)
    groups, sent = advance(groups, 1, [in_send])
    grad_tokens, norms = norm_back(
        proj, in_weight, n1, inv1, row(norm1_gain), d_hidden1, norms2, after=sent)

    late = [
        all_of(blocked(in_keep)) + all_of(blocked(norms)),
        all_of(blocked(in_got)) + all_of(jnp.zeros_like(blocked(norms))),
    ]
    rest = list(range(bits))
    stages = list(range(2, bits))
    while rest:
        now = rest[:2]
        split = [(b, rest.index(b)) for b in now]
        rest = rest[2:]
        (kept, *sent), = stage([(late, split)])
        pairs = list(zip(sent, patterns(now)))
        if now[0]:
            pairs = pairs[1:] + pairs[:1]
        late = [all_of(kept)] + [all_of(send_across(s, p)) for s, p in pairs]
        token = [kept]
        while stages:
            groups, token = advance(groups, stages.pop(0), token)
            if rest:
                break
    early = [arrays[0][0] for arrays in groups[0]]
    half = gup_own.shape[1]
    down_at = half + out_half
    outs_at = [slice(half, down_at), slice(down_at + half, down_at + half + out_half)]
    (total,), = stage([(late, [])], us=1e3)
    final = last([total], early, outs_at)
    grad_in, grad_out, grad_up, grad_down, *norms = join(
        final, swap(final, "ffn", 1), early, slice(0, half), slice(down_at, down_at + half))
    return (output[None], grad_tokens[None], grad_in, grad_out, grad_up, grad_down, *norms)


def solution(mesh):
    rows = P("dp", ("seq", "ffn"), None)
    owned = P(("dp", "seq"))
    return jax.shard_map(
        on_device,
        mesh=mesh,
        in_specs=(
            rows, P("dp", None), P(), P(), P(), P(), P(), P(),
            P(None, "ffn"), P(None, "ffn"), rows,
        ),
        out_specs=(
            rows, rows, P(("dp", "seq"), None), P(("dp", "seq"), None),
            P(("dp", "seq"), "ffn"), P(("dp", "seq"), "ffn"),
            owned, owned, owned, owned,
        ),
        check_vma=False,
    )
```

```python
import functools

import jax
import jax.numpy as jnp
from jax import lax
from jax.experimental import pallas as pl
from jax.experimental.pallas import tpu as pltpu
from jax.sharding import PartitionSpec as P

HEADS = 8
HEAD = 64
EPSILON = 1e-05
BF = jnp.bfloat16
F32 = jnp.float32
GELU_A = 0.7978845608028654
GELU_B = 0.044715
SCALE = HEAD**-0.5
K1_VMEM = 48
SPLIT = 2
SIDE = HEADS // 2
PACK = HEADS * HEAD + 64


def nn(a, b):
    return lax.dot_general(a, b, (((1,), (0,)), ((), ())), preferred_element_type=F32)


def nt(a, b):
    return lax.dot_general(a, b, (((1,), (1,)), ((), ())), preferred_element_type=F32)


def tn(a, b):
    return lax.dot_general(a, b, (((0,), (0,)), ((), ())), preferred_element_type=F32)


def swap(a, axis, bit):
    size = lax.axis_size(axis)
    return lax.ppermute(a, axis, [(i, i ^ bit) for i in range(size)])


ANY = pl.BlockSpec(memory_space=pl.ANY)


def call(body, grid, in_specs, out_specs, out_shape, scratch=(), us=1.0, after=(), vmem=20):
    count = len(in_specs)

    def run(*refs):
        body(*refs[:count], *refs[count + len(after) :])

    def start(*operands):
        return pl.pallas_call(
            run,
            grid=grid,
            in_specs=list(in_specs) + [ANY] * len(after),
            out_specs=out_specs,
            out_shape=out_shape,
            scratch_shapes=list(scratch),
            cost_estimate=pl.CostEstimate(flops=int(us * 1e7), bytes_accessed=2**13, transcendentals=0),
            compiler_params=pltpu.CompilerParams(vmem_limit_bytes=vmem * 2**20),
        )(*operands, *after)

    return start


def whole(shape):
    return pl.BlockSpec(shape, lambda *_: (0,) * len(shape))


VM = pl.BlockSpec(memory_space=pltpu.MemorySpace.VMEM)


def shape(dtype, *dims):
    return jax.ShapeDtypeStruct(dims, dtype)


SMEM = pl.BlockSpec(memory_space=pltpu.SMEM)


def shard_of():
    return lax.axis_index("seq") * 2 + lax.axis_index("ffn")


def doc_begin_row(starts_ref, length):
    begin = shard_of() * length
    place = lax.broadcasted_iota(jnp.int32, (1, length), 1)
    row = jnp.full((1, length), -(2**30), jnp.int32)
    for j in range(starts_ref.shape[1]):
        s = starts_ref[0, j] - begin
        row = jnp.where(place >= s, jnp.maximum(row, s), row)
    return row


def passes(starts_ref, which, length):
    hit = jnp.int32(0)
    for j in range(starts_ref.shape[1]):
        s = starts_ref[0, j]
        hit = hit | ((s >= which * length) & (s < which * length + length)).astype(jnp.int32)
    return 1.0 - hit.astype(F32)


def visible(doc_row, length):
    i = lax.broadcasted_iota(jnp.int32, (length, length), 0)
    t = lax.broadcasted_iota(jnp.int32, (length, length), 1)
    return jnp.where((i <= t) & (i >= doc_row), 1.0, 0.0).astype(BF)


def tail_row(doc_row, length):
    place = lax.broadcasted_iota(jnp.int32, (1, length), 1)
    last = doc_row[:, length - 1 :]
    return jnp.where(place >= last, 1.0, 0.0)


def pack_totals(pack_ref, totals8):
    base = HEADS * HEAD
    hi = totals8.astype(BF)
    lo = (totals8 - hi.astype(F32)).astype(BF)
    for a in range(4):
        cols = slice(128 * a, 128 * a + 128)
        pack_ref[base + 16 * a : base + 16 * a + 16, :] = jnp.concatenate(
            [hi[:, cols], lo[:, cols]], axis=0
        )


def unpack(rows, totals8_of):
    base = HEADS * HEAD
    out = []
    for a in range(4):
        block = totals8_of(slice(base + 16 * a, base + 16 * a + 16))
        out.append(block[:8] + block[8:])
    return rows(slice(0, base)), jnp.concatenate(out, axis=1)


def combine_body(backward, rows_ref, own_ref, partner_ref, out_ref):
    is_first = (lax.axis_index("ffn") == 0).astype(F32)
    base = HEADS * HEAD
    if backward:
        p = rows_ref[2:3, :128]
        own_by, partner_by = is_first + (1 - is_first) * p, is_first * p + (1 - is_first)
    else:
        p = rows_ref[3:4, :128]
        own_by, partner_by = is_first * p + (1 - is_first), is_first + (1 - is_first) * p

    def sum_of(at):
        return own_ref[at, :].astype(F32) * own_by + partner_ref[at, :].astype(F32) * partner_by

    memory, totals8 = unpack(sum_of, sum_of)
    out_ref[:base, :] = memory.astype(BF)
    pack_totals(out_ref, totals8)


def combine(backward, rows, own, partner, after=()):
    return call(
        functools.partial(combine_body, backward),
        (),
        [VM] * 3,
        VM,
        shape(BF, PACK, 128),
        after=after,
    )(rows, own, partner)


def arrived(backward, rows_ref, partner_ref, far_ref, mem_ref, totals_ref):
    is_first = (lax.axis_index("ffn") == 0).astype(F32)
    if backward:
        p = rows_ref[3:4, :128]
        far_by, partner_by = is_first * p + (1 - is_first), is_first
        valid = lax.axis_index("seq") == 0
    else:
        p = rows_ref[2:3, :128]
        far_by, partner_by = is_first + (1 - is_first) * p, 1 - is_first
        valid = lax.axis_index("seq") == 1

    def sum_of(at):
        far = jnp.where(valid, far_ref[at, :].astype(F32), 0.0)
        return far * far_by + partner_ref[at, :].astype(F32) * partner_by

    memory, totals8 = unpack(sum_of, sum_of)
    mem_ref[...] = memory.astype(BF)
    totals_ref[...] = totals8.T


def head_of(own_side, h):
    ffn = lax.axis_index("ffn")
    return (ffn if own_side else 1 - ffn) * SIDE + h


def head_rows(head):
    return pl.ds(pl.multiple_of(head * HEAD, HEAD), HEAD)


def project_body(x_hbm, gain_hbm, bias_hbm, w_hbm, starts_ref,
                 heads_ref, raw_ref, xn_ref, pack_ref, mask_ref, rows_ref, n_ref, inv_ref, wq_ref,
                 x_ref, gain_ref, bias_ref, w_ref, sems):
    length, width = x_ref.shape
    copies = [
        pltpu.make_async_copy(x_hbm, x_ref, sems.at[0]),
        pltpu.make_async_copy(gain_hbm, gain_ref, sems.at[1]),
        pltpu.make_async_copy(bias_hbm, bias_ref, sems.at[2]),
    ]
    columns = [
        pltpu.make_async_copy(w_hbm.at[:, pl.ds((j + 1) * width, width)], w_ref.at[j], sems.at[3 + j])
        for j in range(3)
    ]
    later = pltpu.make_async_copy(w_hbm.at[:, pl.ds(0, width)], wq_ref, sems.at[6])
    for copy in copies + columns + [later]:
        copy.start()
    doc_row = doc_begin_row(starts_ref, length)
    tail = tail_row(doc_row, length)
    first = 2 * lax.axis_index("seq")
    rows = [jnp.where(doc_row < 0, 1.0, 0.0), tail] + [
        jnp.full((1, length), passes(starts_ref, which, length)) for which in (first, first + 1)
    ]
    rows_ref[...] = jnp.concatenate(rows + rows, axis=0)
    mask_ref[...] = visible(doc_row, length)
    for copy in copies:
        copy.wait()
    x = x_ref[...].astype(F32)
    mean = jnp.mean(x, axis=-1, keepdims=True)
    centered = x - mean
    inverse = lax.rsqrt(jnp.mean(centered * centered, axis=-1, keepdims=True) + EPSILON)
    n = centered * inverse
    n_ref[...] = n
    inv_ref[...] = jnp.broadcast_to(inverse, inv_ref.shape)
    xn = (n * gain_ref[...] + bias_ref[...]).astype(BF)
    xn_ref[...] = xn
    projected = []
    for j in range(3):
        columns[j].wait()
        projected.append(nn(xn, w_ref[j]))
    raw_ref[...] = projected[2]
    c = jnp.exp(projected[2]).astype(BF).T
    for j in range(2):
        t = projected[j].astype(BF).T
        for h in range(HEADS):
            heads_ref[h, j * HEAD : j * HEAD + HEAD, :] = t[h * HEAD : h * HEAD + HEAD]
    c_tail = c * tail.astype(BF)
    for h in range(HEADS):
        rows = slice(h * HEAD, h * HEAD + HEAD)
        heads_ref[h, 2 * HEAD :, :] = c[rows]
        mem_k = nt(c_tail[rows], heads_ref[h, :HEAD, :])
        mem_vt = nt(heads_ref[h, HEAD : 2 * HEAD, :], c_tail[rows])
        pack_ref[rows, :] = jnp.concatenate([mem_k, mem_vt], axis=1).astype(BF)
    tail8 = jnp.broadcast_to(tail, (8, length)).astype(BF)
    pack_totals(pack_ref, nt(tail8, c))
    later.wait()


def project(x, gain, bias, w, starts):
    length, width = x.shape
    hbm = pl.BlockSpec(memory_space=pltpu.MemorySpace.HBM)
    pin = lambda a: pltpu.with_memory_space_constraint(a, pltpu.HBM)
    return call(
        project_body,
        (),
        [hbm, hbm, hbm, hbm, SMEM],
        [VM] * 9,
        [
            shape(BF, HEADS, 3 * HEAD, length), shape(F32, length, width), shape(BF, length, width),
            shape(BF, PACK, 128), shape(BF, length, length), shape(F32, 8, length),
            shape(F32, length, width), shape(F32, length, 128), shape(BF, width, width),
        ],
        [
            pltpu.VMEM((length, width), BF), pltpu.VMEM((1, width), F32), pltpu.VMEM((1, width), F32),
            pltpu.VMEM((3, width, width), BF), pltpu.SemaphoreType.DMA((7,)),
        ],
        us=4.3,
        vmem=K1_VMEM,
    )(*(pin(a) for a in (x, gain, bias, w, starts)))


def query_body(xn_ref, w_ref, q_ref):
    t = nn(xn_ref[...], w_ref[...]).astype(BF).T
    for h in range(HEADS):
        q_ref[h] = t[h * HEAD : h * HEAD + HEAD]


def query(xn, w, after=()):
    return call(query_body, (), [VM] * 2, VM, shape(BF, HEADS, HEAD, xn.shape[0]), us=1e3, after=after)(xn, w)


def parts(refs, head):
    q_ref, heads_ref = refs
    return [q_ref[head]] + [heads_ref[head, j * HEAD : j * HEAD + HEAD, :] for j in range(3)]


def mask_pair(mask_ref):
    half = mask_ref.shape[0] // 2
    return mask_ref[:half, :half], mask_ref[:, half:]


def causal_pairs(left, right, mask_ref):
    half = mask_ref.shape[0] // 2
    early, late = mask_pair(mask_ref)
    rows = left.T
    return nn(rows[:half], right[:, :half]).astype(BF) * early, nn(rows, right[:, half:]).astype(BF) * late


def causal_sum(left, pairs):
    a, b = pairs
    half = a.shape[0]
    return jnp.concatenate([nn(left[:, :half], a), nn(left, b)], axis=1)


def causal_back(pairs, right):
    a, b = pairs
    half = a.shape[0]
    late = nn(b, right[half:])
    return jnp.concatenate([late[:half] + nn(a, right[:half]), late[half:]], axis=0)


def padded(rows, second):
    zero = jnp.zeros_like(rows)
    return jnp.concatenate([zero, rows] if second else [rows, zero], axis=0).T


def pair_shapes(length, count=SIDE):
    half = length // 2
    return [shape(BF, count, half, half), shape(BF, count, length, half)]


def store_pairs(refs, i, pairs):
    refs[0][i], refs[1][i] = pairs


def load_pairs(refs, i):
    return refs[0][i], refs[1][i]


def local_body(own_side, q_ref, heads_ref, mask_ref, number_ref, total_ref, *pair_refs):
    held = [parts((q_ref, heads_ref), head_of(own_side, i)) for i in range(SIDE)]
    pairs = [causal_pairs(k, q, mask_ref) for q, k, v, c in held]
    for i in range(SIDE):
        store_pairs(pair_refs, i, pairs[i])
    c = jnp.concatenate([h[3] for h in held], axis=0)
    total_ref[...] = causal_sum(c, mask_pair(mask_ref))
    for i in range(SIDE):
        number_ref[i * HEAD : i * HEAD + HEAD, :] = causal_sum(held[i][3], pairs[i])


def local_sums(own_side, heads, mask, after=()):
    length = heads[0].shape[2]
    return call(
        functools.partial(local_body, own_side),
        (),
        [VM] * 3,
        [VM] * 4,
        [shape(F32, SIDE * HEAD, length)] * 2 + pair_shapes(length),
        us=3.0,
        after=after,
    )(*heads, mask)


def mix_body(rows_ref, q_ref, heads_ref, mask_ref, partner_ref, far_ref, *refs):
    refs = list(refs)
    take = lambda n: [refs.pop(0) for _ in range(n)]
    ins = [take(2), take(2)]
    mixed_ref, mem_ref = take(2)
    outs = [take(5), take(5)]
    (totals_ref,) = refs
    arrived(False, rows_ref, partner_ref, far_ref, mem_ref, totals_ref)
    enters = rows_ref[0:1, :]
    jobs = [(own_side, i) for own_side in (False, True) for i in range(SIDE)]
    spreads, links = [], []
    for own_side, i in jobs:
        number_in, total_in = ins[own_side]
        number_ref, inverse_ref, weight_ref, *_ = outs[own_side]
        head, at = head_of(own_side, i), slice(i * HEAD, i * HEAD + HEAD)
        mem_k = mem_ref[head_rows(head), :][:, :HEAD]
        number = number_in[at, :] + enters * nn(mem_k, parts((q_ref, heads_ref), head)[0])
        inverse = 1.0 / (total_in[at, :] + enters * totals_ref[head_rows(head), 0:1])
        score = number * (inverse * SCALE)
        e = jnp.exp(score - jnp.max(score, axis=0, keepdims=True))
        weight = e * (1.0 / jnp.sum(e, axis=0, keepdims=True))
        number_ref[at, :] = number
        inverse_ref[at, :] = inverse
        weight_ref[at, :] = weight
        spreads.append((weight * inverse).astype(BF))
    for (own_side, i), spread in zip(jobs, spreads):
        links.append(causal_pairs(parts((q_ref, heads_ref), head_of(own_side, i))[3], spread, mask_ref))
        store_pairs(outs[own_side][3:], i, links[-1])
    for (own_side, i), spread, link in zip(jobs, spreads, links):
        head = head_of(own_side, i)
        mem_vt = mem_ref[head_rows(head), :][:, HEAD:]
        mixed = causal_sum(parts((q_ref, heads_ref), head)[2], link) + enters * nn(mem_vt, spread)
        mixed_ref[head_rows(head), :] = mixed.astype(BF)


def mix(rows, heads, mask, partner, far, local_other, local_own, after=()):
    length, width = heads[0].shape[2], HEADS * HEAD
    side = [shape(F32, SIDE * HEAD, length)] * 3 + pair_shapes(length)
    mixed, mem, *rest = call(
        mix_body,
        (),
        [VM] * 10,
        [VM] * 12,
        [shape(BF, width, length), shape(BF, width, 128)] + side + side,
        [pltpu.VMEM((width, 8), F32)],
        us=4.0,
        after=after,
    )(rows, *heads, mask, partner, far, *local_other, *local_own)
    return mixed, mem, rest[:5], rest[5:]


def prepare_body(cot_ref, down_ref, down_other_ref, raw_ref, xn_ref, other_ref, own_ref, cott_ref, control_ref, xnt_ref):
    cot = cot_ref[...]
    other_ref[...] = nn(cot, down_other_ref[...])
    own_ref[...] = nn(cot, down_ref[...])
    cott_ref[...] = cot.T
    xnt_ref[...] = xn_ref[...].T
    control_ref[...] = jnp.exp(raw_ref[...]).T


def prepare(cotangent, down, down_other, raw, xn, after=()):
    length, width = cotangent.shape
    return call(
        prepare_body,
        (),
        [VM] * 5,
        [VM] * 5,
        [shape(F32, length, down.shape[1])] * 2
        + [shape(BF, width, length), shape(F32, width, length), shape(BF, width, length)],
        us=2.0,
        after=after,
    )(cotangent, down, down_other, raw, xn)


def activations(xn, d_hidden_ref, up_ref):
    cols = [slice(j, j + 512) for j in range(0, up_ref.shape[1], 512)]
    pres = [nn(xn, up_ref[:, at]) for at in cols]
    hidden, grad_pre = [], []
    for pre, at in zip(pres, cols):
        v2 = pre * pre
        h = 0.5 + 0.5 * jnp.tanh(pre * (GELU_A + (GELU_A * GELU_B) * v2))
        act = pre * h
        hidden.append(act.astype(BF))
        slope = h + act * (1.0 - h) * (2.0 * GELU_A + (6.0 * GELU_A * GELU_B) * v2)
        grad_pre.append((d_hidden_ref[:, at] * slope).astype(BF))
    return jnp.concatenate(hidden, axis=1), jnp.concatenate(grad_pre, axis=1)


def feed_other_body(x_ref, mixed_ref, cott_ref, d_hidden_ref, w_out_ref, gain_ref, bias_ref, up_ref, down_ref,
                    gup_ref, gdown_ref, hidden1_ref, n_ref, inv_ref, xn_ref, xnt_ref,
                    part_ref, d_ref):
    hidden1 = x_ref[...].astype(F32) + tn(mixed_ref[...], w_out_ref[...])
    hidden1_ref[...] = hidden1
    mean = jnp.mean(hidden1, axis=-1, keepdims=True)
    centered = hidden1 - mean
    inverse = lax.rsqrt(jnp.mean(centered * centered, axis=-1, keepdims=True) + EPSILON)
    n = centered * inverse
    n_ref[...] = n
    inv_ref[...] = jnp.broadcast_to(inverse, inv_ref.shape)
    xn = (n * gain_ref[...] + bias_ref[...]).astype(BF)
    xnt = xn.T
    xn_ref[...] = xn
    xnt_ref[...] = xnt
    hidden, grad_pre = activations(xn, d_hidden_ref, up_ref)
    gdown_ref[...] = nn(cott_ref[...], hidden).astype(BF)
    gup_ref[...] = nn(xnt, grad_pre).astype(BF)
    part_ref[...] = nt(hidden, down_ref[...])
    d_ref[...] = nt(grad_pre, up_ref[...])


def feed_own_body(hidden1_ref, n_ref, inv_ref, xn_ref, xnt_ref, part_ref, d_in_ref, cott_ref, d_hidden_ref,
                  mixed_ref, cot_ref, w_out_ref, gain_ref, up_ref, down_ref,
                  output_ref, d_hidden1_ref, g_ref, out_send_ref, out_keep_ref, norms_ref,
                  gup_ref, gdown_ref):
    hidden, grad_pre = activations(xn_ref[...], d_hidden_ref, up_ref)
    dx, n = d_in_ref[...] + nt(grad_pre, up_ref[...]), n_ref[...]
    norms_ref[...] = jnp.concatenate(
        [jnp.sum(dx * n, axis=0, keepdims=True), jnp.sum(dx, axis=0, keepdims=True)] * 4, axis=0
    )
    output_ref[...] = (hidden1_ref[...] + (part_ref[...] + nt(hidden, down_ref[...]))).astype(BF)
    gdown_ref[...] = nn(cott_ref[...], hidden).astype(BF)
    d_n = dx * gain_ref[...]
    d_in = (
        d_n
        - jnp.mean(d_n, axis=-1, keepdims=True)
        - n * jnp.mean(d_n * n, axis=-1, keepdims=True)
    ) * inv_ref[:, 0:1]
    d_hidden1 = cot_ref[...].astype(F32) + d_in
    d_hidden1_ref[...] = d_hidden1
    d_branch = d_hidden1.astype(BF)
    gup_ref[...] = nn(xnt_ref[...], grad_pre).astype(BF)
    g_ref[...] = nt(w_out_ref[...], d_branch).astype(BF)
    grad_out = nn(mixed_ref[...], d_branch).astype(BF)
    half = grad_out.shape[1] // 2
    second = lax.axis_index("ffn") == 1
    out_keep_ref[...] = jnp.where(second, grad_out[:, half:], grad_out[:, :half])
    out_send_ref[...] = jnp.where(second, grad_out[:, :half], grad_out[:, half:])


def feed_other(x, mixed, cott, d_hidden, w_out, gain, bias, up, down):
    length, width = x.shape
    half, sq = shape(BF, *up.shape), lambda dt: shape(dt, length, width)
    return call(
        feed_other_body,
        (),
        [VM] * 9,
        [VM] * 9,
        [half, half, sq(F32), sq(F32), shape(F32, length, 128), sq(BF), sq(BF), sq(F32), sq(F32)],
        us=6.0,
    )(x, mixed, cott, d_hidden, w_out, gain, bias, up, down)


def feed_own(saved, cott, d_hidden, mixed, cotangent, w_out, gain, up, down, after=()):
    length, width = mixed.shape
    half, sq = shape(BF, *up.shape), lambda dt: shape(dt, length, width)
    return call(
        feed_own_body,
        (),
        [VM] * 15,
        [VM] * 8,
        [sq(BF), sq(F32), sq(BF)] + [shape(BF, width, width // 2)] * 2 + [shape(F32, 8, width), half, half],
        us=6.0,
        after=after,
    )(*saved, cott, d_hidden, mixed, cotangent, w_out, gain, up, down)


def scores_back_body(own_side, rows_ref, q_ref, heads_ref, mask_ref, g_ref, mem_ref, number_ref, inverse_ref, weight_ref,
                     *refs):
    if own_side:
        pack_in, sums_in, a_ref, spread_ref, d_total_ref, early_ref, late_ref, pack_ref, sums_ref = refs
        pack_ref[...] = pack_in[...]
        sums_ref[...] = sums_in[...]
    else:
        a_ref, spread_ref, d_total_ref, early_ref, late_ref, pack_ref, sums_ref = refs
    enters = rows_ref[0:1, :]
    heads = [head_of(own_side, i) for i in range(SIDE)]
    rows = [head_rows(head) for head in heads]
    held = [parts((q_ref, heads_ref), head) for head in heads]
    values = [causal_pairs(held[i][2], g_ref[rows[i], :], mask_ref) for i in range(SIDE)]
    for i in range(SIDE):
        store_pairs((early_ref, late_ref), i, values[i])
    numbers = [
        causal_sum(held[i][3], values[i]) + enters * tn(mem_ref[rows[i], :][:, HEAD:], g_ref[rows[i], :])
        for i in range(SIDE)
    ]
    kept = []
    for i, number_v in enumerate(numbers):
        at = slice(i * HEAD, i * HEAD + HEAD)
        number, inverse, weight = number_ref[at, :], inverse_ref[at, :], weight_ref[at, :]
        d_weight = number_v * inverse
        d_score = weight * (d_weight - jnp.sum(weight * d_weight, axis=0, keepdims=True))
        a = d_score * (inverse * SCALE)
        spread = weight * inverse
        d_total = -(a * number + spread * number_v) * inverse
        a_ref[at, :] = a.astype(BF)
        spread_ref[at, :] = spread.astype(BF)
        d_total_ref[at, :] = d_total.astype(BF)
        kept.append(((a * enters).astype(BF), (spread * enters).astype(BF), d_total * enters))
    for i, (a, spread, d_total) in enumerate(kept):
        d_k = nt(a, held[i][0])
        d_vt = nt(g_ref[rows[i], :], spread)
        pack_ref[rows[i], :] = jnp.concatenate([d_k, d_vt], axis=1).astype(BF)
        sums_ref[rows[i], :] = jnp.broadcast_to(jnp.sum(d_total, axis=1, keepdims=True), (HEAD, 128))
    if own_side:
        pack_totals(pack_ref, sums_ref[...].T[0:8])


def scores_back(own_side, rows, heads, mask, g, mem, saved, packs=(), after=()):
    length, width = heads[0].shape[2], HEADS * HEAD
    sums = [] if own_side else [shape(F32, width, 128)]
    outs = [shape(BF, SIDE * HEAD, length)] * 3 + pair_shapes(length) + [shape(BF, PACK, 128)] + sums
    return call(
        functools.partial(scores_back_body, own_side),
        (),
        [VM] * (9 + len(packs)),
        [VM] * len(outs),
        outs,
        [pltpu.VMEM((width, 128), F32)] if own_side else [],
        us=3.0,
        after=after,
    )(rows, *heads, mask, g, mem, *saved[:3], *packs)


def heads_back_body(own_side, begin, rows_ref, q_ref, heads_ref, mask_ref, g_ref, mem_ref, a_ref, spread_ref, d_total_ref,
                    v_early, v_late, l_early, l_late, p_early, p_late, d_ref):
    enters = rows_ref[0:1, :]
    count = d_ref.shape[0]
    order = range(begin, begin + count)
    heads = [head_of(own_side, i) for i in order]
    rows = [head_rows(head) for head in heads]
    held = [parts((q_ref, heads_ref), head) for head in heads]
    ats = [slice(i * HEAD, i * HEAD + HEAD) for i in order]
    steps = [causal_pairs(h[3], a_ref[at, :], mask_ref) for h, at in zip(held, ats)]
    totals = d_total_ref[begin * HEAD : (begin + count) * HEAD, :]
    from_totals = causal_back(mask_pair(mask_ref), totals.T).T
    controls = []
    for i, at in zip(order, ats):
        odd = i % 2 == 1
        controls.append(
            causal_back(load_pairs((p_early, p_late), i), padded(a_ref[at, :], odd))
            + causal_back(load_pairs((v_early, v_late), i), padded(spread_ref[at, :], odd))
        )
    for n in range(count):
        mem_k = mem_ref[rows[n], :][:, :HEAD]
        d_ref[n, :HEAD, :] = causal_sum(held[n][1], steps[n]) + enters * tn(mem_k, a_ref[ats[n], :])
    for n, i in enumerate(order):
        d_ref[n, HEAD : 3 * HEAD, :] = (
            causal_back(steps[n], padded(held[n][0], False))
            + causal_back(load_pairs((l_early, l_late), i), padded(g_ref[rows[n], :], True))
        ).T
    for n in range(0, count, 2):
        two = (controls[n] + controls[n + 1]).T
        for m in range(2):
            d_ref[n + m, 3 * HEAD :, :] = (
                two[m * HEAD : m * HEAD + HEAD] + from_totals[(n + m) * HEAD : (n + m) * HEAD + HEAD]
            )


def heads_back(own_side, begin, count, rows, heads, mask, g, mem, scores, links, pairs, after=()):
    length = heads[0].shape[2]
    return call(
        functools.partial(heads_back_body, own_side, begin),
        (),
        [VM] * 15,
        VM,
        shape(F32, count, 4 * HEAD, length),
        us=1.0,
        after=after,
    )(rows, *heads, mask, g, mem, *scores, *links, *pairs)


def project_back_body(counts, rows_ref, q_ref, heads_ref, control_ref, partner_ref, far_ref, xnt_ref, *refs):
    d_refs, (proj_ref, keep_ref, send_ref, mem_ref, totals_ref) = refs[: len(counts)], refs[len(counts) :]
    arrived(True, rows_ref, partner_ref, far_ref, mem_ref, totals_ref)
    tail = rows_ref[1:2, :]
    tail_bf = tail.astype(BF)
    places = [(d_ref, n) for d_ref, count in zip(d_refs, counts) for n in range(count)]
    jobs = [(d_ref, n, head_of(i >= SIDE, i % SIDE)) for i, (d_ref, n) in enumerate(places)]
    more = []
    for d_ref, n, head in jobs:
        mem = mem_ref[head_rows(head), :]
        back_k, back_vt = mem[:, :HEAD], mem[:, HEAD:]
        q, k, v, c = parts((q_ref, heads_ref), head)
        c_tail = c * tail_bf
        more.append((tn(back_k, c_tail), nn(back_vt, c_tail), nn(back_k, k) + tn(back_vt, v)))
    for (d_ref, n, head), (more_k, more_v, more_c) in zip(jobs, more):
        rows = head_rows(head)
        proj_ref[0, rows, :] = d_ref[n, :HEAD, :].astype(BF)
        proj_ref[1, rows, :] = (d_ref[n, HEAD : 2 * HEAD, :] + more_k).astype(BF)
        proj_ref[2, rows, :] = (d_ref[n, 2 * HEAD : 3 * HEAD, :] + more_v).astype(BF)
        d_control = d_ref[n, 3 * HEAD :, :] + tail * (more_c + totals_ref[rows, 0:1])
        proj_ref[3, rows, :] = (d_control * control_ref[rows, :]).astype(BF)
    for own_side in (False, True):
        first = pl.ds(pl.multiple_of(head_of(own_side, 0) * HEAD, SIDE * HEAD), SIDE * HEAD)
        for m in range(4):
            grad = nt(xnt_ref[...], proj_ref[m, first, :]).astype(BF)
            if own_side:
                keep_ref[:, m * SIDE * HEAD : (m + 1) * SIDE * HEAD] = grad
            else:
                send_ref[:, m * SIDE * HEAD : (m + 1) * SIDE * HEAD] = grad


def project_back(rows, heads, ds, control, partner, far, xnt, after=()):
    width, length = xnt.shape
    return call(
        functools.partial(project_back_body, [d.shape[0] for d in ds]),
        (),
        [VM] * (7 + len(ds)),
        [VM] * 3,
        [shape(BF, 4, width, length)] + [shape(BF, width, 4 * SIDE * HEAD)] * 2,
        [pltpu.VMEM((width, 128), BF), pltpu.VMEM((width, 8), F32)],
        us=5.0,
        after=after,
    )(rows, *heads, control, partner, far, xnt, *ds)


def norm_back_body(proj_ref, w_ref, n_ref, inv_ref, gain_ref, d_hidden1_ref, norms2_ref, grad_x_ref, norms_ref):
    length, width = n_ref.shape
    proj = proj_ref[...].reshape(4 * width, length)
    halves = [slice(0, length // 2), slice(length // 2, length)]
    ds = [
        lax.dot_general(proj[:, at], w_ref[...], (((0,), (1,)), ((), ())), preferred_element_type=F32)
        for at in halves
    ]
    sums = []
    for at, d in zip(halves, ds):
        n = n_ref[at, :]
        sums.append([jnp.sum(d * n, axis=0, keepdims=True), jnp.sum(d, axis=0, keepdims=True)])
        d_n = d * gain_ref[...]
        grad_x_ref[at, :] = d_hidden1_ref[at, :] + (
            d_n
            - jnp.mean(d_n, axis=-1, keepdims=True)
            - n * jnp.mean(d_n * n, axis=-1, keepdims=True)
        ) * inv_ref[at, 0:1]
    rows8 = jnp.concatenate([a + b for a, b in zip(*sums)] + [norms2_ref[0:6, :]], axis=0)
    norms_ref[...] = jnp.concatenate([rows8, jnp.zeros((120, length), F32)], axis=0).T.astype(BF)


def norm_back(proj, w, n, inv, gain, d_hidden1, norms2, after=()):
    length, width = n.shape
    return call(
        norm_back_body,
        (),
        [VM] * 7,
        [VM] * 2,
        [shape(F32, length, width), shape(BF, width, 128)],
        us=1e3,
        after=after,
    )(proj, w, n, inv, gain, d_hidden1, norms2)


def bit_axis(bit):
    return ("seq", 1) if bit == 0 else ("dp", 1 << (bit - 1))


def my_bit(bit):
    axis, step = bit_axis(bit)
    return (lax.axis_index(axis) // step) % 2


def send_across(a, bits):
    seqs, dps = lax.axis_size("seq"), lax.axis_size("dp")
    flip = sum(1 << bit for bit in bits)
    return lax.ppermute(a, ("dp", "seq"), [(i, i ^ flip) for i in range(seqs * dps)])


def place_of(t, places, values):
    index, rest, bit = 0, t, 0
    fixed = dict(zip(places, values))
    while rest or fixed:
        if bit in fixed:
            index = index + fixed.pop(bit) * (1 << bit)
        else:
            index = index + ((rest & 1) << bit)
            rest >>= 1
        bit += 1
    return index


def stage_body(plan, *refs):
    refs = list(refs)
    ins = [
        [[refs.pop(0).at[:, :, pl.ds(*piece)] for piece in pieces] for pieces in arrays] for arrays, _ in plan
    ]
    for (arrays, split), sources in zip(plan, ins):
        outs = [refs.pop(0) for _ in range(1 << len(split))]
        blocks = outs[0].shape[0]
        places = [place for _, place in split]
        mine = [my_bit(bit) for bit, _ in split]
        for pattern, out in enumerate(outs):
            values = [
                (1 - m) if (pattern >> n) & 1 else m for n, m in enumerate(mine)
            ]
            for t in range(blocks):
                at = place_of(t, places, values)
                rows = [
                    jnp.concatenate([p[at] for p in pieces], axis=1) if len(pieces) > 1 else pieces[0][at]
                    for pieces in sources
                ]
                if len(rows) == 1 or (len(rows) == 2 and out.dtype == BF):
                    total = sum(rows[1:], rows[0])
                else:
                    total = sum(row.astype(F32) for row in rows)
                out[t] = total.astype(out.dtype)


def stage(groups, after=(), dtype=BF, us=1.0):
    plan, operands, out_shape = [], [], []
    for arrays, split in groups:
        for pieces in arrays:
            operands += [array for array, _, _ in pieces]
        (array, _, _), width = arrays[0][0], sum(p[2] for p in arrays[0])
        plan.append(([[(first, count) for _, first, count in pieces] for pieces in arrays], split))
        out_shape += [shape(dtype, array.shape[0] >> len(split), array.shape[1], width)] * (1 << len(split))
    outs = list(
        call(functools.partial(stage_body, plan), (), [VM] * len(operands), [VM] * len(out_shape), out_shape, us=us, after=after)(
            *operands
        )
    )
    return [[outs.pop(0) for _ in range(1 << len(split))] for _, split in groups]


def all_of(a):
    return [(a, 0, a.shape[2])]


def patterns(bits):
    return [[b for n, b in enumerate(bits) if (p >> n) & 1] for p in range(1, 1 << len(bits))]


def last_body(late_count, columns, *refs):
    *ins, out_ref = refs
    sums = [
        sum(ref[0].astype(F32) for ref in ins[:late_count]),
        *(sum(ref[0][:, at].astype(F32) for ref in ins[late_count:]) for at in columns),
    ]
    out_ref[...] = jnp.concatenate(sums, axis=1).astype(BF)


def last(late, early, columns):
    rows = late[0].shape[1]
    width = late[0].shape[2] + sum(at.stop - at.start for at in columns)
    return call(
        functools.partial(last_body, len(late), columns),
        (),
        [VM] * (len(late) + len(early)),
        VM,
        shape(BF, rows, width),
    )(*late, *early)


def join_body(up_at, down_at, own_ref, other_ref, a_ref, b_ref,
              grad_in_ref, grad_out_ref, grad_up_ref, grad_down_ref, *norm_refs):
    second = lax.axis_index("ffn") == 1
    own, other = own_ref[...].astype(F32), other_ref[...].astype(F32)
    for f in range(2):
        keep_own = second if f else jnp.logical_not(second)
        half = jnp.where(keep_own, own, other)
        for m in range(4):
            grad_in_ref[:, m * 512 + f * 256 : m * 512 + f * 256 + 256] = half[:, m * 256 : m * 256 + 256]
        grad_out_ref[:, f * 256 : f * 256 + 256] = half[:, 1152:]
    for at, ref in ((up_at, grad_up_ref), (down_at, grad_down_ref)):
        ref[...] = a_ref[0][:, at].astype(F32) + b_ref[0][:, at].astype(F32)
    norms = (own[:, 1024:1152] + other[:, 1024:1152]).T
    for n, ref in enumerate(norm_refs):
        ref[...] = norms[n]


def join(own, other, early, up_at, down_at):
    rows = own.shape[0]
    half = up_at.stop - up_at.start
    return call(
        functools.partial(join_body, up_at, down_at),
        (),
        [VM] * 4,
        [VM] * 8,
        [shape(F32, rows, n) for n in (2048, 512, half, half)] + [shape(F32, rows)] * 4,
    )(own, other, *early)


def on_device(tokens, doc_starts, norm1_gain, norm1_bias, in_weight, out_weight,
              norm2_gain, norm2_bias, up_own, down_own, output_cotangent):
    x, cotangent, starts = tokens[0], output_cotangent[0], doc_starts
    length, width = x.shape
    owners = lax.axis_size("dp") * lax.axis_size("seq")
    bits = owners.bit_length() - 1
    row = lambda a: a.reshape(1, width)
    blocked = lambda a: a.reshape(owners, width // owners, a.shape[1])

    kvc, raw, xn, own, mask, rows, n1, inv1, wq = project(
        x, row(norm1_gain), row(norm1_bias), in_weight, starts)
    up_other, down_other = swap(up_own, "ffn", 1), swap(down_own, "ffn", 1)
    partner = swap(own, "ffn", 1)
    heads = (query(xn, wq), kvc)
    both = combine(False, rows, own, partner, after=heads[:1])
    far = swap(both, "seq", 1)
    number_o, total_o, *pairs_other = local_sums(False, heads, mask, after=[both])
    number, total, *pairs_own = local_sums(True, heads, mask, after=[both])
    d_hidden_other, d_hidden_own, cott, control, xnt = prepare(
        cotangent, down_own, down_other, raw, xn, after=[number])
    mixed, memory, saved_other, saved_own = mix(
        rows, heads, mask, partner, far, (number_o, total_o), (number, total), after=[cott])
    gup_send, gdown_send, *saved = feed_other(
        x, mixed, cott, d_hidden_other, out_weight, row(norm2_gain), row(norm2_bias), up_other, down_other)
    gup_got, gdown_got = swap(gup_send, "ffn", 1), swap(gdown_send, "ffn", 1)
    (output, d_hidden1, g, out_send, out_keep, norms2, gup_own, gdown_own) = feed_own(
        saved, cott, d_hidden_own, mixed, cotangent, out_weight, row(norm2_gain), up_own, down_own)
    out_got = swap(out_send, "ffn", 1)

    out_half = width // 4
    ups, downs, outs = [
        [blocked(a) for a in pair]
        for pair in ((gup_own, gup_got), (gdown_own, gdown_got), (out_keep, out_got))
    ]
    groups = [
        [[*all_of(a), (o, 0, out_half)] for a, o in zip(ups, outs)],
        [[*all_of(a), (o, out_half, out_half)] for a, o in zip(downs, outs)],
    ]
    orders = [[2, 1], [1, 2]]
    left = [list(range(bits)) for _ in groups]

    def advance(groups, n, after):
        if n >= 2:
            if n == 2:
                groups = [[pieces_a + pieces_b for pieces_a, pieces_b in zip(*groups)]]
            bits_now = left[0][-1:]
            splits = [[(bits_now[0], len(left[0]) - 1)]]
            for rest in left:
                rest.pop()
        else:
            bits_now = [order[n] for order in orders]
            splits = [[(bit, rest.index(bit))] for bit, rest in zip(bits_now, left)]
            for bit, rest in zip(bits_now, left):
                rest.remove(bit)
        outs = stage(list(zip(groups, splits)), after=after)
        got = [send_across(sent, [bit]) for (_, sent), bit in zip(outs, bits_now)]
        sent = [s for _, s in outs]
        return [[all_of(kept), all_of(r)] for (kept, _), r in zip(outs, got)], sent

    back = (rows, heads, mask, g, memory)
    *scores_other, pack, sums = scores_back(False, *back, saved_other)
    groups, sent = advance(groups, 0, [pack])
    *scores_own, d_own = scores_back(True, *back, saved_own, packs=(pack, sums), after=sent)
    d_partner = swap(d_own, "ffn", 1)
    other_side, own_side = (scores_other, saved_other[3:], pairs_other), (scores_own, saved_own[3:], pairs_own)
    ds = []
    if SPLIT:
        ds.append(heads_back(False, 0, SPLIT, *back, *other_side, after=[d_own]))
    d_both = combine(True, rows, d_own, d_partner, after=ds)
    d_far = swap(d_both, "seq", 1)
    ds.append(heads_back(False, SPLIT, SIDE - SPLIT, *back, *other_side, after=[d_both]))
    ds.append(heads_back(True, 0, SIDE, *back, *own_side, after=ds[-1:]))
    proj, in_keep, in_send = project_back(rows, heads, ds, control, d_partner, d_far, xnt)
    in_got = swap(in_send, "ffn", 1)
    groups, sent = advance(groups, 1, [in_send])
    grad_tokens, norms = norm_back(
        proj, in_weight, n1, inv1, row(norm1_gain), d_hidden1, norms2, after=sent)

    late = [
        all_of(blocked(in_keep)) + all_of(blocked(norms)),
        all_of(blocked(in_got)) + all_of(jnp.zeros_like(blocked(norms))),
    ]
    rest = list(range(bits))
    stages = list(range(2, bits))
    while rest:
        now = rest[:2]
        split = [(b, rest.index(b)) for b in now]
        rest = rest[2:]
        (kept, *sent), = stage([(late, split)])
        pairs = list(zip(sent, patterns(now)))
        if now[0]:
            pairs = pairs[1:] + pairs[:1]
        late = [all_of(kept)] + [all_of(send_across(s, p)) for s, p in pairs]
        token = [kept]
        while stages:
            groups, token = advance(groups, stages.pop(0), token)
            if rest:
                break
    early = [arrays[0][0] for arrays in groups[0]]
    half = gup_own.shape[1]
    down_at = half + out_half
    outs_at = [slice(half, down_at), slice(down_at + half, down_at + half + out_half)]
    (total,), = stage([(late, [])], us=1e3)
    final = last([total], early, outs_at)
    grad_in, grad_out, grad_up, grad_down, *norms = join(
        final, swap(final, "ffn", 1), early, slice(0, half), slice(down_at, down_at + half))
    return (output[None], grad_tokens[None], grad_in, grad_out, grad_up, grad_down, *norms)


def solution(mesh):
    rows = P("dp", ("seq", "ffn"), None)
    owned = P(("dp", "seq"))
    return jax.shard_map(
        on_device,
        mesh=mesh,
        in_specs=(
            rows, P("dp", None), P(), P(), P(), P(), P(), P(),
            P(None, "ffn"), P(None, "ffn"), rows,
        ),
        out_specs=(
            rows, rows, P(("dp", "seq"), None), P(("dp", "seq"), None),
            P(("dp", "seq"), "ffn"), P(("dp", "seq"), "ffn"),
            owned, owned, owned, owned,
        ),
        check_vma=False,
    )
```
